32 devices in a mesh: dp: 8 (over z, core), ffn: 4 (over y, x).
Axes of the slice: x: 2, y: 2, z: 4, core: 2. Of those that a mesh axis runs over, the one named last changes fastest.
Arguments:
- tokens: bfloat16 [32768, 768], P(('dp', 'ffn')), may hold values from -6 to 6
- seq_lengths: int32 [8], P('dp'), may hold values from 1024 to 4096, as said below
- out_grad: bfloat16 [32768, 768], P(('dp', 'ffn')), may hold values from -6 to 6
- ln1_gain: float32 [768], replicated, may hold values from 0.5 to 1.5
- ln1_bias: float32 [768], replicated, may hold values from -1 to 1
- time_decay: float32 [768], replicated, may hold values from -11 to -3.2
- time_first: float32 [768], replicated, may hold values from -1 to 1
- time_mix_k: float32 [768], replicated, may hold values from 0.05 to 0.95
- time_mix_v: float32 [768], replicated, may hold values from 0.05 to 0.95
- time_mix_r: float32 [768], replicated, may hold values from 0.05 to 0.95
- key_weight: bfloat16 [768, 768], replicated, may hold values from -0.21875 to 0.21875
- value_weight: bfloat16 [768, 768], replicated, may hold values from -0.21875 to 0.21875
- recept_weight: bfloat16 [768, 768], replicated, may hold values from -0.21875 to 0.21875
- output_weight: bfloat16 [768, 768], replicated, may hold values from -0.875 to 0.875
- ln2_gain: float32 [768], replicated, may hold values from 0.5 to 1.5
- ln2_bias: float32 [768], replicated, may hold values from -1 to 1
- cm_mix_k: float32 [768], replicated, may hold values from 0.05 to 0.95
- cm_mix_r: float32 [768], replicated, may hold values from 0.05 to 0.95
- cm_key: bfloat16 [768, 3072], P(None, 'ffn'), may hold values from -0.21875 to 0.21875
- cm_value: bfloat16 [3072, 768], P('ffn'), may hold values from -0.109375 to 0.109375
- cm_recept: bfloat16 [768, 768], replicated, may hold values from -0.21875 to 0.21875
Outputs:
- mixed: bfloat16 [32768, 768], P(('dp', 'ffn'))
- input_grad: bfloat16 [32768, 768], P(('dp', 'ffn'))
- ln1_gain_grad: float32 [768], replicated
- ln1_bias_grad: float32 [768], replicated
- time_decay_grad: float32 [768], replicated
- time_first_grad: float32 [768], replicated
- time_mix_k_grad: float32 [768], replicated
- time_mix_v_grad: float32 [768], replicated
- time_mix_r_grad: float32 [768], replicated
- key_weight_grad: float32 [768, 768], replicated
- value_weight_grad: float32 [768, 768], replicated
- recept_weight_grad: float32 [768, 768], replicated
- output_weight_grad: float32 [768, 768], replicated
- ln2_gain_grad: float32 [768], replicated
- ln2_bias_grad: float32 [768], replicated
- cm_mix_k_grad: float32 [768], replicated
- cm_mix_r_grad: float32 [768], replicated
- cm_key_grad: float32 [768, 3072], P(None, 'ffn')
- cm_value_grad: float32 [3072, 768], P('ffn')
- cm_recept_grad: float32 [768, 768], replicated
The draws below stay inside these ranges and needn't reach their ends.
Inputs may be any that keep to these rules, and one draw needn't show every extreme that they name: `seq_lengths`: each of the 1 slots of 4096 rows of a data group holds one sequence from its first row; some sequence has length 4096.
All inputs are finite; a program needn't handle non-finite values.
Results may differ from the reference program's by a relative error of at most 0.014.
Values may be sent and summed in bfloat16 or wider, within the bound.
A program may use at most 256 MiB of HBM per device.

```python
import math
import jax
import jax.numpy as jnp
from jax import lax

D = 768
FF = 3072
MIN_LEN = 1024
SPAN = 128
SLOT = 4096
SEQS = 8
TOKENS = 32768


def draw_seq_lengths(key, part):
    first_key, second_key = jax.random.split(jax.random.fold_in(key, 11))
    ranks = jax.random.randint(first_key, (SEQS,), 0, 1024)
    cubed = ranks * ranks // 1024 * ranks // 1024
    lengths = SLOT - cubed * (SLOT - MIN_LEN) // 1021
    longest = jax.random.randint(second_key, (), 0, SEQS)
    return jnp.where(jnp.arange(SEQS) == longest, SLOT, lengths).astype(jnp.int32)


def draw_time_decay(key, part):
    first_key = jax.random.fold_in(jax.random.fold_in(key, 23), 0)
    return jax.random.uniform(first_key, (D,), jnp.float32, math.log(0.5 / SLOT), math.log(0.04))


def steps_of(key, extent, cuts, least, high):
    level = 1.0
    for axis_at, blocks in cuts:
        heights = jax.random.uniform(jax.random.fold_in(jax.random.fold_in(key, 6), axis_at), (blocks,), jnp.float32, least / len(cuts), high / len(cuts))
        level = level * jnp.repeat(jnp.exp(heights), extent[axis_at] // blocks).reshape((-1,) + (1,) * (len(extent) - 1 - axis_at))
    return level


def noise(key, dims, scale, limit, cuts=(), kind=jnp.bfloat16):
    result = jax.random.normal(key, dims, jnp.float32) * scale
    if len(cuts) > 0:
        result = steps_of(key, dims, cuts, -0.22, 0.18) * result
    return jnp.clip(result, min=-limit, max=limit).astype(kind)


def setup_inputs(seed: int = 0) -> dict:
    key_list = jax.random.split(jax.random.key(seed), 22)
    return {
        "tokens": noise(key_list[0], (TOKENS, D), 1.0, 6.0, ((0, 32),)),
        "seq_lengths": draw_seq_lengths(jax.random.fold_in(key_list[21], 71), 0),
        "out_grad": noise(key_list[2], (TOKENS, D), 1.0, 6.0, ((0, 32),)),
        "ln1_gain": jnp.clip(1.0 + 0.1 * jax.random.normal(key_list[3], (D,), jnp.float32), 0.5, 1.5),
        "ln1_bias": noise(key_list[4], (D,), 0.2, 1.0, (), jnp.float32),
        "time_decay": draw_time_decay(jax.random.fold_in(key_list[21], 71), 0),
        "time_first": jnp.clip(jax.random.uniform(key_list[6], (D,), jnp.float32, -1.0, 1.0), -1.0, 1.0),
        "time_mix_k": jnp.clip(jax.random.uniform(key_list[7], (D,), jnp.float32, 0.05, 0.95), 0.05, 0.95),
        "time_mix_v": jnp.clip(jax.random.uniform(key_list[8], (D,), jnp.float32, 0.05, 0.95), 0.05, 0.95),
        "time_mix_r": jnp.clip(jax.random.uniform(key_list[9], (D,), jnp.float32, 0.05, 0.95), 0.05, 0.95),
        "key_weight": noise(key_list[10], (D, D), D ** -0.5, 0.21875),
        "value_weight": noise(key_list[11], (D, D), D ** -0.5, 0.21875),
        "recept_weight": noise(key_list[12], (D, D), D ** -0.5, 0.21875),
        "output_weight": noise(key_list[13], (D, D), (D // 16) ** -0.5, 0.875),
        "ln2_gain": jnp.clip(1.0 + 0.1 * jax.random.normal(key_list[14], (D,), jnp.float32), 0.5, 1.5),
        "ln2_bias": noise(key_list[15], (D,), 0.2, 1.0, (), jnp.float32),
        "cm_mix_k": jnp.clip(jax.random.uniform(key_list[16], (D,), jnp.float32, 0.05, 0.95), 0.05, 0.95),
        "cm_mix_r": jnp.clip(jax.random.uniform(key_list[17], (D,), jnp.float32, 0.05, 0.95), 0.05, 0.95),
        "cm_key": noise(key_list[18], (D, FF), D ** -0.5, 0.21875, ((1, 4),)),
        "cm_value": noise(key_list[19], (FF, D), FF ** -0.5, 0.109375, ((0, 4),)),
        "cm_recept": noise(key_list[20], (D, D), D ** -0.5, 0.21875),
    }


HIGH = lax.Precision.HIGHEST
EPSILON = 1e-05

@jax.custom_vjp
def low(v):
    return lax.optimization_barrier(v.astype(jnp.bfloat16)).astype(jnp.float32)

@jax.custom_vjp
def low_back(v):
    return v

def low_keep(v):
    return (low(v), None)

def low_pass(kept, grad):
    return (grad,)

def back_keep(v):
    return (v, None)

def back_low(kept, grad):
    return (low(grad),)
low.defvjp(low_keep, low_pass)
low_back.defvjp(back_keep, back_low)

def layer_norm(value_in, gain_vec, bias_vec):
    centered = value_in - lax.optimization_barrier(jnp.mean(value_in, axis=-1, keepdims=True))
    spread = lax.optimization_barrier(jnp.mean(centered * centered, axis=-1, keepdims=True))
    return centered * lax.rsqrt(spread + EPSILON) * gain_vec + bias_vec

def matmul(left_side, right_side):
    return jnp.dot(left_side, right_side, precision=HIGH, preferred_element_type=jnp.float32)

def blend(norm_rows, shifted_rows, mix_rate):
    return norm_rows * mix_rate + shifted_rows * (1.0 - mix_rate)

def segment_stride(carry_pair, segment_pair, fade_ratio, extra_log_gain):
    upper_sum_entry, lower_sum_entry = carry_pair
    key_rows, value_rows = segment_pair
    block_len = key_rows.shape[0]
    channel_extent = key_rows.shape[1]
    offsets = jnp.arange(block_len, dtype=jnp.float32)[:, None]
    lookup_rows_array = jnp.exp(key_rows)
    lookup_content_scale = lookup_rows_array * value_rows
    growth = jnp.exp(offsets * fade_ratio)
    lower_tri = (jnp.arange(block_len)[:, None] > jnp.arange(block_len)[None, :]).astype(jnp.float32)
    stacked = jnp.concatenate([growth * lookup_content_scale, growth * lookup_rows_array], axis=1)
    earlier_summands = jnp.dot(lower_tri, stacked, precision=HIGH, preferred_element_type=jnp.float32)
    fade_scaling = jnp.exp((1.0 - offsets) * fade_ratio)
    fading_ratio = jnp.exp(-offsets * fade_ratio)
    extra_gain_scale = jnp.exp(extra_log_gain)
    upper_sum_carry = fade_scaling * earlier_summands[:, :channel_extent] + extra_gain_scale * lookup_content_scale + fading_ratio * upper_sum_entry
    lower_sum_carry = fade_scaling * earlier_summands[:, channel_extent:] + extra_gain_scale * lookup_rows_array + fading_ratio * lower_sum_entry
    tail_fade = jnp.exp((1.0 - block_len) * fade_ratio)
    full_fade = jnp.exp(-1.0 * block_len * fade_ratio)
    num_out = tail_fade * lax.optimization_barrier(jnp.sum(stacked[:, :channel_extent], axis=0)) + full_fade * upper_sum_entry
    den_out = tail_fade * lax.optimization_barrier(jnp.sum(stacked[:, channel_extent:], axis=0)) + full_fade * lower_sum_entry
    return ((num_out, den_out), upper_sum_carry / lower_sum_carry)

def wkv_run(key_rows, value_rows, time_decay, time_first, upper_sum_entry, lower_sum_entry):
    fade_ratio = jnp.exp(time_decay)
    row_count, channel_extent = key_rows.shape
    blocks = (key_rows.reshape(row_count // SPAN, SPAN, channel_extent), value_rows.reshape(row_count // SPAN, SPAN, channel_extent))

    def advance(carry_pair, segment_pair):
        return jax.checkpoint(segment_stride)(carry_pair, segment_pair, fade_ratio, time_first)
    _, mixed_out = lax.scan(advance, (upper_sum_entry, lower_sum_entry), blocks)
    return mixed_out.reshape(row_count, channel_extent)

def slot_forward(row_block, row_mask, weights):
    ln1_gain, ln1_bias, time_decay, time_first, time_mix_k, time_mix_v, time_mix_r, key_weight, value_weight, recept_weight, output_weight, ln2_gain, ln2_bias, cm_mix_k, cm_mix_r, cm_key, cm_value, cm_recept = weights
    norm_one = layer_norm(row_block, ln1_gain, ln1_bias)
    shifted_one = jnp.concatenate([jnp.zeros_like(norm_one[:1]), norm_one[:-1]], axis=0)
    key_rows = low_back(matmul(low(blend(norm_one, shifted_one, time_mix_k)), key_weight))
    value_rows = low_back(matmul(low(blend(norm_one, shifted_one, time_mix_v)), value_weight))
    recept_rows = low_back(matmul(low(blend(norm_one, shifted_one, time_mix_r)), recept_weight))
    zeros_vec = jnp.zeros((key_rows.shape[1],), jnp.float32)
    wkv_rows = wkv_run(key_rows, value_rows, time_decay, time_first, zeros_vec, zeros_vec)
    attended = low(jax.nn.sigmoid(recept_rows) * wkv_rows)
    middle = row_block + low_back(matmul(attended, output_weight))
    norm_two = layer_norm(middle, ln2_gain, ln2_bias)
    shifted_two = jnp.concatenate([jnp.zeros_like(norm_two[:1]), norm_two[:-1]], axis=0)
    hidden_pre = low_back(matmul(low(blend(norm_two, shifted_two, cm_mix_k)), cm_key))
    hidden = low(jnp.square(jax.nn.relu(hidden_pre)))
    channel_out = low_back(matmul(hidden, cm_value))
    gate_pre = low_back(matmul(low(blend(norm_two, shifted_two, cm_mix_r)), cm_recept))
    block_out = middle + jax.nn.sigmoid(gate_pre) * channel_out
    return block_out * row_mask[:, None]

def reference(tokens, seq_lengths, out_grad, ln1_gain, ln1_bias, time_decay, time_first, time_mix_k, time_mix_v, time_mix_r, key_weight, value_weight, recept_weight, output_weight, ln2_gain, ln2_bias, cm_mix_k, cm_mix_r, cm_key, cm_value, cm_recept):
    weights = tuple((entry.astype(jnp.float32) for entry in (ln1_gain, ln1_bias, time_decay, time_first, time_mix_k, time_mix_v, time_mix_r, key_weight, value_weight, recept_weight, output_weight, ln2_gain, ln2_bias, cm_mix_k, cm_mix_r, cm_key, cm_value, cm_recept)))
    inputs = tokens.astype(jnp.float32).reshape(SEQS, SLOT, D)
    positions = jnp.arange(SLOT, dtype=jnp.int32)
    row_mask = (positions[None, :] < seq_lengths[:, None]).astype(jnp.float32)

    def forward(slot_inputs, slot_weights):

        def one_slot(scan_carry, slot_item):
            return (scan_carry, jax.checkpoint(slot_forward)(slot_item[0], slot_item[1], slot_weights))
        _, outputs = lax.scan(one_slot, jnp.zeros((), jnp.float32), (slot_inputs, row_mask))
        return outputs
    outputs, backward = jax.vjp(forward, inputs, weights)
    grad_in, grads = backward(out_grad.astype(jnp.float32).reshape(SEQS, SLOT, D))
    return (outputs.reshape(TOKENS, D).astype(jnp.bfloat16), grad_in.reshape(TOKENS, D).astype(jnp.bfloat16), grads[0], grads[1], grads[2], grads[3], grads[4], grads[5], grads[6], grads[7], grads[8], grads[9], grads[10], grads[11], grads[12], grads[13], grads[14], grads[15], grads[16], grads[17])
```

```python
import functools

import jax
import jax.numpy as jnp
from jax import lax
from jax.experimental import pallas as pl
from jax.experimental.pallas import tpu as pltpu
from jax.sharding import PartitionSpec as P

MAX_LEN = 4096
SPAN = 128
EPS = 1e-05
MESH = pl.DeviceIdType.MESH
F32 = jnp.float32
BF16 = jnp.bfloat16
ANY = pl.BlockSpec(memory_space=pl.ANY)
VMEM = pl.BlockSpec(memory_space=pltpu.VMEM)
SMEM = pl.BlockSpec(memory_space=pltpu.SMEM)
VLIMIT = 62 * 2**20
G1, B1, TD, TF, MK, MV, MR, G2, B2, CK, CR = range(11)


def dot(a, b, da=1, db=0):
    return lax.dot_general(a, b, (((da,), (db,)), ((), ())), preferred_element_type=F32)


def sds(shape, dtype=F32):
    return jax.ShapeDtypeStruct(shape, dtype)


def flip(i, bit):
    s = 1 << bit
    return i + s - 2 * s * ((i // s) % 2)


def rows_of(i, n):
    return pl.ds(pl.multiple_of(i * n, n), n)


def sigmoid(x):
    return 1.0 / (1.0 + jnp.exp(-x))


def normed(x):
    c = x - jnp.mean(x, axis=-1, keepdims=True)
    rs = lax.rsqrt(jnp.mean(c * c, axis=-1, keepdims=True) + EPS)
    return c * rs, rs


def split2(x):
    hi = x.astype(BF16)
    lo = (x - hi.astype(F32)).astype(BF16)
    return jnp.concatenate([hi, lo], axis=0)


def tri_pair(below):
    r = lax.broadcasted_iota(jnp.int32, (SPAN, 2 * SPAN), 0)
    c = lax.broadcasted_iota(jnp.int32, (SPAN, 2 * SPAN), 1) % SPAN
    keep = (r > c) if below else (r < c)
    return jnp.where(keep, 1.0, 0.0).astype(BF16)


def greet(peers):
    bar = pltpu.get_barrier_semaphore()
    for p in peers:
        pl.semaphore_signal(bar, inc=1, device_id=p, device_id_type=MESH)
    pl.semaphore_wait(bar, len(peers))


def remote(src, dst, ssem, rsem, dev):
    return pltpu.make_async_remote_copy(
        src_ref=src, dst_ref=dst, send_sem=ssem, recv_sem=rsem, device_id=dev, device_id_type=MESH
    )


class Layout:
    def __init__(self, mesh, rows, width, local_units):
        self.n_f = mesh.shape["ffn"]
        self.n_dp = mesh.shape["dp"]
        self.R = rows
        self.D = width
        self.U = local_units
        self.BR = 256
        self.nblk = rows // self.BR
        self.nspan = rows // SPAN
        slot_len = min(MAX_LEN, rows * self.n_f)
        self.per_slot = slot_len // rows
        self.bits = self.n_f.bit_length() - 1
        self.parts = 2 if self.bits == 2 else 1
        self.nz = self.n_dp // 2

    def order(self, part):
        b = list(range(self.bits))
        return b if part == 0 else b[::-1]


def subsets(bits):
    out = [[]]
    for b in bits:
        out = out + [s + [b] for s in out]
    return out


def flips(i, bits):
    for b in bits:
        i = flip(i, b)
    return i


def gather_steps(L):
    steps, flat = [], 0
    for t in range(L.bits):
        here = []
        for p in range(L.parts):
            o = L.order(p)
            for s in subsets(o[:t]):
                here.append((p, o[t], s, flat))
                flat += 1
        steps.append(here)
    return steps, flat


def front_kernel(
    L, tok, par, wk, wv, wr, wo, wc, kshard, vshard,
    xk_o, xv_o, xr_o, y_o, ck_o, cr_o, a_o, v_o, rd_o, wkv_o, sr_o, x1_o, gate_o, edge_o, kall, vall,
    tokv, w5, npad, xk_s, xv_s, xr_s, y_s, ck_s, cr_s, a_s, v_s, S_s, D_s, sr_s, x1_s, gate_s,
    grow, fade, tri, ent, st_out, st_in, tedge, nedge, dev_in,
    in_sem, out_sem, own_sem, e_ssem, e_rsem, s_ssem, s_rsem, g_ssem, g_rsem, c_ssem, c_rsem,
):
    D, BR, n_f = L.D, L.BR, L.n_f
    dp, me = lax.axis_index("dp"), lax.axis_index("ffn")
    core = dp % 2
    buddy = dp + 1 - 2 * core
    place = me % L.per_slot
    keep = jnp.where(place == 0, 0.0, 1.0).astype(F32)
    ins = [pltpu.make_async_copy(tok, tokv, in_sem.at[0])]
    for n, w in enumerate((wk, wv, wr, wo, wc)):
        ins.append(pltpu.make_async_copy(w, w5.at[n], in_sem.at[1 + n]))
    for cp in ins:
        cp.start()
    owns = [
        pltpu.make_async_copy(kshard, kall.at[me], own_sem.at[0]),
        pltpu.make_async_copy(vshard, vall.at[me], own_sem.at[1]),
    ]
    for cp in owns:
        cp.start()

    greet([(dp, (me + k) % n_f) for k in range(1, n_f)] + [(buddy, me)])

    nxt = (me + 1) % n_f
    tok_edge = remote(tok.at[pl.ds(L.R - 16, 16)], tedge, e_ssem.at[0], e_rsem.at[0], (dp, nxt))
    tok_edge.start()

    segs = ((kshard, kall, D // 2), (vshard, vall, L.U // 2))
    steps, _ = gather_steps(L)

    def gather_copies(t):
        out = []
        for q, (shard, full, half) in enumerate(segs):
            n = half // L.parts
            for p, bit, sub, flat in steps[t]:
                r = pl.ds(pl.multiple_of(core * half + p * n, 16), n)
                j = flips(me, sub)
                src = full.at[j, r] if sub else shard.at[r]
                out.append(
                    remote(src, full.at[j, r], g_ssem.at[q, flat], g_rsem.at[q, flat], (dp, flip(me, bit)))
                )
        return out

    def core_copies(t):
        out = []
        for q, (shard, full, half) in enumerate(segs):
            n = half // L.parts
            for p, bit, sub, flat in steps[t]:
                r = pl.ds(pl.multiple_of(core * half + p * n, 16), n)
                j = flip(flips(me, sub), bit)
                out.append(
                    remote(full.at[j, r], full.at[j, r], c_ssem.at[q, flat], c_rsem.at[q, flat], (buddy, me))
                )
        return out

    for cp in gather_copies(0):
        cp.start()

    w = jnp.exp(par[TD : TD + 1, :])
    ew = jnp.exp(w)
    eu = jnp.exp(par[TF : TF + 1, :])
    age = lax.broadcasted_iota(jnp.int32, (SPAN, D), 0).astype(F32) * w
    grow[...] = jnp.exp(age)
    fade[...] = jnp.exp(-age)
    tri[...] = tri_pair(True)
    full_fade = jnp.exp(-float(SPAN) * w)
    tail_fade = jnp.exp(-float(SPAN - 1) * w)
    st_out[...] = jnp.zeros_like(st_out)

    ins[0].wait()
    tok_edge.wait()
    en, _ = normed(tedge[...].astype(F32))
    en = (en * par[G1 : G1 + 1, :] + par[B1 : B1 + 1, :])[8:16] * keep
    npad[0:8, :] = en
    edge_o[0:8, :] = en
    for cp in ins[1:4]:
        cp.wait()

    outs_a = ((xk_s, xk_o), (xv_s, xv_o), (xr_s, xr_o), (a_s, a_o), (v_s, v_o), (sr_s, sr_o))
    outs_c = ((y_s, y_o), (S_s, wkv_o), (D_s, rd_o), (x1_s, x1_o))
    outs_d = ((ck_s, ck_o), (cr_s, cr_o), (gate_s, gate_o))

    def ship(outs, base, i):
        return [
            pltpu.make_async_copy(s.at[rows_of(i, BR)], o.at[rows_of(i, BR)], out_sem.at[base + n, i])
            for n, (s, o) in enumerate(outs)
        ]

    def phase_a(i, carry):
        r = rows_of(i, BR)
        n1, _ = normed(tokv[r, :].astype(F32))
        n1 = n1 * par[G1 : G1 + 1, :] + par[B1 : B1 + 1, :]
        npad[pl.ds(pl.multiple_of(i * BR + 8, 8), BR), :] = n1
        prev = pltpu.roll(npad[pl.ds(pl.multiple_of(i * BR, 8), BR + 8), :], 1, 0)[8:]
        d = n1 - prev
        xk = (prev + d * par[MK : MK + 1, :]).astype(BF16)
        xv = (prev + d * par[MV : MV + 1, :]).astype(BF16)
        xr = (prev + d * par[MR : MR + 1, :]).astype(BF16)
        xk_s[r, :] = xk
        xv_s[r, :] = xv
        xr_s[r, :] = xr
        a = jnp.exp(dot(xk, w5[0]))
        v = dot(xv, w5[1])
        a_s[r, :] = a
        v_s[r, :] = v
        for sb in range(BR // SPAN):
            b = i * (BR // SPAN) + sb
            aa = a[sb * SPAN : (sb + 1) * SPAN]
            vv = v[sb * SPAN : (sb + 1) * SPAN]
            ga = grow[...] * aa
            both = jnp.concatenate([ga * vv, ga], axis=1)
            pre = dot(tri[...], split2(both))
            fs = fade[...] * ew
            S_s[rows_of(b, SPAN), :] = fs * pre[:, :D]
            D_s[rows_of(b, SPAN), :] = fs * pre[:, D:]
            tot = pre[SPAN - 1 : SPAN] + both[SPAN - 1 : SPAN]
            num, den = st_out[0:1, :], st_out[1:2, :]
            ent[b, 0:1, :] = num
            ent[b, 1:2, :] = den
            st_out[0:1, :] = full_fade * num + tail_fade * tot[:, :D]
            st_out[1:2, :] = full_fade * den + tail_fade * tot[:, D:]
        sr_s[r, :] = sigmoid(dot(xr, w5[2]))
        for cp in ship(outs_a, 0, i):
            cp.start()
        return carry

    lax.fori_loop(0, L.nblk, phase_a, 0)

    states = [
        remote(st_out, st_in.at[k], s_ssem.at[k], s_rsem.at[k], (dp, (me + k) % n_f)) for k in range(1, n_f)
    ]
    for cp in states:
        cp.start()

    first = gather_copies(0)
    for cp in first:
        cp.wait_recv()
    for t in range(1, L.bits):
        for cp in gather_copies(t):
            cp.start()
        if t < L.bits - 1:
            for cp in gather_copies(t):
                cp.wait_recv()
    for t in range(L.bits - 1):
        for cp in core_copies(t):
            cp.start()

    for cp in states:
        cp.wait()
    num_in = jnp.zeros((1, D), F32)
    den_in = jnp.zeros((1, D), F32)
    for k in range(1, L.per_slot):
        ok = jnp.where(place >= k, 1.0, 0.0).astype(F32)
        f = jnp.exp(-float((k - 1) * L.R) * w) * ok
        num_in = num_in + f * st_in[k, 0:1, :]
        den_in = den_in + f * st_in[k, 1:2, :]
    dev_in[0:1, :] = num_in
    dev_in[1:2, :] = den_in
    for cp in ins[4:]:
        cp.wait()

    def phase_c(i, carry):
        r = rows_of(i, BR)
        for sb in range(BR // SPAN):
            b = i * (BR // SPAN) + sb
            rb = rows_of(b, SPAN)
            fb = jnp.exp(w * (b * (-SPAN)).astype(F32))
            en = ent[b, 0:1, :] + fb * dev_in[0:1, :]
            ed = ent[b, 1:2, :] + fb * dev_in[1:2, :]
            F = eu * a_s[rb, :]
            fd = fade[...]
            num = S_s[rb, :] + fd * en + F * v_s[rb, :]
            rd = 1.0 / (D_s[rb, :] + fd * ed + F)
            wkv = num * rd
            S_s[rb, :] = wkv
            D_s[rb, :] = rd
            y_s[rb, :] = (sr_s[rb, :] * wkv).astype(BF16)
        x1 = tokv[r, :].astype(F32) + dot(y_s[r, :], w5[3])
        x1_s[r, :] = x1
        n2, _ = normed(x1)
        npad[pl.ds(pl.multiple_of(i * BR + 8, 8), BR), :] = n2 * par[G2 : G2 + 1, :] + par[B2 : B2 + 1, :]
        for cp in ship(outs_c, 6, i):
            cp.start()
        return carry

    lax.fori_loop(0, L.nblk, phase_c, 0)

    n_edge = remote(npad.at[pl.ds(L.R, 8)], nedge, e_ssem.at[1], e_rsem.at[1], (dp, nxt))
    n_edge.start()

    def phase_d(ii, carry):
        i = L.nblk - 1 - ii
        r = rows_of(i, BR)
        win = npad[pl.ds(pl.multiple_of(i * BR, 8), BR + 8), :]
        prev = pltpu.roll(win, 1, 0)[8:]
        d = win[8:] - prev
        cr = (prev + d * par[CR : CR + 1, :]).astype(BF16)
        ck_s[r, :] = (prev + d * par[CK : CK + 1, :]).astype(BF16)
        cr_s[r, :] = cr
        gate_s[r, :] = sigmoid(dot(cr, w5[4]))
        for cp in ship(outs_d, 10, i):
            cp.start()
        return carry

    lax.fori_loop(0, L.nblk - 1, phase_d, 0)
    n_edge.wait()
    npad[0:8, :] = nedge[...] * keep
    edge_o[8:16, :] = nedge[...] * keep
    phase_d(L.nblk - 1, 0)

    last = gather_copies(L.bits - 1)
    for cp in last:
        cp.wait_recv()
    for cp in core_copies(L.bits - 1):
        cp.start()
    for t in range(L.bits):
        for cp in gather_copies(t):
            cp.wait_send()
        for cp in core_copies(t):
            cp.wait()
    for cp in owns:
        cp.wait()

    def drain(i, carry):
        for outs, base in ((outs_a, 0), (outs_c, 6), (outs_d, 10)):
            for cp in ship(outs, base, i):
                cp.wait()
        return carry

    lax.fori_loop(0, L.nblk, drain, 0)


def front(L, tok, par, wk, wv, wr, wo, wc, kshard, vshard):
    R, D, n_f, U = L.R, L.D, L.n_f, L.U
    _, flat = gather_steps(L)
    rb, rf = sds((R, D), BF16), sds((R, D))
    dma = pltpu.SemaphoreType.DMA
    return pl.pallas_call(
        functools.partial(front_kernel, L),
        out_shape=(rb,) * 6 + (rf,) * 7 + (sds((16, D)), sds((n_f, D, U), BF16), sds((n_f, U, D), BF16)),
        in_specs=[ANY, VMEM] + [ANY] * 7,
        out_specs=(ANY,) * 13 + (VMEM, ANY, ANY),
        scratch_shapes=[
            pltpu.VMEM((R, D), BF16), pltpu.VMEM((5, D, D), BF16), pltpu.VMEM((R + 8, D), F32),
            *([pltpu.VMEM((R, D), BF16)] * 6), *([pltpu.VMEM((R, D), F32)] * 7),
            pltpu.VMEM((SPAN, D), F32), pltpu.VMEM((SPAN, D), F32), pltpu.VMEM((SPAN, 2 * SPAN), BF16),
            pltpu.VMEM((L.nspan, 8, D), F32), pltpu.VMEM((8, D), F32), pltpu.VMEM((n_f, 8, D), F32),
            pltpu.VMEM((16, D), BF16), pltpu.VMEM((8, D), F32), pltpu.VMEM((8, D), F32),
            dma((6,)), dma((13, L.nblk)), dma((2,)), dma((2,)), dma((2,)), dma((n_f,)), dma((n_f,)),
            dma((2, flat)), dma((2, flat)), dma((2, flat)), dma((2, flat)),
        ],
        compiler_params=pltpu.CompilerParams(collective_id=0, has_side_effects=True, vmem_limit_bytes=VLIMIT),
        cost_estimate=pl.CostEstimate(flops=10 * R * D * D, bytes_accessed=40 * R * D, transcendentals=4 * R * D),
        name="front",
    )(tok, par, wk, wv, wr, wo, wc, kshard, vshard)


def middle_kernel(
    L, lens, ck, cr, x1, gate, og, kall, vall, wc,
    mixed_o, g2_o, gck_o, gcr_o, dk_o, dv_o, dc_o,
    kv, vv, wcv, ck_s, cr_s, x1_s, gate_s, og_s, mix_s, gv_s, gg_s, ckt_s, gvt_s, h_s, p_s, dk_s, dv_s, dc_s, inc,
    in_sem, w_sem, out_sem, g_sem, x_ssem, x_rsem,
):
    BR, n_f, D = L.BR, L.n_f, L.D
    dp, me = lax.axis_index("dp"), lax.axis_index("ffn")
    core = dp % 2
    buddy = dp + 1 - 2 * core
    half = D // 2
    length = lens[me // L.per_slot]
    start = (me % L.per_slot) * L.R

    w_cp = [pltpu.make_async_copy(kall.at[j], kv.at[j], w_sem.at[0, j]) for j in range(n_f)]
    w_cp += [pltpu.make_async_copy(vall.at[j], vv.at[j], w_sem.at[1, j]) for j in range(n_f)]
    pairs = ((ck, ck_s), (x1, x1_s), (gate, gate_s), (og, og_s), (cr, cr_s), (wc, wcv))
    ins = [pltpu.make_async_copy(s, d, in_sem.at[n]) for n, (s, d) in enumerate(pairs)]
    ins[0].start()
    for cp in w_cp + ins[1:]:
        cp.start()
    for cp in w_cp + ins:
        cp.wait()

    def ship(i):
        r = rows_of(i, BR)
        both = ((mix_s, mixed_o), (og_s, g2_o), (x1_s, gck_o), (gate_s, gcr_o))
        return [pltpu.make_async_copy(s.at[r], d.at[r], out_sem.at[n, i]) for n, (s, d) in enumerate(both)]

    def block(i, carry):
        r = rows_of(i, BR)
        ck_i = ck_s[r, :]
        vsum = jnp.zeros((BR, D), F32)
        for j in range(n_f):
            p = jnp.maximum(dot(ck_i, kv[j]), 0.0)
            h = (p * p).astype(BF16)
            p_s[j, r, :] = p.astype(BF16)
            h_s[j, r, :] = h
            vsum = vsum + dot(h, vv[j])
        pos = start + i * BR + lax.broadcasted_iota(jnp.int32, (BR, 1), 0)
        live = jnp.where(pos < length, 1.0, 0.0).astype(F32)
        gate_i = gate_s[r, :]
        mix_s[r, :] = ((x1_s[r, :] + gate_i * vsum) * live).astype(BF16)
        g2 = og_s[r, :].astype(F32) * live
        og_s[r, :] = g2.astype(BF16)
        gv32 = g2 * gate_i
        gv = gv32.astype(BF16)
        gg = (gv32 * vsum * (1.0 - gate_i)).astype(BF16)
        gv_s[r, :] = gv
        gg_s[r, :] = gg
        cols = pl.ds(pl.multiple_of(i * BR, 128), BR)
        ckt_s[:, cols] = ck_i.T
        gvt_s[:, cols] = gv.T
        gck = jnp.zeros((BR, D), F32)
        for j in range(n_f):
            dh = dot(gv, vv[j], 1, 1)
            gk = (dh * (2.0 * p_s[j, r, :].astype(F32))).astype(BF16)
            p_s[j, r, :] = gk
            gck = gck + dot(gk, kv[j], 1, 1)
        x1_s[r, :] = gck
        gate_s[r, :] = dot(gg, wcv[...], 1, 1)
        for cp in ship(i):
            cp.start()
        return carry

    lax.fori_loop(0, L.nblk, block, 0)

    greet([(buddy, me)])

    def swaps(j):
        away = pl.ds(pl.multiple_of((1 - core) * half, 16), half)
        return [
            remote(g.at[j, away], inc.at[n, j], x_ssem.at[n, j], x_rsem.at[n, j], (buddy, me))
            for n, g in enumerate((dk_s, dv_s))
        ]

    def grads(j, carry):
        for c in range(D // BR):
            rr = slice(c * BR, (c + 1) * BR)
            dk_s[j, rr, :] = dot(ckt_s[rr, :], p_s[j]).astype(BF16)
            dv_s[j, rr, :] = dot(gvt_s[rr, :], h_s[j]).astype(BF16)
        for cp in swaps(j):
            cp.start()
        return carry

    lax.fori_loop(0, n_f, grads, 0)
    for c in range(D // BR):
        rr = slice(c * BR, (c + 1) * BR)
        dc_s[rr, :] = dot(cr_s[:, rr], gg_s[...], 0, 0).astype(BF16)
    last = pltpu.make_async_copy(dc_s, dc_o, in_sem.at[0])
    last.start()
    kept = pl.ds(pl.multiple_of(core * half, 16), half)

    def merge(j, carry):
        for n, (g, o) in enumerate(((dk_s, dk_o), (dv_s, dv_o))):
            swaps(j)[n].wait_recv()
            g[j, kept, :] = (g[j, kept, :].astype(F32) + inc[n, j].astype(F32)).astype(BF16)
            pltpu.make_async_copy(g.at[j, kept], o.at[j], g_sem.at[n, j]).start()
        return carry

    lax.fori_loop(0, n_f, merge, 0)

    def drain(j, carry):
        for n, (g, o) in enumerate(((dk_s, dk_o), (dv_s, dv_o))):
            swaps(j)[n].wait_send()
            pltpu.make_async_copy(g.at[j, kept], o.at[j], g_sem.at[n, j]).wait()
        return carry

    lax.fori_loop(0, n_f, drain, 0)
    for i in range(L.nblk):
        for cp in ship(i):
            cp.wait()
    last.wait()


def middle(L, lens, ck, cr, x1, gate, og, kall, vall, wc):
    R, D, n_f, U = L.R, L.D, L.n_f, L.U
    dma = pltpu.SemaphoreType.DMA
    rb, rf, grad = sds((R, D), BF16), sds((R, D)), sds((n_f, D // 2, U), BF16)
    vb, vf = pltpu.VMEM((R, D), BF16), pltpu.VMEM((R, D), F32)
    hid = pltpu.VMEM((n_f, R, U), BF16)
    return pl.pallas_call(
        functools.partial(middle_kernel, L),
        out_shape=(rb, rb, rf, rf, grad, grad, sds((D, D), BF16)),
        in_specs=[SMEM] + [ANY] * 8,
        out_specs=(ANY,) * 7,
        scratch_shapes=[
            pltpu.VMEM((n_f, D, U), BF16), pltpu.VMEM((n_f, U, D), BF16), pltpu.VMEM((D, D), BF16),
            vb, vb, vf, vf, vb, vb, vb, vb, pltpu.VMEM((D, R), BF16), pltpu.VMEM((D, R), BF16), hid, hid,
            pltpu.VMEM((n_f, D, U), BF16), pltpu.VMEM((n_f, D, U), BF16), pltpu.VMEM((D, D), BF16),
            pltpu.VMEM((2, n_f, D // 2, U), BF16),
            dma((6,)), dma((2, n_f)), dma((4, L.nblk)), dma((2, n_f)), dma((2, n_f)), dma((2, n_f)),
        ],
        compiler_params=pltpu.CompilerParams(collective_id=1, has_side_effects=True, vmem_limit_bytes=VLIMIT),
        cost_estimate=pl.CostEstimate(flops=52 * R * D * D, bytes_accessed=60 * R * D, transcendentals=0),
        name="middle",
    )(lens, ck, cr, x1, gate, og, kall, vall, wc)


class Pool:
    def __init__(self, ssem, rsem):
        self.ssem, self.rsem, self.n = ssem, rsem, 0

    def copy(self, src, dst, dev):
        k = self.n
        self.n = k + 1
        return remote(src, dst, self.ssem.at[k], self.rsem.at[k], dev)


def begin(copies):
    for cp in copies:
        cp.start()
    return copies


def landed(copies):
    for cp in copies:
        cp.wait_recv()


def z_pieces(rows, nz):
    n = nz
    while (rows // n) % 16:
        n //= 2
    return n


class Unit:
    def __init__(self, env, order, rows, acc, rbuf, zbuf, final):
        self.env, self.order, self.rows = env, order, rows
        self.acc, self.rbuf, self.zbuf, self.final = acc, rbuf, zbuf, final
        self.nzp = z_pieces(rows, env.nz)
        self.sent = []

    def keep(self, copies):
        self.sent += copies
        return begin(copies)

    def halve(self, t, src=None):
        e, bit = self.env, self.order[t]
        base = sum(1 << (len(self.order) - 1 - k) for k in range(t))
        out = []
        for n, sub in enumerate(subsets(self.order[t + 1 :])):
            there = flip(flips(e.me, sub), bit)
            ref = (src or self.acc)(there)
            out.append(e.pool.copy(ref, self.rbuf(base + n), (e.dp, flip(e.me, bit))))
        self.now = self.keep(out)

    def halve_end(self, t):
        e = self.env
        base = sum(1 << (len(self.order) - 1 - k) for k in range(t))
        landed(self.now)
        for n, sub in enumerate(subsets(self.order[t + 1 :])):
            view = self.acc(flips(e.me, sub))
            view[...] = (view[...].astype(F32) + self.rbuf(base + n)[...].astype(F32)).astype(BF16)

    def piece(self, q):
        n = self.rows // self.nzp
        return pl.ds(pl.multiple_of((q % self.nzp) * n, 16), n)

    def spread(self):
        e = self.env
        mine = self.acc(e.me)
        out = []
        for k in range(1, e.nz):
            q = (e.zi + k) % e.nz
            out.append(e.pool.copy(mine.at[self.piece(q)], self.zbuf(k), (q * 2 + e.core, e.me)))
        self.now = self.keep(out)

    def spread_end(self):
        e = self.env
        landed(self.now)
        own = self.acc(e.me).at[self.piece(e.zi)]
        self.zbuf(0)[...] = own[...]
        total = None
        for z in range(e.nz):
            term = self.zbuf((e.zi - z + e.nz) % e.nz)[...].astype(F32)
            total = term if total is None else total + term
        self.zbuf(0)[...] = total.astype(BF16)

    def collect(self):
        e = self.env
        home = pltpu.make_async_copy(self.zbuf(0), self.final(e.me, self.piece(e.zi)), e.lsem.at[e.nl])
        e.nl += 1
        home.start()
        e.homes.append(home)
        out = []
        g0 = (e.zi // self.nzp) * self.nzp
        for k in range(1, self.nzp):
            q = g0 + (e.zi - g0 + k) % self.nzp
            out.append(e.pool.copy(self.zbuf(0), self.final(e.me, self.piece(e.zi)), (q * 2 + e.core, e.me)))
        self.now = self.keep(out)
        self.home = home

    def collect_end(self):
        landed(self.now)
        self.home.wait()

    def double(self, t):
        e, o = self.env, self.order
        bit = o[t]
        out = []
        for sub in subsets(o[:t]):
            v = self.final(flips(e.me, sub), None)
            out.append(e.pool.copy(v, v, (e.dp, flip(e.me, bit))))
        self.now = self.keep(out)

    def double_end(self, t):
        landed(self.now)


class Env:
    pass


KEY, VALUE, RECEPT, OUT, CMR = range(5)
V_LN1G, V_LN1B, V_TD, V_TF, V_MK, V_MV, V_MR, V_LN2G, V_LN2B, V_CMK, V_CMR = range(11)


def back_kernel(
    L, tok, par, edge, g2, gck, gcr, x1, y, sr, wkv, rd, a, v, xk, xv, xr, wk, wv, wr, wo, dkh, dvh, dch,
    ig_o, dkr, dvr, rep, vec_o,
    gck_s, gcr_s, x1_s, sr_s, wkv_s, rd_s, v_s, g2_s, y_s, xr_s, gr_s, gk_s, gv_s, w3, dw, acc1,
    inc, r1, r2, z1, z2, grow, fade, tri, ent, st_out, st_in, carry, gpad, tpad, vacc, vown, vf, vd, dev_in,
    blk_sem, in_sem, out_sem, e_ssem, e_rsem, s_ssem, s_rsem, v_ssem, v_rsem, lsem, p_ssem, p_rsem,
):
    D, BR, n_f, n_dp, U, R = L.D, L.BR, L.n_f, L.n_dp, L.U, L.R
    dp, me = lax.axis_index("dp"), lax.axis_index("ffn")
    core = dp % 2
    buddy = dp + 1 - 2 * core
    place = me % L.per_slot
    opens = jnp.where(place == 0, 0.0, 1.0).astype(F32)
    stays = jnp.where(place == L.per_slot - 1, 0.0, 1.0).astype(F32)
    half = D // 2

    blocks = ((gck, gck_s), (gcr, gcr_s), (x1, x1_s), (g2, g2_s), (sr, sr_s), (wkv, wkv_s), (rd, rd_s))

    def load(i, which):
        r = rows_of(i, BR)
        return [pltpu.make_async_copy(blocks[n][0].at[r], blocks[n][1].at[r], blk_sem.at[n, i]) for n in which]

    wo_cp = pltpu.make_async_copy(wo, w3.at[2], in_sem.at[0])
    begin(load(0, range(7)) + [wo_cp])
    for i in range(1, L.nblk):
        begin(load(i, range(7)))
    accs = [pltpu.make_async_copy(g, acc1.at[n], in_sem.at[1 + n]) for n, g in enumerate((dkh, dvh))]
    y_cp = pltpu.make_async_copy(y, y_s, in_sem.at[3])
    xr_cp = pltpu.make_async_copy(xr, xr_s, in_sem.at[4])
    v_cp = pltpu.make_async_copy(v, v_s, in_sem.at[5])
    dc_cps = [
        pltpu.make_async_copy(dch.at[:, pl.ds(h * half, half)], dw.at[CMR, h], in_sem.at[6 + h]) for h in range(2)
    ]
    w_cps = [pltpu.make_async_copy(w, w3.at[n], in_sem.at[8 + n]) for n, w in enumerate((wk, wv))]
    begin(accs + dc_cps + [y_cp, xr_cp, v_cp] + w_cps)

    greet(
        [(dp, (me + k) % n_f) for k in range(1, n_f)] + [((dp + k) % n_dp, me) for k in range(1, n_dp)]
    )

    prv = (me + n_f - 1) % n_f
    edges = begin([
        remote(g.at[pl.ds(0, 8)], gpad.at[n], e_ssem.at[n], e_rsem.at[n], (dp, prv)) for n, g in enumerate((gck, gcr))
    ])

    e = Env()
    e.me, e.dp, e.core, e.nz, e.zi = me, dp, core, L.nz, dp // 2
    e.pool, e.lsem, e.nl, e.homes = Pool(p_ssem, p_rsem), lsem, 0, []

    hk = half // L.parts
    big = []
    for n, res in enumerate((dkr, dvr)):
        for p in range(L.parts):
            off = p * hk

            def acc(j, n=n, off=off):
                return acc1.at[n, j, pl.ds(off, hk)]

            def rbuf(k, n=n, p=p):
                return r1.at[n, p, k]

            def zbuf(k, n=n, p=p):
                return z1.at[n, p, k]

            def final(j, r, res=res, off=off):
                return res.at[pl.ds(pl.multiple_of(core * half + off + r.start, 16), r.size)]

            big.append(Unit(e, L.order(p), hk, acc, rbuf, zbuf, final))
    shard = D // n_f
    small = []
    for m in range(5):
        def acc(j, m=m):
            return dw.at[m, core, pl.ds(pl.multiple_of(j * shard, 16), shard)]

        def rbuf(k, m=m):
            return r2.at[m, k]

        def zbuf(k, m=m):
            return z2.at[m, k]

        def final(j, r, m=m):
            r0, n = (j * shard, shard) if r is None else (j * shard + r.start, r.size)
            return rep.at[m, pl.ds(pl.multiple_of(r0, 16), n), pl.ds(pl.multiple_of(core * half, 128), half)]

        small.append(Unit(e, L.order(0) if m in (CMR, KEY) else L.order(1), shard, acc, rbuf, zbuf, final))

    def source(n, p):
        g, off = (dkh, dvh)[n], p * hk
        return lambda j: g.at[j, pl.ds(off, hk)]

    for n in range(2):
        for p in range(L.parts):
            big[n * L.parts + p].halve(0, source(n, p))

    def swap(m):
        u = small[m]
        u.now = u.keep([e.pool.copy(dw.at[m, 1 - core], inc.at[m % 4], (buddy, me))])

    def swap_end(m):
        landed(small[m].now)
        dw[m, core] = (dw[m, core].astype(F32) + inc[m % 4].astype(F32)).astype(BF16)

    w = jnp.exp(par[TD : TD + 1, :])
    ew = jnp.exp(w)
    eu = jnp.exp(par[TF : TF + 1, :])
    age = lax.broadcasted_iota(jnp.int32, (SPAN, D), 0).astype(F32) * w
    grow[...] = jnp.exp(age)
    fade[...] = jnp.exp(-age)
    tri[...] = tri_pair(False)
    full_fade = jnp.exp(-float(SPAN) * w)
    tail_fade = jnp.exp(-float(SPAN - 1) * w)
    vacc[...] = jnp.zeros_like(vacc)
    carry[...] = edge[8:16, :]

    def add_up(n, x):
        vacc[n] = vacc[n] + jnp.sum(x.reshape(-1, 8, D), axis=0)

    for cp in dc_cps:
        cp.wait()
    swap(CMR)
    wo_cp.wait()
    for cp in load(0, (0, 1)):
        cp.wait()

    def phase_1(i, _):
        @pl.when(i + 1 < L.nblk)
        def _wait():
            for cp in load(i + 1, (0, 1)):
                cp.wait()

        for cp in load(i, range(2, 7)):
            cp.wait()
        r = rows_of(i, BR)
        win = pl.ds(pl.multiple_of(i * BR, 8), BR + 8)
        mk, mr = par[CK : CK + 1, :], par[CR : CR + 1, :]
        gk = gck_s[win, :]
        gr = gcr_s[win, :]
        t = gk * (1.0 - mk) + gr * (1.0 - mr)
        t = pltpu.roll(t, BR + 7, 0)[:BR]
        gk, gr = gk[:BR], gr[:BR]
        gn = gk * mk + gr * mr + t
        n2, rs = normed(x1_s[r, :])
        norm2 = n2 * par[G2 : G2 + 1, :] + par[B2 : B2 + 1, :]
        prev = pltpu.roll(jnp.concatenate([carry[...], norm2], axis=0), 1, 0)[8:]
        carry[...] = norm2[BR - 8 :]
        d = norm2 - prev
        add_up(V_CMK, gk * d)
        add_up(V_CMR, gr * d)
        add_up(V_LN2G, gn * n2)
        add_up(V_LN2B, gn)
        q1 = gn * par[G2 : G2 + 1, :]
        m1 = jnp.mean(q1, axis=-1, keepdims=True)
        m2 = jnp.mean(q1 * n2, axis=-1, keepdims=True)
        g1 = g2_s[r, :].astype(F32) + (q1 - m1 - n2 * m2) * rs
        x1_s[r, :] = g1
        ga = g1.astype(BF16)
        g2_s[r, :] = ga
        s = sr_s[r, :]
        gys = dot(ga, w3[2], 1, 1) * s
        wk_ = wkv_s[r, :]
        gr_s[r, :] = (gys * wk_ * (1.0 - s)).astype(BF16)
        q = gys * rd_s[r, :]
        qw = q * wk_
        rd_s[r, :] = q
        wkv_s[r, :] = qw
        for sb in range(BR // SPAN):
            b = i * (BR // SPAN) + sb
            rb = rows_of(b, SPAN)
            sl = slice(sb * SPAN, (sb + 1) * SPAN)
            fd = fade[...]
            both = jnp.concatenate([fd * q[sl], fd * qw[sl]], axis=1)
            suf = dot(tri[...], split2(both))
            gs = grow[...] * ew
            gck_s[rb, :] = gs * suf[:, :D]
            gcr_s[rb, :] = gs * suf[:, D:]
            tot = suf[0:1] + both[0:1]
            ent[b, 0:1, :] = tot[:, :D]
            ent[b, 1:2, :] = tot[:, D:]
        return 0

    lax.fori_loop(0, L.nblk // 2, phase_1, 0)
    swap_end(CMR)
    small[CMR].halve(0)
    lax.fori_loop(L.nblk // 2, L.nblk - 1, phase_1, 0)
    for cp in edges:
        cp.wait()
    gck_s[R : R + 8, :] = gpad[0] * stays
    gcr_s[R : R + 8, :] = gpad[1] * stays
    phase_1(L.nblk - 1, 0)

    xq = jnp.zeros((1, D), F32)
    xw = jnp.zeros((1, D), F32)
    for b in reversed(range(L.nspan)):
        tq, tw = ent[b, 0:1, :], ent[b, 1:2, :]
        ent[b, 0:1, :] = xq
        ent[b, 1:2, :] = xw
        xq = tq + full_fade * xq
        xw = tw + full_fade * xw
    st_out[...] = jnp.zeros_like(st_out)
    st_out[0:1, :] = xq
    st_out[1:2, :] = xw
    states = begin([
        remote(st_out, st_in.at[k], s_ssem.at[k], s_rsem.at[k], (dp, (me + n_f - k) % n_f)) for k in range(1, n_f)
    ])
    a_cp = pltpu.make_async_copy(a, sr_s, in_sem.at[11])
    a_cp.start()
    w_cps.append(pltpu.make_async_copy(wr, w3.at[2], in_sem.at[10]))
    w_cps[-1].start()

    def product(m, left, right):
        for c in range(D // BR):
            rr = slice(c * BR, (c + 1) * BR)
            full = dot(left[:, rr], right[...], 0, 0).astype(BF16)
            dw[m, 0, rr, :] = full[:, :half]
            dw[m, 1, rr, :] = full[:, half:]

    for cp in accs:
        cp.wait()
    n1 = L.parts
    for u in big[:n1]:
        u.halve_end(0)
        u.halve(1 % L.bits) if L.bits > 1 else None
    y_cp.wait()
    product(OUT, y_s, g2_s)
    swap(OUT)
    xk_cp = pltpu.make_async_copy(xk, y_s, in_sem.at[12])
    tok_cp = pltpu.make_async_copy(tok, g2_s, in_sem.at[13])
    begin([xk_cp, tok_cp])
    xr_cp.wait()
    product(RECEPT, xr_s, gr_s)
    swap(RECEPT)
    xv_cp = pltpu.make_async_copy(xv, xr_s, in_sem.at[14])
    xv_cp.start()
    small[CMR].halve_end(0)
    small[CMR].halve(1)

    for cp in states:
        cp.wait()
    qi = jnp.zeros((1, D), F32)
    wi = jnp.zeros((1, D), F32)
    for k in range(1, L.per_slot):
        f = jnp.exp(-float((k - 1) * R) * w) * jnp.where(place + k < L.per_slot, 1.0, 0.0).astype(F32)
        qi = qi + f * st_in[k, 0:1, :]
        wi = wi + f * st_in[k, 1:2, :]
    dev_in[0:1, :] = qi
    dev_in[1:2, :] = wi
    a_cp.wait()
    v_cp.wait()
    first = place * R - (L.per_slot * R) // 2

    def phase_2(b, _):
        rb = rows_of(b, SPAN)
        fb = jnp.exp(w * ((b + 1 - L.nspan) * SPAN).astype(F32))
        eq = ent[b, 0:1, :] + fb * dev_in[0:1, :]
        ewk = ent[b, 1:2, :] + fb * dev_in[1:2, :]
        ff = grow[...] * tail_fade
        q, qw, av, vv = rd_s[rb, :], wkv_s[rb, :], sr_s[rb, :], v_s[rb, :]
        gvr = av * (eu * q + gck_s[rb, :] + ff * eq)
        gkr = vv * gvr - av * (eu * qw + gcr_s[rb, :] + ff * ewk)
        gk_s[rb, :] = gkr.astype(BF16)
        gv_s[rb, :] = gvr.astype(BF16)
        add_up(V_TF, eu * av * (q * vv - qw))
        pos = (first + b * SPAN + lax.broadcasted_iota(jnp.int32, (SPAN, 1), 0)).astype(F32)
        add_up(V_TD, pos * gkr)
        return 0

    lax.fori_loop(0, L.nspan, phase_2, 0)
    swap_end(OUT)
    small[OUT].halve(0)
    swap_end(RECEPT)
    small[RECEPT].halve(0)
    xk_cp.wait()
    product(KEY, y_s, gk_s)
    swap(KEY)
    xv_cp.wait()
    product(VALUE, xr_s, gv_s)
    swap(VALUE)
    for u in big[n1:]:
        u.halve_end(0)
        u.halve(1)
    for u in big[:n1]:
        for t in range(1, L.bits):
            u.halve_end(t)
            if t + 1 < L.bits:
                u.halve(t + 1)
        u.spread()
    swap_end(KEY)
    small[KEY].halve(0)
    swap_end(VALUE)
    small[VALUE].halve(0)

    for cp in w_cps:
        cp.wait()
    tok_cp.wait()
    carry[...] = edge[0:8, :]

    def phase_3(i, _):
        r = rows_of(i, BR)
        mk, mv, mr = par[MK : MK + 1, :], par[MV : MV + 1, :], par[MR : MR + 1, :]
        n1_, _rs = normed(g2_s[r, :].astype(F32))
        norm1 = n1_ * par[G1 : G1 + 1, :] + par[B1 : B1 + 1, :]
        prev = pltpu.roll(jnp.concatenate([carry[...], norm1], axis=0), 1, 0)[8:]
        carry[...] = norm1[BR - 8 :]
        d = norm1 - prev
        gxk = dot(gk_s[r, :], w3[0], 1, 1)
        gxv = dot(gv_s[r, :], w3[1], 1, 1)
        gxr = dot(gr_s[r, :], w3[2], 1, 1)
        add_up(V_MK, gxk * d)
        add_up(V_MV, gxv * d)
        add_up(V_MR, gxr * d)
        now = gxk * mk + gxv * mv + gxr * mr
        gck_s[r, :] = gxk + gxv + gxr - now
        gcr_s[r, :] = now
        return 0

    lax.fori_loop(0, L.nblk // 2, phase_3, 0)
    t_cp = remote(gck_s.at[pl.ds(0, 8)], tpad, e_ssem.at[2], e_rsem.at[2], (dp, prv))
    t_cp.start()

    def rest_of_halving(u):
        for t in range(1, L.bits):
            u.halve_end(t)
            if t + 1 < L.bits:
                u.halve(t + 1)
        u.spread()

    rest_of_halving(small[CMR])
    for m in (OUT, RECEPT):
        small[m].halve_end(0)
        small[m].halve(1)
    for u in big[n1:]:
        rest_of_halving(u)
    lax.fori_loop(L.nblk // 2, L.nblk, phase_3, 0)
    for u in big[:n1]:
        u.spread_end()
        u.collect()
    for m in (KEY, VALUE):
        small[m].halve_end(0)
        small[m].halve(1)
    t_cp.wait()
    gck_s[R : R + 8, :] = tpad[...] * stays

    def phase_4(i, _):
        r = rows_of(i, BR)
        t = gck_s[pl.ds(pl.multiple_of(i * BR, 8), BR + 8), :]
        gn = gcr_s[r, :] + pltpu.roll(t, BR + 7, 0)[:BR]
        n1_, rs = normed(g2_s[r, :].astype(F32))
        add_up(V_LN1G, gn * n1_)
        add_up(V_LN1B, gn)
        q1 = gn * par[G1 : G1 + 1, :]
        m1 = jnp.mean(q1, axis=-1, keepdims=True)
        m2 = jnp.mean(q1 * n1_, axis=-1, keepdims=True)
        g2_s[r, :] = (x1_s[r, :] + (q1 - m1 - n1_ * m2) * rs).astype(BF16)
        pltpu.make_async_copy(g2_s.at[r], ig_o.at[r], out_sem.at[i]).start()
        return 0

    lax.fori_loop(0, L.nblk, phase_4, 0)
    vown[...] = jnp.sum(vacc[...], axis=1)
    vf[0] = vown[...]
    vs = begin([
        remote(vown, vf.at[k], v_ssem.at[0, k], v_rsem.at[0, k], (dp, (me + k) % n_f)) for k in range(1, n_f)
    ])
    for m in (OUT, RECEPT):
        rest_of_halving(small[m])
    small[CMR].spread_end()
    small[CMR].collect()
    for cp in vs:
        cp.wait()
    total = vf[(me + n_f) % n_f]
    for f in range(1, n_f):
        total = total + vf[(me - f + n_f) % n_f]
    vd[0] = total
    vs = begin([
        remote(vd.at[0], vd.at[k], v_ssem.at[1, k], v_rsem.at[1, k], ((dp + k) % n_dp, me)) for k in range(1, n_dp)
    ])
    for m in (KEY, VALUE):
        rest_of_halving(small[m])
    for m in (OUT, RECEPT):
        small[m].spread_end()
        small[m].collect()
    for u in big[n1:]:
        u.spread_end()
        u.collect()
    for m in (KEY, VALUE):
        small[m].spread_end()
        small[m].collect()
    for cp in vs:
        cp.wait()
    total = vd[dp % n_dp]
    for f in range(1, n_dp):
        total = total + vd[(dp - f + n_dp) % n_dp]
    vec_o[...] = total
    vec_o[V_TD : V_TD + 1, :] = w * (total[V_TD : V_TD + 1] - total[V_TF : V_TF + 1])

    order = (CMR, OUT, RECEPT, KEY, VALUE)
    for t in range(L.bits):
        for m in order:
            if t == 0:
                small[m].collect_end()
            else:
                small[m].double_end(t - 1)
            small[m].double(t)
    cross = []
    for n, res in enumerate((dkr, dvr)):
        for u in big[n * n1 : (n + 1) * n1]:
            u.collect_end()
        rr = pl.ds(pl.multiple_of(core * half, 16), half)
        cross += begin([e.pool.copy(res.at[rr], res.at[rr], (buddy, me))])
    for m in order:
        small[m].double_end(L.bits - 1)
        cc = pl.ds(pl.multiple_of(core * half, 128), half)
        cross += begin([e.pool.copy(rep.at[m, :, cc], rep.at[m, :, cc], (buddy, me))])
    for cp in cross:
        cp.wait()
    for u in big + small:
        for cp in u.sent:
            cp.wait_send()
    for i in range(L.nblk):
        pltpu.make_async_copy(g2_s.at[rows_of(i, BR)], ig_o.at[rows_of(i, BR)], out_sem.at[i]).wait()


def back(L, *args):
    R, D, n_f, n_dp, U = L.R, L.D, L.n_f, L.n_dp, L.U
    half, shard = D // 2, D // L.n_f
    hk = half // L.parts
    dma = pltpu.SemaphoreType.DMA
    fpad, full, low = pltpu.VMEM((R + 8, D), F32), pltpu.VMEM((R, D), F32), pltpu.VMEM((R, D), BF16)
    rows8 = pltpu.VMEM((8, D), F32)
    zk = hk // z_pieces(hk, L.nz)
    zs = shard // z_pieces(shard, L.nz)
    n_r = n_f - 1
    per_unit = n_r + (L.nz - 1) * 2
    n_pool = 2 * L.parts * per_unit + 5 * (per_unit + 1 + n_r) + 7
    return pl.pallas_call(
        functools.partial(back_kernel, L),
        out_shape=(
            sds((R, D), BF16), sds((D, U), BF16), sds((D, U), BF16), sds((5, D, D), BF16), sds((16, D)),
        ),
        in_specs=[ANY, VMEM, VMEM] + [ANY] * 20,
        out_specs=(ANY, ANY, ANY, ANY, VMEM),
        scratch_shapes=[
            fpad, fpad, full, full, full, full, full, low, low, low, low, low, low,
            pltpu.VMEM((3, D, D), BF16), pltpu.VMEM((5, 2, D, half), BF16), pltpu.VMEM((2, n_f, half, U), BF16),
            pltpu.VMEM((4, D, half), BF16), pltpu.VMEM((2, L.parts, n_r, hk, U), BF16),
            pltpu.VMEM((5, n_r, shard, half), BF16), pltpu.VMEM((2, L.parts, L.nz, zk, U), BF16),
            pltpu.VMEM((5, L.nz, zs, half), BF16),
            pltpu.VMEM((SPAN, D), F32), pltpu.VMEM((SPAN, D), F32), pltpu.VMEM((SPAN, 2 * SPAN), BF16),
            pltpu.VMEM((L.nspan, 8, D), F32), rows8, pltpu.VMEM((n_f, 8, D), F32), rows8,
            pltpu.VMEM((2, 8, D), F32), rows8, pltpu.VMEM((16, 8, D), F32), pltpu.VMEM((16, D), F32),
            pltpu.VMEM((n_f, 16, D), F32), pltpu.VMEM((n_dp, 16, D), F32), rows8,
            dma((7, L.nblk)), dma((15,)), dma((L.nblk,)), dma((3,)), dma((3,)), dma((n_f,)), dma((n_f,)),
            dma((2, n_dp)), dma((2, n_dp)), dma((16,)), dma((n_pool,)), dma((n_pool,)),
        ],
        compiler_params=pltpu.CompilerParams(collective_id=2, has_side_effects=True, vmem_limit_bytes=VLIMIT),
        cost_estimate=pl.CostEstimate(flops=20 * R * D * D, bytes_accessed=60 * R * D, transcendentals=0),
        name="back",
    )(*args)


def solution(mesh):
    def step(
        tokens, lens, og, ln1g, ln1b, td, tf, mk, mv, mr, wk, wv, wr, wo, ln2g, ln2b, cmk, cmr, ckw, cvw, wc
    ):
        L = Layout(mesh, tokens.shape[0], tokens.shape[1], ckw.shape[1])
        rows = [ln1g, ln1b, td, tf, mk, mv, mr, ln2g, ln2b, cmk, cmr]
        par = jnp.stack(rows + [ln1g] * (16 - len(rows)))
        xk, xv, xr, y, ck, cr, a, v, rd, wkv, sr, x1, gate, edge, kall, vall = front(
            L, tokens, par, wk, wv, wr, wo, wc, ckw, cvw
        )
        mixed, g2, gck, gcr, dkh, dvh, dc = middle(L, lens, ck, cr, x1, gate, og, kall, vall, wc)
        ig, dkr, dvr, rep, vec = back(
            L, tokens, par, edge, g2, gck, gcr, x1, y, sr, wkv, rd, a, v, xk, xv, xr, wk, wv, wr, wo, dkh, dvh, dc
        )
        return (
            mixed, ig,
            *[vec[n] for n in range(7)],
            *[rep[m].astype(F32) for m in (KEY, VALUE, RECEPT, OUT)],
            *[vec[n] for n in range(7, 11)],
            dkr.astype(F32), dvr.astype(F32).T, rep[CMR].astype(F32),
        )

    row, none = P(("dp", "ffn"), None), P()
    return jax.shard_map(
        step,
        mesh=mesh,
        in_specs=(row, P("dp"), row) + (none,) * 15 + (P(None, "ffn"), P("ffn", None), none),
        out_specs=(row, row) + (none,) * 15 + (P(None, "ffn"), P("ffn", None), none),
        check_vma=False,
    )
```

```python
import functools

import jax
import jax.numpy as jnp
from jax import lax
from jax.experimental import pallas as pl
from jax.experimental.pallas import tpu as pltpu
from jax.sharding import PartitionSpec as P

MAX_LEN = 4096
SPAN = 128
EPS = 1e-05
MESH = pl.DeviceIdType.MESH
F32 = jnp.float32
BF16 = jnp.bfloat16
ANY = pl.BlockSpec(memory_space=pl.ANY)
VMEM = pl.BlockSpec(memory_space=pltpu.VMEM)
SMEM = pl.BlockSpec(memory_space=pltpu.SMEM)
VLIMIT = 62 * 2**20
G1, B1, TD, TF, MK, MV, MR, G2, B2, CK, CR = range(11)
NVEC = 11


def dot(a, b, da=1, db=0):
    return lax.dot_general(a, b, (((da,), (db,)), ((), ())), preferred_element_type=F32)


def sds(shape, dtype=F32):
    return jax.ShapeDtypeStruct(shape, dtype)


def flip(i, bit):
    s = 1 << bit
    return i + s - 2 * s * ((i // s) % 2)


def rows_of(i, n):
    return pl.ds(pl.multiple_of(i * n, n), n)


def sigmoid(x):
    return 1.0 / (1.0 + jnp.exp(-x))


def normed(x):
    c = x - jnp.mean(x, axis=-1, keepdims=True)
    rs = lax.rsqrt(jnp.mean(c * c, axis=-1, keepdims=True) + EPS)
    return c * rs, rs


def split2(x):
    hi = x.astype(BF16)
    lo = (x - hi.astype(F32)).astype(BF16)
    return jnp.concatenate([hi, lo], axis=0)


def tri_pair(below):
    r = lax.broadcasted_iota(jnp.int32, (SPAN, 2 * SPAN), 0)
    c = lax.broadcasted_iota(jnp.int32, (SPAN, 2 * SPAN), 1) % SPAN
    keep = (r > c) if below else (r < c)
    return jnp.where(keep, 1.0, 0.0).astype(BF16)


def greet(peers):
    bar = pltpu.get_barrier_semaphore()
    for p in peers:
        pl.semaphore_signal(bar, inc=1, device_id=p, device_id_type=MESH)
    pl.semaphore_wait(bar, len(peers))


def remote(src, dst, ssem, rsem, dev):
    return pltpu.make_async_remote_copy(
        src_ref=src, dst_ref=dst, send_sem=ssem, recv_sem=rsem, device_id=dev, device_id_type=MESH
    )


class Layout:
    def __init__(self, mesh, rows, width, local_units):
        self.n_f = mesh.shape["ffn"]
        self.n_dp = mesh.shape["dp"]
        self.R = rows
        self.D = width
        self.U = local_units
        self.BR = 256
        self.nblk = rows // self.BR
        self.nspan = rows // SPAN
        slot_len = min(MAX_LEN, rows * self.n_f)
        self.per_slot = slot_len // rows
        self.bits = self.n_f.bit_length() - 1
        self.parts = 2 if self.bits == 2 else 1
        self.nz = self.n_dp // 2

    def order(self, part):
        b = list(range(self.bits))
        return b if part == 0 else b[::-1]


def flips(i, mask):
    b = 0
    while mask >> b:
        if (mask >> b) & 1:
            i = flip(i, b)
        b += 1
    return i


def spans(bits):
    out = [0]
    for b in bits:
        out = out + [m | (1 << b) for m in out]
    return out


def gather_steps(L):
    steps, flat = [], 0
    for t in range(L.bits):
        here = []
        for p in range(L.parts):
            o = L.order(p)
            for m in spans(o[:t]):
                here.append((p, o[t], m, flat))
                flat += 1
        steps.append(here)
    return steps, flat


class Gather:
    def __init__(self, L, core, dp, me, half, source, dest, sems):
        self.L, self.half, self.source, self.dest = L, half, source, dest
        self.core, self.dp, self.me = core, dp, me
        self.g_ssem, self.g_rsem, self.c_ssem, self.c_rsem = sems
        self.steps, _ = gather_steps(L)

    def rows(self, p):
        n = self.half // self.L.parts
        return pl.ds(pl.multiple_of(self.core * self.half + p * n, 16), n)

    def link(self, t):
        return [
            remote(self.source(m, self.rows(p)), self.dest(m | (1 << bit), self.rows(p)),
                   self.g_ssem.at[f], self.g_rsem.at[f], (self.dp, flip(self.me, bit)))
            for p, bit, m, f in self.steps[t]
        ]

    def across(self, t):
        buddy = self.dp + 1 - 2 * self.core
        out = []
        for p, bit, m, f in self.steps[t]:
            ref = self.dest(m | (1 << bit), self.rows(p))
            out.append(remote(ref, ref, self.c_ssem.at[f], self.c_rsem.at[f], (buddy, self.me)))
        return out


def front_kernel(
    L, tok, *refs
):
    vecs, refs = refs[:NVEC], refs[NVEC:]
    (
        wk, wv, wr, wo, wc, kshard, vshard,
        xk_o, xv_o, xr_o, y_o, ck_o, cr_o, a_o, v_o, rd_o, wkv_o, sr_o, x1_o, gate_o, edge_o, par, kall, vall,
        tokv, w5, npad, xk_s, xv_s, xr_s, y_s, ck_s, cr_s, a_s, v_s, S_s, D_s, sr_s, x1_s, gate_s,
        grow, fade, tri, ent, st_out, st_in, tedge, nedge, dev_in,
        in_sem, out_sem, e_ssem, e_rsem, s_ssem, s_rsem, g_ssem, g_rsem, c_ssem, c_rsem,
    ) = refs
    D, BR, n_f = L.D, L.BR, L.n_f
    dp, me = lax.axis_index("dp"), lax.axis_index("ffn")
    core = dp % 2
    buddy = dp + 1 - 2 * core
    place = me % L.per_slot
    keep = jnp.where(place == 0, 0.0, 1.0).astype(F32)
    ins = [pltpu.make_async_copy(tok, tokv, in_sem.at[0])]
    for n, w in enumerate((wk, wv, wr, wo, wc)):
        ins.append(pltpu.make_async_copy(w, w5.at[n], in_sem.at[1 + n]))
    for cp in ins:
        cp.start()
    greet([(dp, (me + k) % n_f) for k in range(1, n_f)] + [(buddy, me)])

    nxt = (me + 1) % n_f
    tok_edge = remote(tok.at[pl.ds(L.R - 16, 16)], tedge, e_ssem.at[0], e_rsem.at[0], (dp, nxt))
    tok_edge.start()

    def gather(n, shard, full, half):
        return Gather(
            L, core, dp, me, half,
            lambda m, r: full.at[m, r] if m else shard.at[r],
            lambda m, r: full.at[m, r],
            (g_ssem.at[n], g_rsem.at[n], c_ssem.at[n], c_rsem.at[n]),
        )

    keys, values = gather(0, kshard, kall, D // 2), gather(1, vshard, vall, L.U // 2)
    for cp in keys.link(0) + values.link(0):
        cp.start()
    for n in range(NVEC):
        par[n : n + 1, :] = vecs[n][...].reshape(1, D)

    w = jnp.exp(par[TD : TD + 1, :])
    ew = jnp.exp(w)
    eu = jnp.exp(par[TF : TF + 1, :])
    age = lax.broadcasted_iota(jnp.int32, (SPAN, D), 0).astype(F32) * w
    grow[...] = jnp.exp(age)
    fade[...] = jnp.exp(-age)
    tri[...] = tri_pair(True)
    full_fade = jnp.exp(-float(SPAN) * w)
    tail_fade = jnp.exp(-float(SPAN - 1) * w)
    st_out[...] = jnp.zeros_like(st_out)

    ins[0].wait()
    tok_edge.wait()
    en, _ = normed(tedge[...].astype(F32))
    en = (en * par[G1 : G1 + 1, :] + par[B1 : B1 + 1, :])[8:16] * keep
    npad[0:8, :] = en
    edge_o[0:8, :] = en
    for cp in ins[1:4]:
        cp.wait()

    outs_a = ((xk_s, xk_o), (xv_s, xv_o), (xr_s, xr_o), (a_s, a_o), (v_s, v_o), (sr_s, sr_o))
    outs_c = ((y_s, y_o), (S_s, wkv_o), (D_s, rd_o), (x1_s, x1_o))
    outs_d = ((ck_s, ck_o), (cr_s, cr_o), (gate_s, gate_o))

    def ship(outs, base, i):
        return [
            pltpu.make_async_copy(s.at[rows_of(i, BR)], o.at[rows_of(i, BR)], out_sem.at[base + n, i])
            for n, (s, o) in enumerate(outs)
        ]

    def phase_a(i, carry):
        r = rows_of(i, BR)
        n1, _ = normed(tokv[r, :].astype(F32))
        n1 = n1 * par[G1 : G1 + 1, :] + par[B1 : B1 + 1, :]
        npad[pl.ds(pl.multiple_of(i * BR + 8, 8), BR), :] = n1
        prev = pltpu.roll(npad[pl.ds(pl.multiple_of(i * BR, 8), BR + 8), :], 1, 0)[8:]
        d = n1 - prev
        xk = (prev + d * par[MK : MK + 1, :]).astype(BF16)
        xv = (prev + d * par[MV : MV + 1, :]).astype(BF16)
        xr = (prev + d * par[MR : MR + 1, :]).astype(BF16)
        xk_s[r, :] = xk
        xv_s[r, :] = xv
        xr_s[r, :] = xr
        a = jnp.exp(dot(xk, w5[0]))
        v = dot(xv, w5[1])
        a_s[r, :] = a
        v_s[r, :] = v
        for sb in range(BR // SPAN):
            b = i * (BR // SPAN) + sb
            aa = a[sb * SPAN : (sb + 1) * SPAN]
            vv = v[sb * SPAN : (sb + 1) * SPAN]
            ga = grow[...] * aa
            both = jnp.concatenate([ga * vv, ga], axis=1)
            pre = dot(tri[...], split2(both))
            fs = fade[...] * ew
            S_s[rows_of(b, SPAN), :] = fs * pre[:, :D]
            D_s[rows_of(b, SPAN), :] = fs * pre[:, D:]
            tot = pre[SPAN - 1 : SPAN] + both[SPAN - 1 : SPAN]
            num, den = st_out[0:1, :], st_out[1:2, :]
            ent[b, 0:1, :] = num
            ent[b, 1:2, :] = den
            st_out[0:1, :] = full_fade * num + tail_fade * tot[:, :D]
            st_out[1:2, :] = full_fade * den + tail_fade * tot[:, D:]
        sr_s[r, :] = sigmoid(dot(xr, w5[2]))
        for cp in ship(outs_a, 0, i):
            cp.start()
        return carry

    lax.fori_loop(0, L.nblk, phase_a, 0)

    states = [
        remote(st_out, st_in.at[k], s_ssem.at[k], s_rsem.at[k], (dp, (me + k) % n_f)) for k in range(1, n_f)
    ]
    for cp in states:
        cp.start()

    for cp in keys.link(0):
        cp.wait_recv()
    for t in range(1, L.bits):
        for cp in keys.link(t):
            cp.start()
        if t < L.bits - 1:
            for cp in keys.link(t):
                cp.wait_recv()
    for cp in values.link(0):
        cp.wait_recv()
    for t in range(L.bits - 1):
        for cp in keys.across(t):
            cp.start()
    for cp in values.across(0):
        cp.start()

    for cp in states:
        cp.wait()
    num_in = jnp.zeros((1, D), F32)
    den_in = jnp.zeros((1, D), F32)
    for k in range(1, L.per_slot):
        ok = jnp.where(place >= k, 1.0, 0.0).astype(F32)
        f = jnp.exp(-float((k - 1) * L.R) * w) * ok
        num_in = num_in + f * st_in[k, 0:1, :]
        den_in = den_in + f * st_in[k, 1:2, :]
    dev_in[0:1, :] = num_in
    dev_in[1:2, :] = den_in
    for cp in ins[4:]:
        cp.wait()

    def phase_c(i, carry):
        r = rows_of(i, BR)
        for sb in range(BR // SPAN):
            b = i * (BR // SPAN) + sb
            rb = rows_of(b, SPAN)
            fb = jnp.exp(w * (b * (-SPAN)).astype(F32))
            en = ent[b, 0:1, :] + fb * dev_in[0:1, :]
            ed = ent[b, 1:2, :] + fb * dev_in[1:2, :]
            F = eu * a_s[rb, :]
            fd = fade[...]
            num = S_s[rb, :] + fd * en + F * v_s[rb, :]
            rd = 1.0 / (D_s[rb, :] + fd * ed + F)
            wkv = num * rd
            S_s[rb, :] = wkv
            D_s[rb, :] = rd
            y_s[rb, :] = (sr_s[rb, :] * wkv).astype(BF16)
        x1 = tokv[r, :].astype(F32) + dot(y_s[r, :], w5[3])
        x1_s[r, :] = x1
        n2, _ = normed(x1)
        npad[pl.ds(pl.multiple_of(i * BR + 8, 8), BR), :] = n2 * par[G2 : G2 + 1, :] + par[B2 : B2 + 1, :]
        for cp in ship(outs_c, 6, i):
            cp.start()
        return carry

    lax.fori_loop(0, L.nblk, phase_c, 0)

    n_edge = remote(npad.at[pl.ds(L.R, 8)], nedge, e_ssem.at[1], e_rsem.at[1], (dp, nxt))
    n_edge.start()

    def phase_d(ii, carry):
        i = L.nblk - 1 - ii
        r = rows_of(i, BR)
        win = npad[pl.ds(pl.multiple_of(i * BR, 8), BR + 8), :]
        prev = pltpu.roll(win, 1, 0)[8:]
        d = win[8:] - prev
        cr = (prev + d * par[CR : CR + 1, :]).astype(BF16)
        ck_s[r, :] = (prev + d * par[CK : CK + 1, :]).astype(BF16)
        cr_s[r, :] = cr
        gate_s[r, :] = sigmoid(dot(cr, w5[4]))
        for cp in ship(outs_d, 10, i):
            cp.start()
        return carry

    lax.fori_loop(0, L.nblk - 1, phase_d, 0)
    n_edge.wait()
    npad[0:8, :] = nedge[...] * keep
    edge_o[8:16, :] = nedge[...] * keep
    phase_d(L.nblk - 1, 0)

    for cp in keys.link(L.bits - 1):
        cp.wait_recv()
    for cp in keys.across(L.bits - 1):
        cp.start()
    for t in range(L.bits):
        for cp in keys.link(t):
            cp.wait_send()
        for cp in keys.across(t):
            cp.wait()
    for cp in values.link(0):
        cp.wait_send()
    for cp in values.across(0):
        cp.wait()

    def drain(i, carry):
        for outs, base in ((outs_a, 0), (outs_c, 6), (outs_d, 10)):
            for cp in ship(outs, base, i):
                cp.wait()
        return carry

    lax.fori_loop(0, L.nblk, drain, 0)


def front(L, tok, vecs, wk, wv, wr, wo, wc, kshard, vshard):
    R, D, n_f, U = L.R, L.D, L.n_f, L.U
    _, flat = gather_steps(L)
    rb, rf = sds((R, D), BF16), sds((R, D))
    dma = pltpu.SemaphoreType.DMA
    return pl.pallas_call(
        functools.partial(front_kernel, L),
        out_shape=(rb,) * 6 + (rf,) * 7 + (sds((16, D)), sds((16, D)), sds((n_f, D, U), BF16), sds((n_f, U, D), BF16)),
        in_specs=[ANY] + [VMEM] * NVEC + [ANY] * 7,
        out_specs=(ANY,) * 13 + (VMEM, VMEM, ANY, ANY),
        scratch_shapes=[
            pltpu.VMEM((R, D), BF16), pltpu.VMEM((5, D, D), BF16), pltpu.VMEM((R + 8, D), F32),
            *([pltpu.VMEM((R, D), BF16)] * 6), *([pltpu.VMEM((R, D), F32)] * 7),
            pltpu.VMEM((SPAN, D), F32), pltpu.VMEM((SPAN, D), F32), pltpu.VMEM((SPAN, 2 * SPAN), BF16),
            pltpu.VMEM((L.nspan, 8, D), F32), pltpu.VMEM((8, D), F32), pltpu.VMEM((n_f, 8, D), F32),
            pltpu.VMEM((16, D), BF16), pltpu.VMEM((8, D), F32), pltpu.VMEM((8, D), F32),
            dma((6,)), dma((13, L.nblk)), dma((2,)), dma((2,)), dma((n_f,)), dma((n_f,)),
            dma((2, flat)), dma((2, flat)), dma((2, flat)), dma((2, flat)),
        ],
        compiler_params=pltpu.CompilerParams(collective_id=0, has_side_effects=True, vmem_limit_bytes=VLIMIT),
        cost_estimate=pl.CostEstimate(flops=10 * R * D * D, bytes_accessed=40 * R * D, transcendentals=4 * R * D),
        name="front",
    )(tok, *vecs, wk, wv, wr, wo, wc, kshard, vshard)


def squeeze(mask, bit):
    return ((mask >> (bit + 1)) << bit) | (mask & ((1 << bit) - 1))


def middle_kernel(
    L, lens, ck, cr, x1, gate, og, kall, vall, kshard, vshard, wc,
    mixed_o, g2_o, gck_o, gcr_o, big_o, dc_o,
    kv, vv, wcv, ck_s, cr_s, x1_s, gate_s, og_s, mix_s, gv_s, gg_s, ckt_s, gvt_s, h_s, p_s, dk_s, dv_s, dc_s, inc, r0,
    in_sem, w_sem, out_sem, g_sem, x_ssem, x_rsem, h_ssem, h_rsem, g_ssem, g_rsem, c_ssem, c_rsem,
):
    BR, n_f, D, U = L.BR, L.n_f, L.D, L.U
    dp, me = lax.axis_index("dp"), lax.axis_index("ffn")
    core = dp % 2
    buddy = dp + 1 - 2 * core
    half = D // 2
    hk = half // L.parts
    length = lens[me // L.per_slot]
    start = (me % L.per_slot) * L.R
    masks = sorted(range(n_f), key=lambda m: (-bin(m).count("1"), m))

    def fetch(n, src, dst):
        return pltpu.make_async_copy(src, dst, w_sem.at[n])

    k_cp = [fetch(m, kall.at[m] if m else kshard, kv.at[m]) for m in range(n_f)]
    v_cp = [fetch(n_f, vshard, vv.at[0])]
    uh = U // 2
    for p in range(L.parts):
        m = 1 << L.order(p)[0]
        for c in range(2):
            r = pl.ds(c * uh + p * (uh // L.parts), uh // L.parts)
            v_cp.append(fetch(n_f + 1 + 2 * p + c, vall.at[m, r], vv.at[m, r]))
    pairs = ((ck, ck_s), (x1, x1_s), (gate, gate_s), (og, og_s), (cr, cr_s), (wc, wcv))
    ins = [pltpu.make_async_copy(s, d, in_sem.at[n]) for n, (s, d) in enumerate(pairs)]
    for cp in [ins[0]] + k_cp + v_cp + ins[1:]:
        cp.start()

    greet([(buddy, me)] + [(dp, flip(me, b)) for b in range(L.bits)])

    first = [1 << L.order(p)[0] for p in range(L.parts)]
    values = Gather(
        L, core, dp, me, uh,
        lambda m, r: vshard.at[r] if m == 0 else (vall.at[m, r] if m in first else vv.at[m, r]),
        lambda m, r: vv.at[m, r],
        (g_ssem, g_rsem, c_ssem, c_rsem),
    )
    if L.bits > 1:
        for cp in values.link(1):
            cp.start()
    for cp in [ins[0]] + k_cp:
        cp.wait()

    def keys_block(i, carry):
        r = rows_of(i, BR)
        ck_i = ck_s[r, :]
        for m in range(n_f):
            p = jnp.maximum(dot(ck_i, kv[m]), 0.0)
            p_s[m, r, :] = p.astype(BF16)
            h_s[m, r, :] = (p * p).astype(BF16)
        ckt_s[:, pl.ds(pl.multiple_of(i * BR, 128), BR)] = ck_i.T
        return carry

    lax.fori_loop(0, L.nblk, keys_block, 0)
    for cp in v_cp + ins[1:]:
        cp.wait()
    for t in range(1, L.bits):
        for cp in values.link(t):
            cp.wait_recv()
        for cp in values.across(t):
            cp.start()
        if t + 1 < L.bits:
            for cp in values.link(t + 1):
                cp.start()
    for t in range(1, L.bits):
        for cp in values.across(t):
            cp.wait_recv()

    def ship(i):
        r = rows_of(i, BR)
        both = ((mix_s, mixed_o), (og_s, g2_o), (x1_s, gck_o), (gate_s, gcr_o))
        return [pltpu.make_async_copy(s.at[r], d.at[r], out_sem.at[n, i]) for n, (s, d) in enumerate(both)]

    def values_block(i, carry):
        r = rows_of(i, BR)
        vsum = jnp.zeros((BR, D), F32)
        for m in range(n_f):
            vsum = vsum + dot(h_s[m, r, :], vv[m])
        pos = start + i * BR + lax.broadcasted_iota(jnp.int32, (BR, 1), 0)
        live = jnp.where(pos < length, 1.0, 0.0).astype(F32)
        gate_i = gate_s[r, :]
        mix_s[r, :] = ((x1_s[r, :] + gate_i * vsum) * live).astype(BF16)
        g2 = og_s[r, :].astype(F32) * live
        og_s[r, :] = g2.astype(BF16)
        gv32 = g2 * gate_i
        gv = gv32.astype(BF16)
        gv_s[r, :] = gv
        gg_s[r, :] = (gv32 * vsum * (1.0 - gate_i)).astype(BF16)
        gvt_s[:, pl.ds(pl.multiple_of(i * BR, 128), BR)] = gv.T
        for cp in ship(i)[:2]:
            cp.start()
        return carry

    lax.fori_loop(0, L.nblk, values_block, 0)

    own = pl.ds(pl.multiple_of(core * half, 16), half)
    away = pl.ds(pl.multiple_of((1 - core) * half, 16), half)

    def swaps(m):
        return [
            remote(g.at[m, away], inc.at[n, m], x_ssem.at[n, m], x_rsem.at[n, m], (buddy, me))
            for n, g in enumerate((dk_s, dv_s))
        ]

    def part_rows(p):
        return pl.ds(pl.multiple_of(core * half + p * hk, 16), hk)

    def halves(m):
        out = []
        for p in range(L.parts):
            bit = L.order(p)[0]
            if (m >> bit) & 1:
                k = squeeze(m, bit)
                for n, g in enumerate((dk_s, dv_s)):
                    out.append(
                        remote(g.at[m, part_rows(p)], r0.at[n, p, k], h_ssem.at[n, p, k], h_rsem.at[n, p, k],
                               (dp, flip(me, bit)))
                    )
        return out

    def merge(m):
        for cp in swaps(m):
            cp.wait_recv()
        for n, g in enumerate((dk_s, dv_s)):
            g[m, own, :] = (g[m, own, :].astype(F32) + inc[n, m].astype(F32)).astype(BF16)
        for cp in halves(m):
            cp.start()

    for n, m in enumerate(masks):
        def block(i, carry, m=m, n=n):
            r = rows_of(i, BR)
            gk = (dot(gv_s[r, :], vv[m], 1, 1) * (2.0 * p_s[m, r, :].astype(F32))).astype(BF16)
            p_s[m, r, :] = gk
            part = dot(gk, kv[m], 1, 1)
            x1_s[r, :] = part if n == 0 else x1_s[r, :] + part
            return carry

        lax.fori_loop(0, L.nblk, block, 0)
        for c in range(D // BR):
            rr = slice(c * BR, (c + 1) * BR)
            dk_s[m, rr, :] = dot(ckt_s[rr, :], p_s[m]).astype(BF16)
            dv_s[m, rr, :] = dot(gvt_s[rr, :], h_s[m]).astype(BF16)
        for cp in swaps(m):
            cp.start()
        if n > 0:
            merge(masks[n - 1])

    def last_block(i, carry):
        r = rows_of(i, BR)
        gate_s[r, :] = dot(gg_s[r, :], wcv[...], 1, 1)
        for cp in ship(i)[2:]:
            cp.start()
        return carry

    lax.fori_loop(0, L.nblk, last_block, 0)
    merge(masks[-1])
    for c in range(D // BR):
        rr = slice(c * BR, (c + 1) * BR)
        dc_s[rr, :] = dot(cr_s[:, rr], gg_s[...], 0, 0).astype(BF16)
    last = pltpu.make_async_copy(dc_s, dc_o, in_sem.at[0])
    last.start()

    outs = []
    for m in masks:
        for cp in halves(m):
            cp.wait_recv()
    for p in range(L.parts):
        bit = L.order(p)[0]
        for m in range(n_f):
            if (m >> bit) & 1:
                continue
            k = squeeze(m, bit)
            for n, g in enumerate((dk_s, dv_s)):
                r = part_rows(p)
                r0[n, p, k] = (g[m, r, :].astype(F32) + r0[n, p, k].astype(F32)).astype(BF16)
                outs.append(pltpu.make_async_copy(r0.at[n, p, k], big_o.at[n, p, k], g_sem.at[n, p, k]))
                outs[-1].start()
    for m in masks:
        for cp in halves(m) + swaps(m):
            cp.wait_send()
    for t in range(1, L.bits):
        for cp in values.link(t) + values.across(t):
            cp.wait_send()
    for i in range(L.nblk):
        for cp in ship(i):
            cp.wait()
    for cp in outs + [last]:
        cp.wait()


def middle(L, lens, ck, cr, x1, gate, og, kall, vall, kshard, vshard, wc):
    R, D, n_f, U = L.R, L.D, L.n_f, L.U
    dma = pltpu.SemaphoreType.DMA
    rb, rf = sds((R, D), BF16), sds((R, D))
    vb, vf = pltpu.VMEM((R, D), BF16), pltpu.VMEM((R, D), F32)
    hid = pltpu.VMEM((n_f, R, U), BF16)
    kept = (2, L.parts, n_f // 2, D // 2 // L.parts, U)
    _, flat = gather_steps(L)
    sem3 = dma(kept[:3])
    return pl.pallas_call(
        functools.partial(middle_kernel, L),
        out_shape=(rb, rb, rf, rf, sds(kept, BF16), sds((D, D), BF16)),
        in_specs=[SMEM] + [ANY] * 10,
        out_specs=(ANY,) * 6,
        scratch_shapes=[
            pltpu.VMEM((n_f, D, U), BF16), pltpu.VMEM((n_f, U, D), BF16), pltpu.VMEM((D, D), BF16),
            vb, vb, vf, vf, vb, vb, vb, vb, pltpu.VMEM((D, R), BF16), pltpu.VMEM((D, R), BF16), hid, hid,
            pltpu.VMEM((n_f, D, U), BF16), pltpu.VMEM((n_f, D, U), BF16), pltpu.VMEM((D, D), BF16),
            pltpu.VMEM((2, n_f, D // 2, U), BF16), pltpu.VMEM(kept, BF16),
            dma((6,)), dma((n_f + 1 + 2 * L.parts,)), dma((4, L.nblk)), sem3, dma((2, n_f)), dma((2, n_f)),
            sem3, sem3, dma((flat,)), dma((flat,)), dma((flat,)), dma((flat,)),
        ],
        compiler_params=pltpu.CompilerParams(collective_id=1, has_side_effects=True, vmem_limit_bytes=VLIMIT),
        cost_estimate=pl.CostEstimate(flops=52 * R * D * D, bytes_accessed=60 * R * D, transcendentals=0),
        name="middle",
    )(lens, ck, cr, x1, gate, og, kall, vall, kshard, vshard, wc)


class Pool:
    def __init__(self, ssem, rsem):
        self.ssem, self.rsem, self.n = ssem, rsem, 0

    def copy(self, src, dst, dev):
        k = self.n
        self.n = k + 1
        return remote(src, dst, self.ssem.at[k], self.rsem.at[k], dev)


def begin(copies):
    for cp in copies:
        cp.start()
    return copies


def landed(copies):
    for cp in copies:
        cp.wait_recv()


class Unit:
    def __init__(self, env, order, rows, done, acc, rbuf, zbuf, final, source=None, swap=None, gather=False):
        self.env, self.rows, self.acc, self.rbuf, self.zbuf, self.final = env, rows, acc, rbuf, zbuf, final
        self.source = source
        self.order = order
        self.sent, self.pending, self.now = [], None, []
        self.off, self.size, self.zoff, self.split, self.slot = 0, rows, 0, [], 0
        steps = [swap] if swap else []
        steps += [functools.partial(self.halve, t) for t in range(done, len(order))]
        steps += [functools.partial(self.halve_z, b) for b in range(env.zbits)]
        steps += [self.home]
        if gather:
            steps += [functools.partial(self.double, t) for t in range(len(order))]
        steps += [self.cross]
        self.steps = steps

    def keep(self, copies):
        self.sent += copies
        self.now = begin(copies)

    def advance(self):
        landed(self.now)
        self.now = []
        if self.pending:
            self.pending()
            self.pending = None
        if not self.steps:
            return False
        self.steps.pop(0)()
        return True

    def halve(self, t):
        e, bit = self.env, self.order[t]
        masks = spans(self.order[t + 1 :])
        base, src = self.slot, self.source or self.acc
        self.slot += len(masks)
        self.source = None
        self.keep([
            e.pool.copy(src(m | (1 << bit)), self.rbuf(base + n), (e.dp, flip(e.me, bit))) for n, m in enumerate(masks)
        ])

        def end():
            for n, m in enumerate(masks):
                view = self.acc(m)
                view[...] = (view[...].astype(F32) + self.rbuf(base + n)[...].astype(F32)).astype(BF16)

        self.pending = end

    def part(self, off, size):
        return pl.ds(pl.multiple_of(off, 16), size)

    def halve_z(self, b):
        e, mine = self.env, (self.env.zi // (1 << b)) % 2
        split = (self.size // 2) % 16 == 0
        size = self.size // 2 if split else self.size
        kept = self.off + (mine * size if split else 0)
        sent = self.off + ((1 - mine) * size if split else 0)
        buf = self.zbuf(pl.ds(self.zoff, size))
        self.zoff += size
        peer = (flip(e.zi, b) * 2 + e.core, e.me)
        self.keep([e.pool.copy(self.acc(0).at[self.part(sent, size)], buf, peer)])
        if split:
            self.split.append((b, self.off, self.size))
        self.off, self.size = kept, size

        def end():
            if not split:
                self.sent.pop().wait_send()
            view = self.acc(0).at[self.part(kept, size)]
            view[...] = (view[...].astype(F32) + buf[...].astype(F32)).astype(BF16)

        self.pending = end

    def home(self):
        e = self.env
        here = self.acc(0).at[self.part(self.off, self.size)]
        self.local = pltpu.make_async_copy(here, self.final(0, self.off, self.size), e.lsem.at[e.nl])
        e.nl += 1
        self.local.start()
        self.steps = [functools.partial(self.double_z, n) for n in reversed(range(len(self.split)))] + self.steps
        self.first = here
        if self.split:
            self.steps.pop(0)()
        else:
            self.pending = self.local.wait

    def double_z(self, n):
        e = self.env
        b, off, size = self.split[n]
        src = self.final(0, self.off, self.size) if self.first is None else self.first
        self.keep([e.pool.copy(src, self.final(0, self.off, self.size), (flip(e.zi, b) * 2 + e.core, e.me))])
        if self.first is not None:
            self.first = None
            self.pending = self.local.wait
        self.off, self.size = off, size

    def double(self, t):
        e, o = self.env, self.order
        out = []
        for m in spans(o[:t]):
            v = self.final(m, 0, self.rows)
            out.append(e.pool.copy(v, v, (e.dp, flip(e.me, o[t]))))
        self.keep(out)

    def cross(self):
        e = self.env
        v = self.final(None, 0, self.rows)
        self.keep([e.pool.copy(v, v, (e.dp + 1 - 2 * e.core, e.me))])


class Env:
    pass


KEY, VALUE, RECEPT, OUT, CMR = range(5)
V_LN1G, V_LN1B, V_TD, V_TF, V_MK, V_MV, V_MR, V_LN2G, V_LN2B, V_CMK, V_CMR = range(11)


def back_kernel(
    L, tok, par, edge, g2, gck, gcr, x1, y, sr, wkv, rd, a, v, xk, xv, xr, wk, wv, wr, wo, bigh, dch,
    ig_o, dkr, dvr, rep, vec_o,
    gck_s, gcr_s, x1_s, sr_s, wkv_s, rd_s, v_s, g2_s, y_s, xr_s, gr_s, gk_s, gv_s, w3, dw, acc1,
    inc, r1, r2, z1, z2, grow, fade, tri, ent, st_out, st_in, carry, gpad, tpad, vacc, vown, vf, vd, dev_in,
    blk_sem, in_sem, out_sem, e_ssem, e_rsem, s_ssem, s_rsem, v_ssem, v_rsem, lsem, p_ssem, p_rsem,
):
    D, BR, n_f, n_dp, U, R = L.D, L.BR, L.n_f, L.n_dp, L.U, L.R
    dp, me = lax.axis_index("dp"), lax.axis_index("ffn")
    core = dp % 2
    buddy = dp + 1 - 2 * core
    place = me % L.per_slot
    opens = jnp.where(place == 0, 0.0, 1.0).astype(F32)
    stays = jnp.where(place == L.per_slot - 1, 0.0, 1.0).astype(F32)
    half = D // 2

    blocks = ((gck, gck_s), (gcr, gcr_s), (x1, x1_s), (g2, g2_s), (sr, sr_s), (wkv, wkv_s), (rd, rd_s))

    def load(i, which):
        r = rows_of(i, BR)
        return [pltpu.make_async_copy(blocks[n][0].at[r], blocks[n][1].at[r], blk_sem.at[n, i]) for n in which]

    wo_cp = pltpu.make_async_copy(wo, w3.at[2], in_sem.at[0])
    begin(load(0, range(7)) + [wo_cp])
    for i in range(1, L.nblk):
        begin(load(i, range(7)))
    acc_cp = pltpu.make_async_copy(bigh, acc1, in_sem.at[1])
    y_cp = pltpu.make_async_copy(y, y_s, in_sem.at[3])
    xr_cp = pltpu.make_async_copy(xr, xr_s, in_sem.at[4])
    v_cp = pltpu.make_async_copy(v, v_s, in_sem.at[5])
    dc_cps = [
        pltpu.make_async_copy(dch.at[:, pl.ds(h * half, half)], dw.at[CMR, h], in_sem.at[6 + h]) for h in range(2)
    ]
    w_cps = [pltpu.make_async_copy(w, w3.at[n], in_sem.at[8 + n]) for n, w in enumerate((wk, wv))]
    begin([acc_cp] + dc_cps + [y_cp, xr_cp, v_cp] + w_cps)

    greet(
        [(dp, (me + k) % n_f) for k in range(1, n_f)] + [((dp + k) % n_dp, me) for k in range(1, n_dp)]
    )

    prv = (me + n_f - 1) % n_f
    edges = begin([
        remote(g.at[pl.ds(0, 8)], gpad.at[n], e_ssem.at[n], e_rsem.at[n], (dp, prv)) for n, g in enumerate((gck, gcr))
    ])

    e = Env()
    e.me, e.dp, e.core, e.zi, e.zbits = me, dp, core, dp // 2, L.nz.bit_length() - 1
    e.pool, e.lsem, e.nl = Pool(p_ssem, p_rsem), lsem, 0

    hk = half // L.parts
    big = []
    for n, res in enumerate((dkr, dvr)):
        for p in range(L.parts):
            o, off = L.order(p), p * hk

            def acc(m, n=n, p=p, o=o):
                return acc1.at[n, p, squeeze(m, o[0])]

            def source(m, n=n, p=p, o=o):
                return bigh.at[n, p, squeeze(m, o[0])]

            def rbuf(k, n=n, p=p):
                return r1.at[n, p, k]

            def zbuf(r, n=n, p=p):
                return z1.at[n, p, r]

            def final(m, r0, size, res=res, off=off):
                return res.at[pl.ds(pl.multiple_of(core * half + off + r0, 16), size)]

            big.append(Unit(e, o, hk, 1, acc, rbuf, zbuf, final, source))
    shard = D // n_f
    small = []
    for m_ in range(5):
        def acc(m, i=m_):
            return dw.at[i, core, pl.ds(pl.multiple_of(flips(me, m) * shard, 16), shard)]

        def rbuf(k, i=m_):
            return r2.at[i, k]

        def zbuf(r, i=m_):
            return z2.at[i, r]

        def final(m, r0, size, i=m_):
            cols = pl.ds(pl.multiple_of(core * half, 128), half)
            if m is None:
                return rep.at[i, :, cols]
            return rep.at[i, pl.ds(pl.multiple_of(flips(me, m) * shard + r0, 16), size), cols]

        def swap(i=m_):
            u = small[i]
            u.keep([e.pool.copy(dw.at[i, 1 - core], inc.at[i % 4], (buddy, me))])

            def end():
                dw[i, core] = (dw[i, core].astype(F32) + inc[i % 4].astype(F32)).astype(BF16)

            u.pending = end

        o = L.order(0) if m_ in (CMR, KEY) else L.order(1)
        small.append(Unit(e, o, shard, 0, acc, rbuf, zbuf, final, None, swap, True))
    KS, VS = big[: L.parts], big[L.parts :]

    def go(*units):
        for u in units:
            u.advance()

    go(*KS, *VS)

    w = jnp.exp(par[TD : TD + 1, :])
    ew = jnp.exp(w)
    eu = jnp.exp(par[TF : TF + 1, :])
    age = lax.broadcasted_iota(jnp.int32, (SPAN, D), 0).astype(F32) * w
    grow[...] = jnp.exp(age)
    fade[...] = jnp.exp(-age)
    tri[...] = tri_pair(False)
    full_fade = jnp.exp(-float(SPAN) * w)
    tail_fade = jnp.exp(-float(SPAN - 1) * w)
    vacc[...] = jnp.zeros_like(vacc)
    carry[...] = edge[8:16, :]

    def add_up(n, x):
        vacc[n] = vacc[n] + jnp.sum(x.reshape(-1, 8, D), axis=0)

    for cp in dc_cps:
        cp.wait()
    go(small[CMR])
    acc_cp.wait()
    wo_cp.wait()
    for cp in load(0, (0, 1)):
        cp.wait()

    def phase_1(i, _):
        @pl.when(i + 1 < L.nblk)
        def _wait():
            for cp in load(i + 1, (0, 1)):
                cp.wait()

        for cp in load(i, range(2, 7)):
            cp.wait()
        r = rows_of(i, BR)
        win = pl.ds(pl.multiple_of(i * BR, 8), BR + 8)
        mk, mr = par[CK : CK + 1, :], par[CR : CR + 1, :]
        gk = gck_s[win, :]
        gr = gcr_s[win, :]
        t = gk * (1.0 - mk) + gr * (1.0 - mr)
        t = pltpu.roll(t, BR + 7, 0)[:BR]
        gk, gr = gk[:BR], gr[:BR]
        gn = gk * mk + gr * mr + t
        n2, rs = normed(x1_s[r, :])
        norm2 = n2 * par[G2 : G2 + 1, :] + par[B2 : B2 + 1, :]
        prev = pltpu.roll(jnp.concatenate([carry[...], norm2], axis=0), 1, 0)[8:]
        carry[...] = norm2[BR - 8 :]
        d = norm2 - prev
        add_up(V_CMK, gk * d)
        add_up(V_CMR, gr * d)
        add_up(V_LN2G, gn * n2)
        add_up(V_LN2B, gn)
        q1 = gn * par[G2 : G2 + 1, :]
        m1 = jnp.mean(q1, axis=-1, keepdims=True)
        m2 = jnp.mean(q1 * n2, axis=-1, keepdims=True)
        g1 = g2_s[r, :].astype(F32) + (q1 - m1 - n2 * m2) * rs
        x1_s[r, :] = g1
        ga = g1.astype(BF16)
        g2_s[r, :] = ga
        s = sr_s[r, :]
        gys = dot(ga, w3[2], 1, 1) * s
        wk_ = wkv_s[r, :]
        gr_s[r, :] = (gys * wk_ * (1.0 - s)).astype(BF16)
        q = gys * rd_s[r, :]
        qw = q * wk_
        rd_s[r, :] = q
        wkv_s[r, :] = qw
        for sb in range(BR // SPAN):
            b = i * (BR // SPAN) + sb
            rb = rows_of(b, SPAN)
            sl = slice(sb * SPAN, (sb + 1) * SPAN)
            fd = fade[...]
            both = jnp.concatenate([fd * q[sl], fd * qw[sl]], axis=1)
            suf = dot(tri[...], split2(both))
            gs = grow[...] * ew
            gck_s[rb, :] = gs * suf[:, :D]
            gcr_s[rb, :] = gs * suf[:, D:]
            tot = suf[0:1] + both[0:1]
            ent[b, 0:1, :] = tot[:, :D]
            ent[b, 1:2, :] = tot[:, D:]
        return 0

    cut = L.nblk // 2
    lax.fori_loop(0, cut, phase_1, 0)
    go(small[CMR], *KS)
    lax.fori_loop(cut, L.nblk - 1, phase_1, 0)
    go(*VS)
    for cp in edges:
        cp.wait()
    gck_s[R : R + 8, :] = gpad[0] * stays
    gcr_s[R : R + 8, :] = gpad[1] * stays
    phase_1(L.nblk - 1, 0)

    xq = jnp.zeros((1, D), F32)
    xw = jnp.zeros((1, D), F32)
    for b in reversed(range(L.nspan)):
        tq, tw = ent[b, 0:1, :], ent[b, 1:2, :]
        ent[b, 0:1, :] = xq
        ent[b, 1:2, :] = xw
        xq = tq + full_fade * xq
        xw = tw + full_fade * xw
    st_out[...] = jnp.zeros_like(st_out)
    st_out[0:1, :] = xq
    st_out[1:2, :] = xw
    states = begin([
        remote(st_out, st_in.at[k], s_ssem.at[k], s_rsem.at[k], (dp, (me + n_f - k) % n_f)) for k in range(1, n_f)
    ])
    a_cp = pltpu.make_async_copy(a, sr_s, in_sem.at[11])
    a_cp.start()
    w_cps.append(pltpu.make_async_copy(wr, w3.at[2], in_sem.at[10]))
    w_cps[-1].start()

    def product(m, left, right):
        for c in range(D // BR):
            rr = slice(c * BR, (c + 1) * BR)
            full = dot(left[:, rr], right[...], 0, 0).astype(BF16)
            dw[m, 0, rr, :] = full[:, :half]
            dw[m, 1, rr, :] = full[:, half:]

    y_cp.wait()
    product(OUT, y_s, g2_s)
    go(small[OUT], *KS, small[CMR])
    xk_cp = pltpu.make_async_copy(xk, y_s, in_sem.at[12])
    xv_cp = pltpu.make_async_copy(xv, g2_s, in_sem.at[14])
    begin([xk_cp, xv_cp])

    for cp in states:
        cp.wait()
    qi = jnp.zeros((1, D), F32)
    wi = jnp.zeros((1, D), F32)
    for k in range(1, L.per_slot):
        f = jnp.exp(-float((k - 1) * R) * w) * jnp.where(place + k < L.per_slot, 1.0, 0.0).astype(F32)
        qi = qi + f * st_in[k, 0:1, :]
        wi = wi + f * st_in[k, 1:2, :]
    dev_in[0:1, :] = qi
    dev_in[1:2, :] = wi
    a_cp.wait()
    v_cp.wait()
    first = place * R - (L.per_slot * R) // 2

    def phase_2(b, _):
        rb = rows_of(b, SPAN)
        fb = jnp.exp(w * ((b + 1 - L.nspan) * SPAN).astype(F32))
        eq = ent[b, 0:1, :] + fb * dev_in[0:1, :]
        ewk = ent[b, 1:2, :] + fb * dev_in[1:2, :]
        ff = grow[...] * tail_fade
        q, qw, av, vv = rd_s[rb, :], wkv_s[rb, :], sr_s[rb, :], v_s[rb, :]
        gvr = av * (eu * q + gck_s[rb, :] + ff * eq)
        gkr = vv * gvr - av * (eu * qw + gcr_s[rb, :] + ff * ewk)
        gk_s[rb, :] = gkr.astype(BF16)
        gv_s[rb, :] = gvr.astype(BF16)
        add_up(V_TF, eu * av * (q * vv - qw))
        pos = (first + b * SPAN + lax.broadcasted_iota(jnp.int32, (SPAN, 1), 0)).astype(F32)
        add_up(V_TD, pos * gkr)
        return 0

    lax.fori_loop(0, L.nspan, phase_2, 0)
    go(*VS)
    xk_cp.wait()
    product(KEY, y_s, gk_s)
    tok_cp = pltpu.make_async_copy(tok, y_s, in_sem.at[13])
    tok_cp.start()
    go(small[OUT], small[KEY], *KS)
    xr_cp.wait()
    product(RECEPT, xr_s, gr_s)
    go(small[RECEPT])
    xv_cp.wait()
    product(VALUE, g2_s, gv_s)
    go(small[VALUE], small[KEY], small[RECEPT], small[CMR], *VS)

    for cp in w_cps:
        cp.wait()
    tok_cp.wait()
    carry[...] = edge[0:8, :]

    def phase_3(i, _):
        r = rows_of(i, BR)
        mk, mv, mr = par[MK : MK + 1, :], par[MV : MV + 1, :], par[MR : MR + 1, :]
        n1_, _rs = normed(y_s[r, :].astype(F32))
        norm1 = n1_ * par[G1 : G1 + 1, :] + par[B1 : B1 + 1, :]
        prev = pltpu.roll(jnp.concatenate([carry[...], norm1], axis=0), 1, 0)[8:]
        carry[...] = norm1[BR - 8 :]
        d = norm1 - prev
        gxk = dot(gk_s[r, :], w3[0], 1, 1)
        gxv = dot(gv_s[r, :], w3[1], 1, 1)
        gxr = dot(gr_s[r, :], w3[2], 1, 1)
        add_up(V_MK, gxk * d)
        add_up(V_MV, gxv * d)
        add_up(V_MR, gxr * d)
        now = gxk * mk + gxv * mv + gxr * mr
        gck_s[r, :] = gxk + gxv + gxr - now
        gcr_s[r, :] = now
        return 0

    lax.fori_loop(0, cut, phase_3, 0)
    t_cp = remote(gck_s.at[pl.ds(0, 8)], tpad, e_ssem.at[2], e_rsem.at[2], (dp, prv))
    t_cp.start()
    go(small[VALUE], *KS, small[OUT], small[CMR])
    lax.fori_loop(cut, L.nblk - 1, phase_3, 0)
    go(small[KEY], small[RECEPT], *VS)
    lax.fori_loop(L.nblk - 1, L.nblk, phase_3, 0)
    go(small[VALUE], small[OUT], small[CMR], *KS)
    t_cp.wait()
    gck_s[R : R + 8, :] = tpad[...] * stays

    def phase_4(i, _):
        r = rows_of(i, BR)
        t = gck_s[pl.ds(pl.multiple_of(i * BR, 8), BR + 8), :]
        gn = gcr_s[r, :] + pltpu.roll(t, BR + 7, 0)[:BR]
        n1_, rs = normed(y_s[r, :].astype(F32))
        add_up(V_LN1G, gn * n1_)
        add_up(V_LN1B, gn)
        q1 = gn * par[G1 : G1 + 1, :]
        m1 = jnp.mean(q1, axis=-1, keepdims=True)
        m2 = jnp.mean(q1 * n1_, axis=-1, keepdims=True)
        y_s[r, :] = (x1_s[r, :] + (q1 - m1 - n1_ * m2) * rs).astype(BF16)
        pltpu.make_async_copy(y_s.at[r], ig_o.at[r], out_sem.at[i]).start()
        return 0

    lax.fori_loop(0, cut, phase_4, 0)
    go(small[KEY], small[RECEPT], small[VALUE], *VS)
    lax.fori_loop(cut, L.nblk, phase_4, 0)
    vown[...] = jnp.sum(vacc[...], axis=1)
    vf[0] = vown[...]
    vs = begin([
        remote(vown, vf.at[k], v_ssem.at[0, k], v_rsem.at[0, k], (dp, (me + k) % n_f)) for k in range(1, n_f)
    ])
    go(small[KEY], small[VALUE], small[OUT], small[RECEPT], small[CMR], *KS)
    for cp in vs:
        cp.wait()
    total = vf[(me + n_f) % n_f]
    for f in range(1, n_f):
        total = total + vf[(me - f + n_f) % n_f]
    vd[0] = total
    vs = begin([
        remote(vd.at[0], vd.at[k], v_ssem.at[1, k], v_rsem.at[1, k], ((dp + k) % n_dp, me)) for k in range(1, n_dp)
    ])
    go(small[KEY], small[VALUE], small[OUT], small[RECEPT], small[CMR], *VS)
    for cp in vs:
        cp.wait()
    total = vd[dp % n_dp]
    for f in range(1, n_dp):
        total = total + vd[(dp - f + n_dp) % n_dp]
    vec_o[...] = total
    vec_o[V_TD : V_TD + 1, :] = w * (total[V_TD : V_TD + 1] - total[V_TF : V_TF + 1])

    live = [small[CMR], small[OUT], *KS, small[KEY], small[VALUE], small[RECEPT], *VS]
    while live:
        live = [u for u in live if u.advance()]
    for u in big + small:
        for cp in u.sent:
            cp.wait_send()
    for i in range(L.nblk):
        pltpu.make_async_copy(y_s.at[rows_of(i, BR)], ig_o.at[rows_of(i, BR)], out_sem.at[i]).wait()


def back(L, *args):
    R, D, n_f, n_dp, U = L.R, L.D, L.n_f, L.n_dp, L.U
    half, shard = D // 2, D // L.n_f
    hk = half // L.parts
    dma = pltpu.SemaphoreType.DMA
    fpad, full, low = pltpu.VMEM((R + 8, D), F32), pltpu.VMEM((R, D), F32), pltpu.VMEM((R, D), BF16)
    rows8 = pltpu.VMEM((8, D), F32)
    zbits = L.nz.bit_length() - 1

    def z_rows(rows):
        total = 0
        for _ in range(zbits):
            rows = rows // 2 if (rows // 2) % 16 == 0 else rows
            total += rows
        return total

    n_r = n_f - 1
    n_pool = 2 * L.parts * (n_r + 2 * zbits + 1) + 5 * (2 * n_r + 2 * zbits + 2)
    return pl.pallas_call(
        functools.partial(back_kernel, L),
        out_shape=(
            sds((R, D), BF16), sds((D, U), BF16), sds((D, U), BF16), sds((5, D, D), BF16), sds((16, D)),
        ),
        in_specs=[ANY, VMEM, VMEM] + [ANY] * 19,
        out_specs=(ANY, ANY, ANY, ANY, VMEM),
        scratch_shapes=[
            fpad, fpad, full, full, full, full, full, low, low, low, low, low, low,
            pltpu.VMEM((3, D, D), BF16), pltpu.VMEM((5, 2, D, half), BF16), pltpu.VMEM((2, L.parts, n_f // 2, hk, U), BF16),
            pltpu.VMEM((4, D, half), BF16), pltpu.VMEM((2, L.parts, max(n_f // 2 - 1, 1), hk, U), BF16),
            pltpu.VMEM((5, n_r, shard, half), BF16), pltpu.VMEM((2, L.parts, z_rows(hk), U), BF16),
            pltpu.VMEM((5, z_rows(shard), half), BF16),
            pltpu.VMEM((SPAN, D), F32), pltpu.VMEM((SPAN, D), F32), pltpu.VMEM((SPAN, 2 * SPAN), BF16),
            pltpu.VMEM((L.nspan, 8, D), F32), rows8, pltpu.VMEM((n_f, 8, D), F32), rows8,
            pltpu.VMEM((2, 8, D), F32), rows8, pltpu.VMEM((16, 8, D), F32), pltpu.VMEM((16, D), F32),
            pltpu.VMEM((n_f, 16, D), F32), pltpu.VMEM((n_dp, 16, D), F32), rows8,
            dma((7, L.nblk)), dma((15,)), dma((L.nblk,)), dma((3,)), dma((3,)), dma((n_f,)), dma((n_f,)),
            dma((2, n_dp)), dma((2, n_dp)), dma((16,)), dma((n_pool,)), dma((n_pool,)),
        ],
        compiler_params=pltpu.CompilerParams(collective_id=2, has_side_effects=True, vmem_limit_bytes=VLIMIT),
        cost_estimate=pl.CostEstimate(flops=20 * R * D * D, bytes_accessed=60 * R * D, transcendentals=0),
        name="back",
    )(*args)


def finish_kernel(n, rep, dkr, dvr, vec, *outs):
    mats, vecs = outs[:7], outs[7:]
    for m in range(5):
        mats[m][...] = rep[m].astype(F32)
    mats[5][...] = dkr[...].astype(F32)
    mats[6][...] = dvr[...].astype(F32).T

    @pl.when(pl.program_id(0) == 0)
    def _():
        for k in range(NVEC):
            vecs[k][...] = vec[k, :]


def finish(L, rep, dkr, dvr, vec):
    D, U, n = L.D, L.U, 3
    rows, cols = D // n, U // n
    mat = pl.BlockSpec((rows, D), lambda i: (i, 0))
    return pl.pallas_call(
        functools.partial(finish_kernel, n),
        grid=(n,),
        out_shape=(sds((D, D)),) * 5 + (sds((D, U)), sds((U, D))) + (sds((D,)),) * NVEC,
        in_specs=[
            pl.BlockSpec((5, rows, D), lambda i: (0, i, 0)), pl.BlockSpec((rows, U), lambda i: (i, 0)),
            pl.BlockSpec((D, cols), lambda i: (0, i)), pl.BlockSpec((16, D), lambda i: (0, 0)),
        ],
        out_specs=(mat,) * 5 + (pl.BlockSpec((rows, U), lambda i: (i, 0)), pl.BlockSpec((cols, D), lambda i: (i, 0)))
        + (pl.BlockSpec((D,), lambda i: (0,)),) * NVEC,
        compiler_params=pltpu.CompilerParams(vmem_limit_bytes=VLIMIT),
        cost_estimate=pl.CostEstimate(flops=0, bytes_accessed=42 * D * D, transcendentals=0),
        name="finish",
    )(rep, dkr, dvr, vec)


def solution(mesh):
    def step(
        tokens, lens, og, ln1g, ln1b, td, tf, mk, mv, mr, wk, wv, wr, wo, ln2g, ln2b, cmk, cmr, ckw, cvw, wc
    ):
        L = Layout(mesh, tokens.shape[0], tokens.shape[1], ckw.shape[1])
        vecs = [ln1g, ln1b, td, tf, mk, mv, mr, ln2g, ln2b, cmk, cmr]
        xk, xv, xr, y, ck, cr, a, v, rd, wkv, sr, x1, gate, edge, par, kall, vall = front(
            L, tokens, vecs, wk, wv, wr, wo, wc, ckw, cvw
        )
        mixed, g2, gck, gcr, big, dc = middle(L, lens, ck, cr, x1, gate, og, kall, vall, ckw, cvw, wc)
        ig, dkr, dvr, rep, vec = back(
            L, tokens, par, edge, g2, gck, gcr, x1, y, sr, wkv, rd, a, v, xk, xv, xr, wk, wv, wr, wo, big, dc
        )
        done = finish(L, rep, dkr, dvr, vec)
        mats, vecs = done[:7], done[7:]
        return (mixed, ig, *vecs[:7], *mats[:4], *vecs[7:], mats[5], mats[6], mats[4])

    row, none = P(("dp", "ffn"), None), P()
    return jax.shard_map(
        step,
        mesh=mesh,
        in_specs=(row, P("dp"), row) + (none,) * 15 + (P(None, "ffn"), P("ffn", None), none),
        out_specs=(row, row) + (none,) * 15 + (P(None, "ffn"), P("ffn", None), none),
        check_vma=False,
    )
```

```python
import functools

import jax
import jax.numpy as jnp
from jax import lax
from jax.experimental import pallas as pl
from jax.experimental.pallas import tpu as pltpu
from jax.sharding import PartitionSpec as P

MAX_LEN = 4096
SPAN = 128
EPS = 1e-05
MESH = pl.DeviceIdType.MESH
F32 = jnp.float32
BF16 = jnp.bfloat16
ANY = pl.BlockSpec(memory_space=pl.ANY)
VMEM = pl.BlockSpec(memory_space=pltpu.VMEM)
SMEM = pl.BlockSpec(memory_space=pltpu.SMEM)
VLIMIT = 62 * 2**20
G1, B1, TD, TF, MK, MV, MR, G2, B2, CK, CR = range(11)
NVEC = 11


def dot(a, b, da=1, db=0):
    return lax.dot_general(a, b, (((da,), (db,)), ((), ())), preferred_element_type=F32)


def sds(shape, dtype=F32):
    return jax.ShapeDtypeStruct(shape, dtype)


def flip(i, bit):
    s = 1 << bit
    return i + s - 2 * s * ((i // s) % 2)


def rows_of(i, n):
    return pl.ds(pl.multiple_of(i * n, n), n)


def sigmoid(x):
    return 1.0 / (1.0 + jnp.exp(-x))


def normed(x):
    c = x - jnp.mean(x, axis=-1, keepdims=True)
    rs = lax.rsqrt(jnp.mean(c * c, axis=-1, keepdims=True) + EPS)
    return c * rs, rs


def split2(x):
    hi = x.astype(BF16)
    lo = (x - hi.astype(F32)).astype(BF16)
    return jnp.concatenate([hi, lo], axis=0)


def tri_pair(below):
    r = lax.broadcasted_iota(jnp.int32, (SPAN, 2 * SPAN), 0)
    c = lax.broadcasted_iota(jnp.int32, (SPAN, 2 * SPAN), 1) % SPAN
    keep = (r > c) if below else (r < c)
    return jnp.where(keep, 1.0, 0.0).astype(BF16)


def greet(peers):
    bar = pltpu.get_barrier_semaphore()
    for p in peers:
        pl.semaphore_signal(bar, inc=1, device_id=p, device_id_type=MESH)
    pl.semaphore_wait(bar, len(peers))


def remote(src, dst, ssem, rsem, dev):
    return pltpu.make_async_remote_copy(
        src_ref=src, dst_ref=dst, send_sem=ssem, recv_sem=rsem, device_id=dev, device_id_type=MESH
    )


class Layout:
    def __init__(self, mesh, rows, width, local_units):
        self.n_f = mesh.shape["ffn"]
        self.n_dp = mesh.shape["dp"]
        self.R = rows
        self.D = width
        self.U = local_units
        self.BR = 256
        self.nblk = rows // self.BR
        self.nspan = rows // SPAN
        slot_len = min(MAX_LEN, rows * self.n_f)
        self.per_slot = slot_len // rows
        self.bits = self.n_f.bit_length() - 1
        self.parts = 2 if self.bits == 2 else 1
        self.nz = self.n_dp // 2

    def order(self, part):
        b = list(range(self.bits))
        return b if part == 0 else b[::-1]


def flips(i, mask):
    b = 0
    while mask >> b:
        if (mask >> b) & 1:
            i = flip(i, b)
        b += 1
    return i


def spans(bits):
    out = [0]
    for b in bits:
        out = out + [m | (1 << b) for m in out]
    return out


def gather_steps(L):
    steps, flat = [], 0
    for t in range(L.bits):
        here = []
        for p in range(L.parts):
            o = L.order(p)
            for m in spans(o[:t]):
                here.append((p, o[t], m, flat))
                flat += 1
        steps.append(here)
    return steps, flat


class Gather:
    def __init__(self, L, core, dp, me, half, source, dest, sems):
        self.L, self.half, self.source, self.dest = L, half, source, dest
        self.core, self.dp, self.me = core, dp, me
        self.g_ssem, self.g_rsem, self.c_ssem, self.c_rsem = sems
        self.steps, _ = gather_steps(L)

    def rows(self, p):
        n = self.half // self.L.parts
        return pl.ds(pl.multiple_of(self.core * self.half + p * n, 16), n)

    def link(self, t):
        return [
            remote(self.source(m, self.rows(p)), self.dest(m | (1 << bit), self.rows(p)),
                   self.g_ssem.at[f], self.g_rsem.at[f], (self.dp, flip(self.me, bit)))
            for p, bit, m, f in self.steps[t]
        ]

    def across(self, t):
        buddy = self.dp + 1 - 2 * self.core
        out = []
        for p, bit, m, f in self.steps[t]:
            ref = self.dest(m | (1 << bit), self.rows(p))
            out.append(remote(ref, ref, self.c_ssem.at[f], self.c_rsem.at[f], (buddy, self.me)))
        return out


def front_kernel(
    L, tok, *refs
):
    vecs, refs = refs[:NVEC], refs[NVEC:]
    (
        wk, wv, wr, wo, kshard, vshard,
        xk_o, xv_o, xr_o, y_o, ck_o, cr_o, a_o, v_o, rd_o, wkv_o, sr_o, x1_o, edge_o, par, kall, vall,
        tokv, w4, npad, xk_s, xv_s, xr_s, y_s, ck_s, cr_s, a_s, v_s, S_s, D_s, sr_s, x1_s, srb_s,
        grow, fade, tri, ent, st_out, st_in, tedge, nedge, dev_in,
        in_sem, out_sem, e_ssem, e_rsem, s_ssem, s_rsem, g_ssem, g_rsem, c_ssem, c_rsem,
    ) = refs
    D, BR, n_f = L.D, L.BR, L.n_f
    dp, me = lax.axis_index("dp"), lax.axis_index("ffn")
    core = dp % 2
    buddy = dp + 1 - 2 * core
    place = me % L.per_slot
    keep = jnp.where(place == 0, 0.0, 1.0).astype(F32)
    ins = [pltpu.make_async_copy(tok, tokv, in_sem.at[0])]
    for n, w in enumerate((wk, wv, wr, wo)):
        ins.append(pltpu.make_async_copy(w, w4.at[n], in_sem.at[1 + n]))
    for cp in ins:
        cp.start()
    greet([(dp, (me + k) % n_f) for k in range(1, n_f)] + [(buddy, me)])

    nxt = (me + 1) % n_f
    tok_edge = remote(tok.at[pl.ds(L.R - 16, 16)], tedge, e_ssem.at[0], e_rsem.at[0], (dp, nxt))
    tok_edge.start()

    def gather(n, shard, full, half):
        return Gather(
            L, core, dp, me, half,
            lambda m, r: full.at[m, r] if m else shard.at[r],
            lambda m, r: full.at[m, r],
            (g_ssem.at[n], g_rsem.at[n], c_ssem.at[n], c_rsem.at[n]),
        )

    keys, values = gather(0, kshard, kall, D // 2), gather(1, vshard, vall, L.U // 2)
    for cp in keys.link(0) + values.link(0):
        cp.start()
    for n in range(NVEC):
        par[n : n + 1, :] = vecs[n][...].reshape(1, D)

    w = jnp.exp(par[TD : TD + 1, :])
    ew = jnp.exp(w)
    eu = jnp.exp(par[TF : TF + 1, :])
    age = lax.broadcasted_iota(jnp.int32, (SPAN, D), 0).astype(F32) * w
    grow[...] = jnp.exp(age)
    fade[...] = jnp.exp(-age)
    tri[...] = tri_pair(True)
    full_fade = jnp.exp(-float(SPAN) * w)
    tail_fade = jnp.exp(-float(SPAN - 1) * w)
    st_out[...] = jnp.zeros_like(st_out)

    ins[0].wait()
    tok_edge.wait()
    en, _ = normed(tedge[...].astype(F32))
    en = (en * par[G1 : G1 + 1, :] + par[B1 : B1 + 1, :])[8:16] * keep
    npad[0:8, :] = en
    edge_o[0:8, :] = en
    for cp in ins[1:4]:
        cp.wait()

    outs_a = ((xk_s, xk_o), (xv_s, xv_o), (xr_s, xr_o), (a_s, a_o), (v_s, v_o), (srb_s, sr_o))
    outs_c = ((y_s, y_o), (S_s, wkv_o), (D_s, rd_o), (x1_s, x1_o))
    outs_d = ((ck_s, ck_o), (cr_s, cr_o))

    def ship(outs, base, i):
        return [
            pltpu.make_async_copy(s.at[rows_of(i, BR)], o.at[rows_of(i, BR)], out_sem.at[base + n, i])
            for n, (s, o) in enumerate(outs)
        ]

    def phase_a(i, carry):
        r = rows_of(i, BR)
        n1, _ = normed(tokv[r, :].astype(F32))
        n1 = n1 * par[G1 : G1 + 1, :] + par[B1 : B1 + 1, :]
        npad[pl.ds(pl.multiple_of(i * BR + 8, 8), BR), :] = n1
        prev = pltpu.roll(npad[pl.ds(pl.multiple_of(i * BR, 8), BR + 8), :], 1, 0)[8:]
        d = n1 - prev
        xk = (prev + d * par[MK : MK + 1, :]).astype(BF16)
        xv = (prev + d * par[MV : MV + 1, :]).astype(BF16)
        xr = (prev + d * par[MR : MR + 1, :]).astype(BF16)
        xk_s[r, :] = xk
        xv_s[r, :] = xv
        xr_s[r, :] = xr
        a = jnp.exp(dot(xk, w4[0]))
        v = dot(xv, w4[1])
        a_s[r, :] = a
        v_s[r, :] = v
        for sb in range(BR // SPAN):
            b = i * (BR // SPAN) + sb
            aa = a[sb * SPAN : (sb + 1) * SPAN]
            vv = v[sb * SPAN : (sb + 1) * SPAN]
            ga = grow[...] * aa
            both = jnp.concatenate([ga * vv, ga], axis=1)
            pre = dot(tri[...], split2(both))
            fs = fade[...] * ew
            S_s[rows_of(b, SPAN), :] = fs * pre[:, :D]
            D_s[rows_of(b, SPAN), :] = fs * pre[:, D:]
            tot = pre[SPAN - 1 : SPAN] + both[SPAN - 1 : SPAN]
            num, den = st_out[0:1, :], st_out[1:2, :]
            ent[b, 0:1, :] = num
            ent[b, 1:2, :] = den
            st_out[0:1, :] = full_fade * num + tail_fade * tot[:, :D]
            st_out[1:2, :] = full_fade * den + tail_fade * tot[:, D:]
        sr = sigmoid(dot(xr, w4[2]))
        sr_s[r, :] = sr
        srb_s[r, :] = sr.astype(BF16)
        for cp in ship(outs_a, 0, i):
            cp.start()
        return carry

    lax.fori_loop(0, L.nblk, phase_a, 0)

    states = [
        remote(st_out, st_in.at[k], s_ssem.at[k], s_rsem.at[k], (dp, (me + k) % n_f)) for k in range(1, n_f)
    ]
    for cp in states:
        cp.start()

    for t in range(L.bits - 1):
        for cp in keys.link(t):
            cp.wait_recv()
        for cp in keys.link(t + 1):
            cp.start()
    for cp in values.link(0):
        cp.wait_recv()
    for t in range(L.bits - 1):
        for cp in keys.across(t):
            cp.start()
    for cp in values.across(0):
        cp.start()

    for cp in states:
        cp.wait()
    num_in = jnp.zeros((1, D), F32)
    den_in = jnp.zeros((1, D), F32)
    for k in range(1, L.per_slot):
        ok = jnp.where(place >= k, 1.0, 0.0).astype(F32)
        f = jnp.exp(-float((k - 1) * L.R) * w) * ok
        num_in = num_in + f * st_in[k, 0:1, :]
        den_in = den_in + f * st_in[k, 1:2, :]
    dev_in[0:1, :] = num_in
    dev_in[1:2, :] = den_in
    for cp in ins[4:]:
        cp.wait()

    def phase_c(i, carry):
        r = rows_of(i, BR)
        for sb in range(BR // SPAN):
            b = i * (BR // SPAN) + sb
            rb = rows_of(b, SPAN)
            fb = jnp.exp(w * (b * (-SPAN)).astype(F32))
            en = ent[b, 0:1, :] + fb * dev_in[0:1, :]
            ed = ent[b, 1:2, :] + fb * dev_in[1:2, :]
            F = eu * a_s[rb, :]
            fd = fade[...]
            num = S_s[rb, :] + fd * en + F * v_s[rb, :]
            rd = 1.0 / (D_s[rb, :] + fd * ed + F)
            wkv = num * rd
            S_s[rb, :] = wkv
            D_s[rb, :] = rd
            y_s[rb, :] = (sr_s[rb, :] * wkv).astype(BF16)
        x1 = tokv[r, :].astype(F32) + dot(y_s[r, :], w4[3])
        x1_s[r, :] = x1
        n2, _ = normed(x1)
        npad[pl.ds(pl.multiple_of(i * BR + 8, 8), BR), :] = n2 * par[G2 : G2 + 1, :] + par[B2 : B2 + 1, :]
        for cp in ship(outs_c, 6, i):
            cp.start()
        return carry

    lax.fori_loop(0, L.nblk, phase_c, 0)

    n_edge = remote(npad.at[pl.ds(L.R, 8)], nedge, e_ssem.at[1], e_rsem.at[1], (dp, nxt))
    n_edge.start()

    def phase_d(ii, carry):
        i = L.nblk - 1 - ii
        r = rows_of(i, BR)
        win = npad[pl.ds(pl.multiple_of(i * BR, 8), BR + 8), :]
        prev = pltpu.roll(win, 1, 0)[8:]
        d = win[8:] - prev
        ck_s[r, :] = (prev + d * par[CK : CK + 1, :]).astype(BF16)
        cr_s[r, :] = (prev + d * par[CR : CR + 1, :]).astype(BF16)
        for cp in ship(outs_d, 10, i):
            cp.start()
        return carry

    lax.fori_loop(0, L.nblk - 1, phase_d, 0)
    n_edge.wait()
    npad[0:8, :] = nedge[...] * keep
    edge_o[8:16, :] = nedge[...] * keep
    phase_d(L.nblk - 1, 0)

    for cp in keys.link(L.bits - 1):
        cp.wait_recv()
    for cp in keys.across(L.bits - 1):
        cp.start()
    for t in range(L.bits):
        for cp in keys.link(t):
            cp.wait_send()
        for cp in keys.across(t):
            cp.wait()
    for cp in values.link(0):
        cp.wait_send()
    for cp in values.across(0):
        cp.wait()

    def drain(i, carry):
        for outs, base in ((outs_a, 0), (outs_c, 6), (outs_d, 10)):
            for cp in ship(outs, base, i):
                cp.wait()
        return carry

    lax.fori_loop(0, L.nblk, drain, 0)


def front(L, tok, vecs, wk, wv, wr, wo, kshard, vshard):
    R, D, n_f, U = L.R, L.D, L.n_f, L.U
    _, flat = gather_steps(L)
    rb, rf = sds((R, D), BF16), sds((R, D))
    dma = pltpu.SemaphoreType.DMA
    return pl.pallas_call(
        functools.partial(front_kernel, L),
        out_shape=(rb,) * 6 + (rf,) * 4 + (rb, rf) + (sds((16, D)), sds((16, D)), sds((n_f, D, U), BF16), sds((n_f, U, D), BF16)),
        in_specs=[ANY] + [VMEM] * NVEC + [ANY] * 6,
        out_specs=(ANY,) * 12 + (VMEM, VMEM, ANY, ANY),
        scratch_shapes=[
            pltpu.VMEM((R, D), BF16), pltpu.VMEM((4, D, D), BF16), pltpu.VMEM((R + 8, D), F32),
            *([pltpu.VMEM((R, D), BF16)] * 6), *([pltpu.VMEM((R, D), F32)] * 6), pltpu.VMEM((R, D), BF16),
            pltpu.VMEM((SPAN, D), F32), pltpu.VMEM((SPAN, D), F32), pltpu.VMEM((SPAN, 2 * SPAN), BF16),
            pltpu.VMEM((L.nspan, 8, D), F32), pltpu.VMEM((8, D), F32), pltpu.VMEM((n_f, 8, D), F32),
            pltpu.VMEM((16, D), BF16), pltpu.VMEM((8, D), F32), pltpu.VMEM((8, D), F32),
            dma((5,)), dma((12, L.nblk)), dma((2,)), dma((2,)), dma((n_f,)), dma((n_f,)),
            dma((2, flat)), dma((2, flat)), dma((2, flat)), dma((2, flat)),
        ],
        compiler_params=pltpu.CompilerParams(collective_id=0, has_side_effects=True, vmem_limit_bytes=VLIMIT),
        cost_estimate=pl.CostEstimate(flops=10 * R * D * D, bytes_accessed=40 * R * D, transcendentals=4 * R * D),
        name="front",
    )(tok, *vecs, wk, wv, wr, wo, kshard, vshard)


def squeeze(mask, bit):
    return ((mask >> (bit + 1)) << bit) | (mask & ((1 << bit) - 1))


def middle_kernel(
    L, lens, ck, cr, x1, og, kall, vall, kshard, vshard, wc,
    mixed_o, g2_o, gck_o, gcr_o, big_o, dc_o,
    kv, vv, wcv, ck_s, cr_s, x1_s, gate_s, og_s, mix_s, gv_s, gg_s, ckt_s, gvt_s, h_s, p_s, dk_s, dv_s, dc_s, inc, r0,
    in_sem, w_sem, out_sem, g_sem, x_ssem, x_rsem, h_ssem, h_rsem, g_ssem, g_rsem, c_ssem, c_rsem,
):
    BR, n_f, D, U = L.BR, L.n_f, L.D, L.U
    dp, me = lax.axis_index("dp"), lax.axis_index("ffn")
    core = dp % 2
    buddy = dp + 1 - 2 * core
    half = D // 2
    hk = half // L.parts
    length = lens[me // L.per_slot]
    start = (me % L.per_slot) * L.R
    masks = sorted(range(n_f), key=lambda m: (-bin(m).count("1"), m))

    def fetch(n, src, dst):
        return pltpu.make_async_copy(src, dst, w_sem.at[n])

    k_cp = [fetch(m, kall.at[m] if m else kshard, kv.at[m]) for m in range(n_f)]
    v_cp = [fetch(n_f, vshard, vv.at[0])]
    uh = U // 2
    for p in range(L.parts):
        m = 1 << L.order(p)[0]
        for c in range(2):
            r = pl.ds(c * uh + p * (uh // L.parts), uh // L.parts)
            v_cp.append(fetch(n_f + 1 + 2 * p + c, vall.at[m, r], vv.at[m, r]))
    pairs = ((ck, ck_s), (cr, cr_s), (wc, wcv), (x1, x1_s), (og, og_s))
    ins = [pltpu.make_async_copy(s, d, in_sem.at[n]) for n, (s, d) in enumerate(pairs)]
    for cp in [ins[0]] + k_cp + v_cp + ins[1:]:
        cp.start()

    greet([(buddy, me)] + [(dp, flip(me, b)) for b in range(L.bits)])

    first = [1 << L.order(p)[0] for p in range(L.parts)]
    values = Gather(
        L, core, dp, me, uh,
        lambda m, r: vshard.at[r] if m == 0 else (vall.at[m, r] if m in first else vv.at[m, r]),
        lambda m, r: vv.at[m, r],
        (g_ssem, g_rsem, c_ssem, c_rsem),
    )
    if L.bits > 1:
        for cp in values.link(1):
            cp.start()
    for cp in [ins[0]] + k_cp:
        cp.wait()

    def keys_block(i, carry):
        r = rows_of(i, BR)
        ck_i = ck_s[r, :]
        for m in range(n_f):
            p = jnp.maximum(dot(ck_i, kv[m]), 0.0)
            p_s[m, r, :] = p.astype(BF16)
            h_s[m, r, :] = (p * p).astype(BF16)
        ckt_s[:, pl.ds(pl.multiple_of(i * BR, 128), BR)] = ck_i.T
        return carry

    lax.fori_loop(0, L.nblk, keys_block, 0)
    for cp in ins[1:3]:
        cp.wait()

    def gate_block(i, carry):
        r = rows_of(i, BR)
        gate_s[r, :] = sigmoid(dot(cr_s[r, :], wcv[...]))
        return carry

    lax.fori_loop(0, L.nblk, gate_block, 0)
    for cp in v_cp + ins[3:]:
        cp.wait()
    for t in range(1, L.bits):
        for cp in values.link(t):
            cp.wait_recv()
        for cp in values.across(t):
            cp.start()
        if t + 1 < L.bits:
            for cp in values.link(t + 1):
                cp.start()
    for t in range(1, L.bits):
        for cp in values.across(t):
            cp.wait_recv()

    def ship(i):
        r = rows_of(i, BR)
        both = ((mix_s, mixed_o), (og_s, g2_o), (ck_s, gck_o), (cr_s, gcr_o))
        return [pltpu.make_async_copy(s.at[r], d.at[r], out_sem.at[n, i]) for n, (s, d) in enumerate(both)]

    def values_block(i, carry):
        r = rows_of(i, BR)
        vsum = jnp.zeros((BR, D), F32)
        for m in range(n_f):
            vsum = vsum + dot(h_s[m, r, :], vv[m])
        pos = start + i * BR + lax.broadcasted_iota(jnp.int32, (BR, 1), 0)
        live = jnp.where(pos < length, 1.0, 0.0).astype(F32)
        gate_i = gate_s[r, :]
        mix_s[r, :] = ((x1_s[r, :] + gate_i * vsum) * live).astype(BF16)
        g2 = og_s[r, :].astype(F32) * live
        og_s[r, :] = g2.astype(BF16)
        gv32 = g2 * gate_i
        gv = gv32.astype(BF16)
        gv_s[r, :] = gv
        gg_s[r, :] = (gv32 * vsum * (1.0 - gate_i)).astype(BF16)
        gvt_s[:, pl.ds(pl.multiple_of(i * BR, 128), BR)] = gv.T
        for cp in ship(i)[:2]:
            cp.start()
        return carry

    lax.fori_loop(0, L.nblk, values_block, 0)

    own = pl.ds(pl.multiple_of(core * half, 16), half)
    away = pl.ds(pl.multiple_of((1 - core) * half, 16), half)

    def swaps(m):
        return [
            remote(g.at[m, away], inc.at[n, m], x_ssem.at[n, m], x_rsem.at[n, m], (buddy, me))
            for n, g in enumerate((dk_s, dv_s))
        ]

    def part_rows(p):
        return pl.ds(pl.multiple_of(core * half + p * hk, 16), hk)

    def halves(m):
        out = []
        for p in range(L.parts):
            bit = L.order(p)[0]
            if (m >> bit) & 1:
                k = squeeze(m, bit)
                for n, g in enumerate((dk_s, dv_s)):
                    out.append(
                        remote(g.at[m, part_rows(p)], r0.at[n, p, k], h_ssem.at[n, p, k], h_rsem.at[n, p, k],
                               (dp, flip(me, bit)))
                    )
        return out

    def merge(n, m):
        swaps(m)[n].wait_recv()
        g = (dk_s, dv_s)[n]
        g[m, own, :] = (g[m, own, :].astype(F32) + inc[n, m].astype(F32)).astype(BF16)
        for cp in halves(m)[n::2]:
            cp.start()

    def weight_grad(n, m):
        left, right, g = ((ckt_s, p_s, dk_s), (gvt_s, h_s, dv_s))[n]
        for c in range(D // BR):
            rr = slice(c * BR, (c + 1) * BR)
            g[m, rr, :] = dot(left[rr, :], right[m]).astype(BF16)
        swaps(m)[n].start()

    for n, m in enumerate(masks):
        weight_grad(1, m)
        if n > 0:
            merge(1, masks[n - 1])

    for n, m in enumerate(masks):
        def block(i, carry, m=m, n=n):
            r = rows_of(i, BR)
            gk = (dot(gv_s[r, :], vv[m], 1, 1) * (2.0 * p_s[m, r, :].astype(F32))).astype(BF16)
            p_s[m, r, :] = gk
            part = dot(gk, kv[m], 1, 1)
            total = part if n == 0 else x1_s[r, :] + part
            if n + 1 < n_f:
                x1_s[r, :] = total
            else:
                ck_s[r, :] = total.astype(BF16)
                ship(i)[2].start()
            return carry

        lax.fori_loop(0, L.nblk, block, 0)
        merge(0, masks[n - 1]) if n > 0 else merge(1, masks[-1])
        weight_grad(0, m)

    for c in range(D // BR):
        rr = slice(c * BR, (c + 1) * BR)
        dc_s[rr, :] = dot(cr_s[:, rr], gg_s[...], 0, 0).astype(BF16)
    merge(0, masks[-1])

    def last_block(i, carry):
        r = rows_of(i, BR)
        cr_s[r, :] = dot(gg_s[r, :], wcv[...], 1, 1).astype(BF16)
        ship(i)[3].start()
        return carry

    lax.fori_loop(0, L.nblk, last_block, 0)
    last = pltpu.make_async_copy(dc_s, dc_o, in_sem.at[0])
    last.start()

    outs = []
    for m in masks:
        for cp in halves(m):
            cp.wait_recv()
    for p in range(L.parts):
        bit = L.order(p)[0]
        for m in range(n_f):
            if (m >> bit) & 1:
                continue
            k = squeeze(m, bit)
            for n, g in enumerate((dk_s, dv_s)):
                r = part_rows(p)
                r0[n, p, k] = (g[m, r, :].astype(F32) + r0[n, p, k].astype(F32)).astype(BF16)
                outs.append(pltpu.make_async_copy(r0.at[n, p, k], big_o.at[n, p, k], g_sem.at[n, p, k]))
                outs[-1].start()
    for m in masks:
        for cp in halves(m) + swaps(m):
            cp.wait_send()
    for t in range(1, L.bits):
        for cp in values.link(t) + values.across(t):
            cp.wait_send()
    for i in range(L.nblk):
        for cp in ship(i):
            cp.wait()
    for cp in outs + [last]:
        cp.wait()


def middle(L, lens, ck, cr, x1, og, kall, vall, kshard, vshard, wc):
    R, D, n_f, U = L.R, L.D, L.n_f, L.U
    dma = pltpu.SemaphoreType.DMA
    rb = sds((R, D), BF16)
    vb, vf = pltpu.VMEM((R, D), BF16), pltpu.VMEM((R, D), F32)
    hid = pltpu.VMEM((n_f, R, U), BF16)
    kept = (2, L.parts, n_f // 2, D // 2 // L.parts, U)
    _, flat = gather_steps(L)
    sem3 = dma(kept[:3])
    return pl.pallas_call(
        functools.partial(middle_kernel, L),
        out_shape=(rb, rb, rb, rb, sds(kept, BF16), sds((D, D), BF16)),
        in_specs=[SMEM] + [ANY] * 9,
        out_specs=(ANY,) * 6,
        scratch_shapes=[
            pltpu.VMEM((n_f, D, U), BF16), pltpu.VMEM((n_f, U, D), BF16), pltpu.VMEM((D, D), BF16),
            vb, vb, vf, vf, vb, vb, vb, vb, pltpu.VMEM((D, R), BF16), pltpu.VMEM((D, R), BF16), hid, hid,
            pltpu.VMEM((n_f, D, U), BF16), pltpu.VMEM((n_f, D, U), BF16), pltpu.VMEM((D, D), BF16),
            pltpu.VMEM((2, n_f, D // 2, U), BF16), pltpu.VMEM(kept, BF16),
            dma((6,)), dma((n_f + 1 + 2 * L.parts,)), dma((4, L.nblk)), sem3, dma((2, n_f)), dma((2, n_f)),
            sem3, sem3, dma((flat,)), dma((flat,)), dma((flat,)), dma((flat,)),
        ],
        compiler_params=pltpu.CompilerParams(collective_id=1, has_side_effects=True, vmem_limit_bytes=VLIMIT),
        cost_estimate=pl.CostEstimate(flops=52 * R * D * D, bytes_accessed=60 * R * D, transcendentals=0),
        name="middle",
    )(lens, ck, cr, x1, og, kall, vall, kshard, vshard, wc)


class Pool:
    def __init__(self, ssem, rsem):
        self.ssem, self.rsem, self.n = ssem, rsem, 0

    def copy(self, src, dst, dev):
        k = self.n
        self.n = k + 1
        return remote(src, dst, self.ssem.at[k], self.rsem.at[k], dev)


def begin(copies):
    for cp in copies:
        cp.start()
    return copies


def landed(copies):
    for cp in copies:
        cp.wait_recv()


class Unit:
    def __init__(self, env, order, rows, done, acc, rbuf, zbuf, final, source=None, swap=None, gather=False):
        self.env, self.rows, self.acc, self.rbuf, self.zbuf, self.final = env, rows, acc, rbuf, zbuf, final
        self.source = source
        self.order = order
        self.sent, self.pending, self.now = [], None, []
        self.off, self.size, self.zoff, self.split, self.slot = 0, rows, 0, [], 0
        steps = [swap] if swap else []
        steps += [functools.partial(self.halve, t) for t in range(done, len(order))]
        steps += [functools.partial(self.halve_z, b) for b in range(env.zbits)]
        steps += [self.home]
        if gather:
            steps += [functools.partial(self.double, t) for t in range(len(order))]
        steps += [self.cross]
        self.steps = steps

    def keep(self, copies):
        self.sent += copies
        self.now = begin(copies)

    def advance(self):
        landed(self.now)
        self.now = []
        if self.pending:
            self.pending()
            self.pending = None
        if not self.steps:
            return False
        self.steps.pop(0)()
        return True

    def halve(self, t):
        e, bit = self.env, self.order[t]
        masks = spans(self.order[t + 1 :])
        base, src = self.slot, self.source or self.acc
        self.slot += len(masks)
        self.source = None
        self.keep([
            e.pool.copy(src(m | (1 << bit)), self.rbuf(base + n), (e.dp, flip(e.me, bit))) for n, m in enumerate(masks)
        ])

        def end():
            for n, m in enumerate(masks):
                view = self.acc(m)
                view[...] = (view[...].astype(F32) + self.rbuf(base + n)[...].astype(F32)).astype(BF16)

        self.pending = end

    def part(self, off, size):
        return pl.ds(pl.multiple_of(off, 16), size)

    def halve_z(self, b):
        e, mine = self.env, (self.env.zi // (1 << b)) % 2
        split = (self.size // 2) % 16 == 0
        size = self.size // 2 if split else self.size
        kept = self.off + (mine * size if split else 0)
        sent = self.off + ((1 - mine) * size if split else 0)
        buf = self.zbuf(pl.ds(self.zoff, size))
        self.zoff += size
        peer = (flip(e.zi, b) * 2 + e.core, e.me)
        self.keep([e.pool.copy(self.acc(0).at[self.part(sent, size)], buf, peer)])
        if split:
            self.split.append((b, self.off, self.size))
        self.off, self.size = kept, size

        def end():
            if not split:
                self.sent.pop().wait_send()
            view = self.acc(0).at[self.part(kept, size)]
            view[...] = (view[...].astype(F32) + buf[...].astype(F32)).astype(BF16)

        self.pending = end

    def home(self):
        e = self.env
        here = self.acc(0).at[self.part(self.off, self.size)]
        self.local = pltpu.make_async_copy(here, self.final(0, self.off, self.size), e.lsem.at[e.nl])
        e.nl += 1
        self.local.start()
        self.steps = [functools.partial(self.double_z, n) for n in reversed(range(len(self.split)))] + self.steps
        self.first = here
        if self.split:
            self.steps.pop(0)()
        else:
            self.pending = self.local.wait

    def double_z(self, n):
        e = self.env
        b, off, size = self.split[n]
        src = self.final(0, self.off, self.size) if self.first is None else self.first
        self.keep([e.pool.copy(src, self.final(0, self.off, self.size), (flip(e.zi, b) * 2 + e.core, e.me))])
        if self.first is not None:
            self.first = None
            self.pending = self.local.wait
        self.off, self.size = off, size

    def double(self, t):
        e, o = self.env, self.order
        out = []
        for m in spans(o[:t]):
            v = self.final(m, 0, self.rows)
            out.append(e.pool.copy(v, v, (e.dp, flip(e.me, o[t]))))
        self.keep(out)

    def cross(self):
        e = self.env
        v = self.final(None, 0, self.rows)
        self.keep([e.pool.copy(v, v, (e.dp + 1 - 2 * e.core, e.me))])


class Env:
    pass


KEY, VALUE, RECEPT, OUT, CMR = range(5)
FLIPPED = (OUT, VALUE)
HOOKS = {
    "1a": "M",
    "1b": "",
    "out": "ac",
    "rec": "",
    "key": "ORMbd",
    "value": "",
    "3a": "",
    "3b": "KVRMab",
    "4a": "O",
    "4b": "",
    "tail": "McdRKOMVWRKVOMRKOWabVRMKOMRVcOKdRVaKbOMV",
    "end": "KcdMabROabVcdRKOcdKVV",
}
V_LN1G, V_LN1B, V_TD, V_TF, V_MK, V_MV, V_MR, V_LN2G, V_LN2B, V_CMK, V_CMR = range(11)


def back_kernel(
    L, tok, par, edge, g2, gck, gcr, x1, y, sr, wkv, rd, a, v, xk, xv, xr, wk, wv, wr, wo, bigh, dch,
    ig_o, dkr, dvr, rep, vec_o,
    gkb_s, grb_s, srb_s, gck_s, gcr_s, x1_s, a_s, wkv_s, rd_s, v_s, g2_s, y_s, xr_s, gr_s, gk_s, gv_s, w3, dw, acc1,
    inc, r1, r2, z1, z2, grow, fade, tri, ent, st_out, st_in, carry, gpad, tpad, vacc, vown, vf, vd, dev_in,
    blk_sem, in_sem, out_sem, e_ssem, e_rsem, s_ssem, s_rsem, v_ssem, v_rsem, lsem, p_ssem, p_rsem,
):
    D, BR, n_f, n_dp, U, R = L.D, L.BR, L.n_f, L.n_dp, L.U, L.R
    dp, me = lax.axis_index("dp"), lax.axis_index("ffn")
    core = dp % 2
    buddy = dp + 1 - 2 * core
    place = me % L.per_slot
    opens = jnp.where(place == 0, 0.0, 1.0).astype(F32)
    stays = jnp.where(place == L.per_slot - 1, 0.0, 1.0).astype(F32)
    half = D // 2

    blocks = ((gck, gkb_s), (gcr, grb_s), (x1, x1_s), (g2, g2_s), (sr, srb_s), (wkv, wkv_s), (rd, rd_s))

    def load(i, which):
        r = rows_of(i, BR)
        return [pltpu.make_async_copy(blocks[n][0].at[r], blocks[n][1].at[r], blk_sem.at[n, i]) for n in which]

    wo_cp = pltpu.make_async_copy(wo, w3.at[2], in_sem.at[0])
    begin(load(0, range(7)) + [wo_cp])
    for i in range(1, L.nblk):
        begin(load(i, range(7)))
    acc_cp = pltpu.make_async_copy(bigh, acc1, in_sem.at[1])
    y_cp = pltpu.make_async_copy(y, y_s, in_sem.at[3])
    xr_cp = pltpu.make_async_copy(xr, xr_s, in_sem.at[4])
    v_cp = pltpu.make_async_copy(v, v_s, in_sem.at[5])
    a_cp = pltpu.make_async_copy(a, a_s, in_sem.at[11])
    dc_cps = [
        pltpu.make_async_copy(dch.at[:, pl.ds(h * half, half)], dw.at[CMR, h], in_sem.at[6 + h]) for h in range(2)
    ]
    w_cps = [pltpu.make_async_copy(w, w3.at[n], in_sem.at[8 + n]) for n, w in enumerate((wk, wv))]
    begin([acc_cp] + dc_cps + [y_cp, xr_cp, v_cp, a_cp] + w_cps)

    greet(
        [(dp, (me + k) % n_f) for k in range(1, n_f)] + [((dp + k) % n_dp, me) for k in range(1, n_dp)]
    )

    prv = (me + n_f - 1) % n_f
    edges = begin([
        remote(g.at[pl.ds(0, 16)], gpad.at[n], e_ssem.at[n], e_rsem.at[n], (dp, prv)) for n, g in enumerate((gck, gcr))
    ])

    e = Env()
    e.me, e.dp, e.core, e.zi, e.zbits = me, dp, core, dp // 2, L.nz.bit_length() - 1
    e.pool, e.lsem, e.nl = Pool(p_ssem, p_rsem), lsem, 0

    hk = half // L.parts
    big = []
    for n, res in enumerate((dkr, dvr)):
        for p in range(L.parts):
            o, off = L.order(p), p * hk

            def acc(m, n=n, p=p, o=o):
                return acc1.at[n, p, squeeze(m, o[0])]

            def source(m, n=n, p=p, o=o):
                return bigh.at[n, p, squeeze(m, o[0])]

            def rbuf(k, n=n, p=p):
                return r1.at[n, p, k]

            def zbuf(r, n=n, p=p):
                return z1.at[n, p, r]

            def final(m, r0, size, res=res, off=off):
                return res.at[pl.ds(pl.multiple_of(core * half + off + r0, 16), size)]

            big.append(Unit(e, o, hk, 1, acc, rbuf, zbuf, final, source))
    shard = D // n_f
    small = []
    for m_ in range(5):
        def acc(m, i=m_):
            return dw.at[i, core, pl.ds(pl.multiple_of(flips(me, m) * shard, 16), shard)]

        def rbuf(k, i=m_):
            return r2.at[i, k]

        def zbuf(r, i=m_):
            return z2.at[i, r]

        def final(m, r0, size, i=m_):
            cols = pl.ds(pl.multiple_of(core * half, 128), half)
            if m is None:
                return rep.at[i, :, cols]
            return rep.at[i, pl.ds(pl.multiple_of(flips(me, m) * shard + r0, 16), size), cols]

        def swap(i=m_):
            u = small[i]
            u.keep([e.pool.copy(dw.at[i, 1 - core], inc.at[i], (buddy, me))])

            def end():
                dw[i, core] = (dw[i, core].astype(F32) + inc[i].astype(F32)).astype(BF16)

            u.pending = end

        o = L.order(1) if m_ in FLIPPED else L.order(0)
        small.append(Unit(e, o, shard, 0, acc, rbuf, zbuf, final, None, swap, True))
    units = dict(zip("MORKV", (small[CMR], small[OUT], small[RECEPT], small[KEY], small[VALUE])))
    units.update(zip("abcd" if L.parts == 2 else "ac", big))

    class Vectors:
        def __init__(self):
            self.stage = 0

        def advance(self):
            self.stage += 1
            if self.stage == 1:
                vown[...] = jnp.sum(vacc[...], axis=1)
                vf[0] = vown[...]
                self.now = begin([
                    remote(vown, vf.at[k], v_ssem.at[0, k], v_rsem.at[0, k], (dp, (me + k) % n_f))
                    for k in range(1, n_f)
                ])
            elif self.stage == 2:
                for cp in self.now:
                    cp.wait()
                total = vf[me % n_f]
                for f in range(1, n_f):
                    total = total + vf[(me - f + n_f) % n_f]
                vd[0] = total
                self.now = begin([
                    remote(vd.at[0], vd.at[k], v_ssem.at[1, k], v_rsem.at[1, k], ((dp + k) % n_dp, me))
                    for k in range(1, n_dp)
                ])
            elif self.stage == 3:
                for cp in self.now:
                    cp.wait()
                total = vd[dp % n_dp]
                for f in range(1, n_dp):
                    total = total + vd[(dp - f + n_dp) % n_dp]
                vec_o[...] = total
                vec_o[V_TD : V_TD + 1, :] = w * (total[V_TD : V_TD + 1] - total[V_TF : V_TF + 1])
            return self.stage < 3

    units["W"] = Vectors()

    def go(names):
        for name in names:
            if name in units:
                units[name].advance()

    go("abcd")

    w = jnp.exp(par[TD : TD + 1, :])
    ew = jnp.exp(w)
    eu = jnp.exp(par[TF : TF + 1, :])
    age = lax.broadcasted_iota(jnp.int32, (SPAN, D), 0).astype(F32) * w
    grow[...] = jnp.exp(age)
    fade[...] = jnp.exp(-age)
    tri[...] = tri_pair(False)
    full_fade = jnp.exp(-float(SPAN) * w)
    tail_fade = jnp.exp(-float(SPAN - 1) * w)
    vacc[...] = jnp.zeros_like(vacc)
    carry[...] = edge[8:16, :]

    def add_up(n, x):
        vacc[n] = vacc[n] + jnp.sum(x.reshape(-1, 8, D), axis=0)

    for cp in dc_cps:
        cp.wait()
    go("M")
    acc_cp.wait()
    wo_cp.wait()
    for cp in load(0, (0, 1)):
        cp.wait()

    def phase_1(i, _):
        @pl.when(i + 1 < L.nblk)
        def _wait():
            for cp in load(i + 1, (0, 1)):
                cp.wait()

        for cp in load(i, range(2, 7)):
            cp.wait()
        r = rows_of(i, BR)
        win = pl.ds(pl.multiple_of(i * BR, 16), BR + 16)
        mk, mr = par[CK : CK + 1, :], par[CR : CR + 1, :]
        gk = gkb_s[win, :].astype(F32)
        gr = grb_s[win, :].astype(F32)
        t = gk * (1.0 - mk) + gr * (1.0 - mr)
        t = pltpu.roll(t, BR + 15, 0)[:BR]
        gk, gr = gk[:BR], gr[:BR]
        gn = gk * mk + gr * mr + t
        n2, rs = normed(x1_s[r, :])
        norm2 = n2 * par[G2 : G2 + 1, :] + par[B2 : B2 + 1, :]
        prev = pltpu.roll(jnp.concatenate([carry[...], norm2], axis=0), 1, 0)[8:]
        carry[...] = norm2[BR - 8 :]
        d = norm2 - prev
        add_up(V_CMK, gk * d)
        add_up(V_CMR, gr * d)
        add_up(V_LN2G, gn * n2)
        add_up(V_LN2B, gn)
        q1 = gn * par[G2 : G2 + 1, :]
        m1 = jnp.mean(q1, axis=-1, keepdims=True)
        m2 = jnp.mean(q1 * n2, axis=-1, keepdims=True)
        g1 = g2_s[r, :].astype(F32) + (q1 - m1 - n2 * m2) * rs
        x1_s[r, :] = g1
        ga = g1.astype(BF16)
        g2_s[r, :] = ga
        s = srb_s[r, :].astype(F32)
        gys = dot(ga, w3[2], 1, 1) * s
        wk_ = wkv_s[r, :]
        gr_s[r, :] = (gys * wk_ * (1.0 - s)).astype(BF16)
        q = gys * rd_s[r, :]
        qw = q * wk_
        rd_s[r, :] = q
        wkv_s[r, :] = qw
        for sb in range(BR // SPAN):
            b = i * (BR // SPAN) + sb
            rb = rows_of(b, SPAN)
            sl = slice(sb * SPAN, (sb + 1) * SPAN)
            fd = fade[...]
            both = jnp.concatenate([fd * q[sl], fd * qw[sl]], axis=1)
            suf = dot(tri[...], split2(both))
            gs = grow[...] * ew
            gck_s[rb, :] = gs * suf[:, :D]
            gcr_s[rb, :] = gs * suf[:, D:]
            tot = suf[0:1] + both[0:1]
            ent[b, 0:1, :] = tot[:, :D]
            ent[b, 1:2, :] = tot[:, D:]
        return 0

    cut = L.nblk // 2
    lax.fori_loop(0, cut, phase_1, 0)
    go(HOOKS["1a"])
    lax.fori_loop(cut, L.nblk - 1, phase_1, 0)
    for cp in edges:
        cp.wait()
    gkb_s[R : R + 16, :] = (gpad[0].astype(F32) * stays).astype(BF16)
    grb_s[R : R + 16, :] = (gpad[1].astype(F32) * stays).astype(BF16)
    phase_1(L.nblk - 1, 0)

    go(HOOKS["1b"])
    xq = jnp.zeros((1, D), F32)
    xw = jnp.zeros((1, D), F32)
    for b in reversed(range(L.nspan)):
        tq, tw = ent[b, 0:1, :], ent[b, 1:2, :]
        ent[b, 0:1, :] = xq
        ent[b, 1:2, :] = xw
        xq = tq + full_fade * xq
        xw = tw + full_fade * xw
    st_out[...] = jnp.zeros_like(st_out)
    st_out[0:1, :] = xq
    st_out[1:2, :] = xw
    states = begin([
        remote(st_out, st_in.at[k], s_ssem.at[k], s_rsem.at[k], (dp, (me + n_f - k) % n_f)) for k in range(1, n_f)
    ])
    w_cps.append(pltpu.make_async_copy(wr, w3.at[2], in_sem.at[10]))
    w_cps[-1].start()

    def product(m, left, right):
        for c in range(D // BR):
            rr = slice(c * BR, (c + 1) * BR)
            full = dot(left[:, rr], right[...], 0, 0).astype(BF16)
            dw[m, 0, rr, :] = full[:, :half]
            dw[m, 1, rr, :] = full[:, half:]

    y_cp.wait()
    product(OUT, y_s, g2_s)
    xk_cp = pltpu.make_async_copy(xk, y_s, in_sem.at[12])
    xv_cp = pltpu.make_async_copy(xv, g2_s, in_sem.at[14])
    begin([xk_cp, xv_cp])
    go("O" + HOOKS["out"])
    xr_cp.wait()
    product(RECEPT, xr_s, gr_s)
    go("R" + HOOKS["rec"])

    for cp in states:
        cp.wait()
    qi = jnp.zeros((1, D), F32)
    wi = jnp.zeros((1, D), F32)
    for k in range(1, L.per_slot):
        f = jnp.exp(-float((k - 1) * R) * w) * jnp.where(place + k < L.per_slot, 1.0, 0.0).astype(F32)
        qi = qi + f * st_in[k, 0:1, :]
        wi = wi + f * st_in[k, 1:2, :]
    dev_in[0:1, :] = qi
    dev_in[1:2, :] = wi
    a_cp.wait()
    v_cp.wait()
    first = place * R - (L.per_slot * R) // 2

    def phase_2(b, _):
        rb = rows_of(b, SPAN)
        fb = jnp.exp(w * ((b + 1 - L.nspan) * SPAN).astype(F32))
        eq = ent[b, 0:1, :] + fb * dev_in[0:1, :]
        ewk = ent[b, 1:2, :] + fb * dev_in[1:2, :]
        ff = grow[...] * tail_fade
        q, qw, av, vv = rd_s[rb, :], wkv_s[rb, :], a_s[rb, :], v_s[rb, :]
        gvr = av * (eu * q + gck_s[rb, :] + ff * eq)
        gkr = vv * gvr - av * (eu * qw + gcr_s[rb, :] + ff * ewk)
        gk_s[rb, :] = gkr.astype(BF16)
        gv_s[rb, :] = gvr.astype(BF16)
        add_up(V_TF, eu * av * (q * vv - qw))
        pos = (first + b * SPAN + lax.broadcasted_iota(jnp.int32, (SPAN, 1), 0)).astype(F32)
        add_up(V_TD, pos * gkr)
        return 0

    lax.fori_loop(0, L.nspan, phase_2, 0)
    xk_cp.wait()
    product(KEY, y_s, gk_s)
    tok_cp = pltpu.make_async_copy(tok, y_s, in_sem.at[13])
    tok_cp.start()
    go("K" + HOOKS["key"])
    xv_cp.wait()
    product(VALUE, g2_s, gv_s)
    go("V" + HOOKS["value"])

    for cp in w_cps:
        cp.wait()
    tok_cp.wait()
    carry[...] = edge[0:8, :]

    def phase_3(i, _):
        r = rows_of(i, BR)
        mk, mv, mr = par[MK : MK + 1, :], par[MV : MV + 1, :], par[MR : MR + 1, :]
        n1_, _rs = normed(y_s[r, :].astype(F32))
        norm1 = n1_ * par[G1 : G1 + 1, :] + par[B1 : B1 + 1, :]
        prev = pltpu.roll(jnp.concatenate([carry[...], norm1], axis=0), 1, 0)[8:]
        carry[...] = norm1[BR - 8 :]
        d = norm1 - prev
        gxk = dot(gk_s[r, :], w3[0], 1, 1)
        gxv = dot(gv_s[r, :], w3[1], 1, 1)
        gxr = dot(gr_s[r, :], w3[2], 1, 1)
        add_up(V_MK, gxk * d)
        add_up(V_MV, gxv * d)
        add_up(V_MR, gxr * d)
        now = gxk * mk + gxv * mv + gxr * mr
        gck_s[r, :] = gxk + gxv + gxr - now
        gcr_s[r, :] = now
        return 0

    lax.fori_loop(0, cut, phase_3, 0)
    t_cp = remote(gck_s.at[pl.ds(0, 8)], tpad, e_ssem.at[2], e_rsem.at[2], (dp, prv))
    t_cp.start()
    go(HOOKS["3a"])
    lax.fori_loop(cut, L.nblk, phase_3, 0)
    go(HOOKS["3b"])
    t_cp.wait()
    gck_s[R : R + 8, :] = tpad[...] * stays

    def phase_4(i, _):
        r = rows_of(i, BR)
        t = gck_s[pl.ds(pl.multiple_of(i * BR, 8), BR + 8), :]
        gn = gcr_s[r, :] + pltpu.roll(t, BR + 7, 0)[:BR]
        n1_, rs = normed(y_s[r, :].astype(F32))
        add_up(V_LN1G, gn * n1_)
        add_up(V_LN1B, gn)
        q1 = gn * par[G1 : G1 + 1, :]
        m1 = jnp.mean(q1, axis=-1, keepdims=True)
        m2 = jnp.mean(q1 * n1_, axis=-1, keepdims=True)
        y_s[r, :] = (x1_s[r, :] + (q1 - m1 - n1_ * m2) * rs).astype(BF16)
        pltpu.make_async_copy(y_s.at[r], ig_o.at[r], out_sem.at[i]).start()
        return 0

    lax.fori_loop(0, cut, phase_4, 0)
    go(HOOKS["4a"])
    lax.fori_loop(cut, L.nblk, phase_4, 0)
    go("W" + HOOKS["4b"])
    go(HOOKS["tail"])
    go(HOOKS["end"])
    live = [u for u in units.values()]
    while live:
        live = [u for u in live if u.advance()]
    for u in big + small:
        for cp in u.sent:
            cp.wait_send()
    for i in range(L.nblk):
        pltpu.make_async_copy(y_s.at[rows_of(i, BR)], ig_o.at[rows_of(i, BR)], out_sem.at[i]).wait()


def back(L, *args):
    R, D, n_f, n_dp, U = L.R, L.D, L.n_f, L.n_dp, L.U
    half, shard = D // 2, D // L.n_f
    hk = half // L.parts
    dma = pltpu.SemaphoreType.DMA
    bpad, fpad, full, low = pltpu.VMEM((R + 16, D), BF16), pltpu.VMEM((R + 8, D), F32), pltpu.VMEM((R, D), F32), pltpu.VMEM((R, D), BF16)
    rows8 = pltpu.VMEM((8, D), F32)
    zbits = L.nz.bit_length() - 1

    def z_rows(rows):
        total = 0
        for _ in range(zbits):
            rows = rows // 2 if (rows // 2) % 16 == 0 else rows
            total += rows
        return total

    n_r = n_f - 1
    n_pool = 2 * L.parts * (n_r + 2 * zbits + 1) + 5 * (2 * n_r + 2 * zbits + 2)
    return pl.pallas_call(
        functools.partial(back_kernel, L),
        out_shape=(
            sds((R, D), BF16), sds((D, U), BF16), sds((D, U), BF16), sds((5, D, D), BF16), sds((16, D)),
        ),
        in_specs=[ANY, VMEM, VMEM] + [ANY] * 19,
        out_specs=(ANY, ANY, ANY, ANY, VMEM),
        scratch_shapes=[
            bpad, bpad, low, fpad, full, full, full, full, full, full, low, low, low, low, low, low,
            pltpu.VMEM((3, D, D), BF16), pltpu.VMEM((5, 2, D, half), BF16), pltpu.VMEM((2, L.parts, n_f // 2, hk, U), BF16),
            pltpu.VMEM((5, D, half), BF16), pltpu.VMEM((2, L.parts, max(n_f // 2 - 1, 1), hk, U), BF16),
            pltpu.VMEM((5, n_r, shard, half), BF16), pltpu.VMEM((2, L.parts, z_rows(hk), U), BF16),
            pltpu.VMEM((5, z_rows(shard), half), BF16),
            pltpu.VMEM((SPAN, D), F32), pltpu.VMEM((SPAN, D), F32), pltpu.VMEM((SPAN, 2 * SPAN), BF16),
            pltpu.VMEM((L.nspan, 8, D), F32), rows8, pltpu.VMEM((n_f, 8, D), F32), rows8,
            pltpu.VMEM((2, 16, D), BF16), rows8, pltpu.VMEM((16, 8, D), F32), pltpu.VMEM((16, D), F32),
            pltpu.VMEM((n_f, 16, D), F32), pltpu.VMEM((n_dp, 16, D), F32), rows8,
            dma((7, L.nblk)), dma((15,)), dma((L.nblk,)), dma((3,)), dma((3,)), dma((n_f,)), dma((n_f,)),
            dma((2, n_dp)), dma((2, n_dp)), dma((16,)), dma((n_pool,)), dma((n_pool,)),
        ],
        compiler_params=pltpu.CompilerParams(collective_id=2, has_side_effects=True, vmem_limit_bytes=VLIMIT),
        cost_estimate=pl.CostEstimate(flops=20 * R * D * D, bytes_accessed=60 * R * D, transcendentals=0),
        name="back",
    )(*args)


def finish_kernel(n, rep, dkr, dvr, mixed, ig, vec, *outs):
    mats, vecs = outs[:7], outs[9:]
    outs[7][...] = mixed[...]
    outs[8][...] = ig[...]
    for m in range(5):
        mats[m][...] = rep[m].astype(F32)
    mats[5][...] = dkr[...].astype(F32)
    mats[6][...] = dvr[...].astype(F32).T

    @pl.when(pl.program_id(0) == 0)
    def _():
        for k in range(NVEC):
            vecs[k][...] = vec[k, :]


def finish(L, rep, dkr, dvr, mixed, ig, vec):
    R, D, U = L.R, L.D, L.U
    n = 4 if U % 512 == 0 else 3
    n = 6 if U % 768 == 0 else n
    rows, cols, lines = D // n, U // n, -(-R // (16 * n)) * 16
    row = pl.BlockSpec((lines, D), lambda i: (i, 0))
    mat = pl.BlockSpec((rows, D), lambda i: (i, 0))
    return pl.pallas_call(
        functools.partial(finish_kernel, n),
        grid=(n,),
        out_shape=(sds((D, D)),) * 5 + (sds((D, U)), sds((U, D))) + (sds((R, D), BF16),) * 2 + (sds((D,)),) * NVEC,
        in_specs=[
            pl.BlockSpec((5, rows, D), lambda i: (0, i, 0)), pl.BlockSpec((rows, U), lambda i: (i, 0)),
            pl.BlockSpec((D, cols), lambda i: (0, i)), row, row, pl.BlockSpec((16, D), lambda i: (0, 0)),
        ],
        out_specs=(mat,) * 5 + (pl.BlockSpec((rows, U), lambda i: (i, 0)), pl.BlockSpec((cols, D), lambda i: (i, 0)), row, row)
        + (pl.BlockSpec((D,), lambda i: (0,)),) * NVEC,
        compiler_params=pltpu.CompilerParams(vmem_limit_bytes=VLIMIT),
        cost_estimate=pl.CostEstimate(flops=0, bytes_accessed=42 * D * D, transcendentals=0),
        name="finish",
    )(rep, dkr, dvr, mixed, ig, vec)


def solution(mesh):
    def step(
        tokens, lens, og, ln1g, ln1b, td, tf, mk, mv, mr, wk, wv, wr, wo, ln2g, ln2b, cmk, cmr, ckw, cvw, wc
    ):
        L = Layout(mesh, tokens.shape[0], tokens.shape[1], ckw.shape[1])
        vecs = [ln1g, ln1b, td, tf, mk, mv, mr, ln2g, ln2b, cmk, cmr]
        xk, xv, xr, y, ck, cr, a, v, rd, wkv, sr, x1, edge, par, kall, vall = front(
            L, tokens, vecs, wk, wv, wr, wo, ckw, cvw
        )
        mixed, g2, gck, gcr, big, dc = middle(L, lens, ck, cr, x1, og, kall, vall, ckw, cvw, wc)
        ig, dkr, dvr, rep, vec = back(
            L, tokens, par, edge, g2, gck, gcr, x1, y, sr, wkv, rd, a, v, xk, xv, xr, wk, wv, wr, wo, big, dc
        )
        done = finish(L, rep, dkr, dvr, mixed, ig, vec)
        mats, (mixed, ig), vecs = done[:7], done[7:9], done[9:]
        return (mixed, ig, *vecs[:7], *mats[:4], *vecs[7:], mats[5], mats[6], mats[4])

    row, none = P(("dp", "ffn"), None), P()
    return jax.shard_map(
        step,
        mesh=mesh,
        in_specs=(row, P("dp"), row) + (none,) * 15 + (P(None, "ffn"), P("ffn", None), none),
        out_specs=(row, row) + (none,) * 15 + (P(None, "ffn"), P("ffn", None), none),
        check_vma=False,
    )
```

```python
import functools

import jax
import jax.numpy as jnp
from jax import lax
from jax.experimental import pallas as pl
from jax.experimental.pallas import tpu as pltpu
from jax.sharding import PartitionSpec as P

MAX_LEN = 4096
SPAN = 128
EPS = 1e-05
MESH = pl.DeviceIdType.MESH
F32 = jnp.float32
BF16 = jnp.bfloat16
ANY = pl.BlockSpec(memory_space=pl.ANY)
VMEM = pl.BlockSpec(memory_space=pltpu.VMEM)
SMEM = pl.BlockSpec(memory_space=pltpu.SMEM)
VLIMIT = 62 * 2**20
G1, B1, TD, TF, MK, MV, MR, G2, B2, CK, CR = range(11)
NVEC = 11


def dot(a, b, da=1, db=0):
    return lax.dot_general(a, b, (((da,), (db,)), ((), ())), preferred_element_type=F32)


def sds(shape, dtype=F32):
    return jax.ShapeDtypeStruct(shape, dtype)


def flip(i, bit):
    s = 1 << bit
    return i + s - 2 * s * ((i // s) % 2)


def rows_of(i, n):
    return pl.ds(pl.multiple_of(i * n, n), n)


def sigmoid(x):
    return 1.0 / (1.0 + jnp.exp(-x))


def normed(x):
    c = x - jnp.mean(x, axis=-1, keepdims=True)
    rs = lax.rsqrt(jnp.mean(c * c, axis=-1, keepdims=True) + EPS)
    return c * rs, rs


def split2(x):
    hi = x.astype(BF16)
    lo = (x - hi.astype(F32)).astype(BF16)
    return jnp.concatenate([hi, lo], axis=0)


def tri_pair(below):
    r = lax.broadcasted_iota(jnp.int32, (SPAN, 2 * SPAN), 0)
    c = lax.broadcasted_iota(jnp.int32, (SPAN, 2 * SPAN), 1) % SPAN
    keep = (r > c) if below else (r < c)
    return jnp.where(keep, 1.0, 0.0).astype(BF16)


def greet(peers):
    bar = pltpu.get_barrier_semaphore()
    for p in peers:
        pl.semaphore_signal(bar, inc=1, device_id=p, device_id_type=MESH)
    pl.semaphore_wait(bar, len(peers))


def remote(src, dst, ssem, rsem, dev):
    return pltpu.make_async_remote_copy(
        src_ref=src, dst_ref=dst, send_sem=ssem, recv_sem=rsem, device_id=dev, device_id_type=MESH
    )


class Layout:
    def __init__(self, mesh, rows, width, local_units):
        self.n_f = mesh.shape["ffn"]
        self.n_dp = mesh.shape["dp"]
        self.R = rows
        self.D = width
        self.U = local_units
        self.BR = 256
        self.nblk = rows // self.BR
        self.nspan = rows // SPAN
        slot_len = min(MAX_LEN, rows * self.n_f)
        self.per_slot = slot_len // rows
        self.bits = self.n_f.bit_length() - 1
        self.parts = 2 if self.bits == 2 else 1
        self.nz = self.n_dp // 2

    def order(self, part):
        b = list(range(self.bits))
        return b if part == 0 else b[::-1]


def flips(i, mask):
    b = 0
    while mask >> b:
        if (mask >> b) & 1:
            i = flip(i, b)
        b += 1
    return i


def spans(bits):
    out = [0]
    for b in bits:
        out = out + [m | (1 << b) for m in out]
    return out


def gather_steps(L):
    steps, flat = [], 0
    for t in range(L.bits):
        here = []
        for p in range(L.parts):
            o = L.order(p)
            for m in spans(o[:t]):
                here.append((p, o[t], m, flat))
                flat += 1
        steps.append(here)
    return steps, flat


class Gather:
    def __init__(self, L, core, dp, me, half, source, dest, sems):
        self.L, self.half, self.source, self.dest = L, half, source, dest
        self.core, self.dp, self.me = core, dp, me
        self.g_ssem, self.g_rsem, self.c_ssem, self.c_rsem = sems
        self.steps, _ = gather_steps(L)

    def rows(self, p):
        n = self.half // self.L.parts
        return pl.ds(pl.multiple_of(self.core * self.half + p * n, 16), n)

    def link(self, t, own=None):
        return [
            remote(self.source(m, self.rows(p)), self.dest(m | (1 << bit), self.rows(p)),
                   self.g_ssem.at[f], self.g_rsem.at[f], (self.dp, flip(self.me, bit)))
            for p, bit, m, f in self.steps[t]
            if own is None or own == (m == 0)
        ]

    def across(self, t):
        buddy = self.dp + 1 - 2 * self.core
        out = []
        for p, bit, m, f in self.steps[t]:
            ref = self.dest(m | (1 << bit), self.rows(p))
            out.append(remote(ref, ref, self.c_ssem.at[f], self.c_rsem.at[f], (buddy, self.me)))
        return out


def front_kernel(
    L, tok, *refs
):
    vecs, refs = refs[:NVEC], refs[NVEC:]
    (
        wk, wv, wr, wo, kshard, vshard,
        xk_o, xv_o, xr_o, y_o, ck_o, cr_o, a_o, v_o, rd_o, wkv_o, sr_o, x1_o, edge_o, par, kall, vall,
        tokv, w4, npad, xk_s, xv_s, xr_s, y_s, ck_s, cr_s, a_s, v_s, S_s, D_s, sr_s, x1_s, srb_s,
        grow, fade, tri, ent, st_out, st_in, tedge, nedge, dev_in,
        in_sem, out_sem, e_ssem, e_rsem, s_ssem, s_rsem, g_ssem, g_rsem, c_ssem, c_rsem,
    ) = refs
    D, BR, n_f = L.D, L.BR, L.n_f
    dp, me = lax.axis_index("dp"), lax.axis_index("ffn")
    core = dp % 2
    buddy = dp + 1 - 2 * core
    place = me % L.per_slot
    keep = jnp.where(place == 0, 0.0, 1.0).astype(F32)
    ins = [pltpu.make_async_copy(tok, tokv, in_sem.at[0])]
    for n, w in enumerate((wk, wv, wr, wo)):
        ins.append(pltpu.make_async_copy(w, w4.at[n], in_sem.at[1 + n]))
    for cp in ins:
        cp.start()
    greet([(dp, (me + k) % n_f) for k in range(1, n_f)] + [(buddy, me)])

    nxt = (me + 1) % n_f
    tok_edge = remote(tok.at[pl.ds(L.R - 16, 16)], tedge, e_ssem.at[0], e_rsem.at[0], (dp, nxt))
    tok_edge.start()

    def gather(n, shard, full, half):
        return Gather(
            L, core, dp, me, half,
            lambda m, r: full.at[m, r] if m else shard.at[r],
            lambda m, r: full.at[m, r],
            (g_ssem.at[n], g_rsem.at[n], c_ssem.at[n], c_rsem.at[n]),
        )

    keys, values = gather(0, kshard, kall, D // 2), gather(1, vshard, vall, L.U // 2)
    for cp in keys.link(0) + values.link(0):
        cp.start()
    for n in range(NVEC):
        par[n : n + 1, :] = vecs[n][...].reshape(1, D)

    w = jnp.exp(par[TD : TD + 1, :])
    ew = jnp.exp(w)
    eu = jnp.exp(par[TF : TF + 1, :])
    age = lax.broadcasted_iota(jnp.int32, (SPAN, D), 0).astype(F32) * w
    grow[...] = jnp.exp(age)
    fade[...] = jnp.exp(-age)
    tri[...] = tri_pair(True)
    full_fade = jnp.exp(-float(SPAN) * w)
    tail_fade = jnp.exp(-float(SPAN - 1) * w)
    st_out[...] = jnp.zeros_like(st_out)

    ins[0].wait()
    tok_edge.wait()
    en, _ = normed(tedge[...].astype(F32))
    en = (en * par[G1 : G1 + 1, :] + par[B1 : B1 + 1, :])[8:16] * keep
    npad[0:8, :] = en
    edge_o[0:8, :] = en
    for cp in ins[1:4]:
        cp.wait()

    outs_a = ((xk_s, xk_o), (xv_s, xv_o), (xr_s, xr_o), (a_s, a_o), (v_s, v_o), (srb_s, sr_o))
    outs_c = ((y_s, y_o), (S_s, wkv_o), (D_s, rd_o), (x1_s, x1_o))
    outs_d = ((ck_s, ck_o), (cr_s, cr_o))

    def ship(outs, base, i):
        return [
            pltpu.make_async_copy(s.at[rows_of(i, BR)], o.at[rows_of(i, BR)], out_sem.at[base + n, i])
            for n, (s, o) in enumerate(outs)
        ]

    def phase_a(i, carry):
        r = rows_of(i, BR)
        n1, _ = normed(tokv[r, :].astype(F32))
        n1 = n1 * par[G1 : G1 + 1, :] + par[B1 : B1 + 1, :]
        npad[pl.ds(pl.multiple_of(i * BR + 8, 8), BR), :] = n1
        prev = pltpu.roll(npad[pl.ds(pl.multiple_of(i * BR, 8), BR + 8), :], 1, 0)[8:]
        d = n1 - prev
        xk = (prev + d * par[MK : MK + 1, :]).astype(BF16)
        xv = (prev + d * par[MV : MV + 1, :]).astype(BF16)
        xr = (prev + d * par[MR : MR + 1, :]).astype(BF16)
        xk_s[r, :] = xk
        xv_s[r, :] = xv
        xr_s[r, :] = xr
        a = jnp.exp(dot(xk, w4[0]))
        v = dot(xv, w4[1])
        a_s[r, :] = a
        v_s[r, :] = v
        for sb in range(BR // SPAN):
            b = i * (BR // SPAN) + sb
            aa = a[sb * SPAN : (sb + 1) * SPAN]
            vv = v[sb * SPAN : (sb + 1) * SPAN]
            ga = grow[...] * aa
            both = jnp.concatenate([ga * vv, ga], axis=1)
            pre = dot(tri[...], split2(both))
            fs = fade[...] * ew
            S_s[rows_of(b, SPAN), :] = fs * pre[:, :D]
            D_s[rows_of(b, SPAN), :] = fs * pre[:, D:]
            tot = pre[SPAN - 1 : SPAN] + both[SPAN - 1 : SPAN]
            num, den = st_out[0:1, :], st_out[1:2, :]
            ent[b, 0:1, :] = num
            ent[b, 1:2, :] = den
            st_out[0:1, :] = full_fade * num + tail_fade * tot[:, :D]
            st_out[1:2, :] = full_fade * den + tail_fade * tot[:, D:]
        sr = sigmoid(dot(xr, w4[2]))
        sr_s[r, :] = sr
        srb_s[r, :] = sr.astype(BF16)
        for cp in ship(outs_a, 0, i):
            cp.start()
        return carry

    lax.fori_loop(0, L.nblk, phase_a, 0)

    states = [
        remote(st_out, st_in.at[k], s_ssem.at[k], s_rsem.at[k], (dp, (me + k) % n_f)) for k in range(1, n_f)
    ]
    for cp in states:
        cp.start()

    for t in range(L.bits - 1):
        for cp in keys.link(t):
            cp.wait_recv()
        for cp in keys.link(t + 1):
            cp.start()
    for cp in values.link(0):
        cp.wait_recv()
    for t in range(L.bits - 1):
        for cp in keys.across(t):
            cp.start()
    for cp in values.across(0):
        cp.start()

    for cp in states:
        cp.wait()
    num_in = jnp.zeros((1, D), F32)
    den_in = jnp.zeros((1, D), F32)
    for k in range(1, L.per_slot):
        ok = jnp.where(place >= k, 1.0, 0.0).astype(F32)
        f = jnp.exp(-float((k - 1) * L.R) * w) * ok
        num_in = num_in + f * st_in[k, 0:1, :]
        den_in = den_in + f * st_in[k, 1:2, :]
    dev_in[0:1, :] = num_in
    dev_in[1:2, :] = den_in
    for cp in ins[4:]:
        cp.wait()

    def phase_c(i, carry):
        r = rows_of(i, BR)
        for sb in range(BR // SPAN):
            b = i * (BR // SPAN) + sb
            rb = rows_of(b, SPAN)
            fb = jnp.exp(w * (b * (-SPAN)).astype(F32))
            en = ent[b, 0:1, :] + fb * dev_in[0:1, :]
            ed = ent[b, 1:2, :] + fb * dev_in[1:2, :]
            F = eu * a_s[rb, :]
            fd = fade[...]
            num = S_s[rb, :] + fd * en + F * v_s[rb, :]
            rd = 1.0 / (D_s[rb, :] + fd * ed + F)
            wkv = num * rd
            S_s[rb, :] = wkv
            D_s[rb, :] = rd
            y_s[rb, :] = (sr_s[rb, :] * wkv).astype(BF16)
        x1 = tokv[r, :].astype(F32) + dot(y_s[r, :], w4[3])
        x1_s[r, :] = x1
        n2, _ = normed(x1)
        npad[pl.ds(pl.multiple_of(i * BR + 8, 8), BR), :] = n2 * par[G2 : G2 + 1, :] + par[B2 : B2 + 1, :]
        for cp in ship(outs_c, 6, i):
            cp.start()
        return carry

    lax.fori_loop(0, L.nblk, phase_c, 0)

    n_edge = remote(npad.at[pl.ds(L.R, 8)], nedge, e_ssem.at[1], e_rsem.at[1], (dp, nxt))
    n_edge.start()

    def phase_d(ii, carry):
        i = L.nblk - 1 - ii
        r = rows_of(i, BR)
        win = npad[pl.ds(pl.multiple_of(i * BR, 8), BR + 8), :]
        prev = pltpu.roll(win, 1, 0)[8:]
        d = win[8:] - prev
        ck_s[r, :] = (prev + d * par[CK : CK + 1, :]).astype(BF16)
        cr_s[r, :] = (prev + d * par[CR : CR + 1, :]).astype(BF16)
        for cp in ship(outs_d, 10, i):
            cp.start()
        return carry

    lax.fori_loop(0, L.nblk - 1, phase_d, 0)
    n_edge.wait()
    npad[0:8, :] = nedge[...] * keep
    edge_o[8:16, :] = nedge[...] * keep
    phase_d(L.nblk - 1, 0)

    for cp in keys.link(L.bits - 1):
        cp.wait_recv()
    for cp in keys.across(L.bits - 1):
        cp.start()
    for t in range(L.bits):
        for cp in keys.link(t):
            cp.wait_send()
        for cp in keys.across(t):
            cp.wait()
    for cp in values.link(0):
        cp.wait_send()
    for cp in values.across(0):
        cp.wait()

    def drain(i, carry):
        for outs, base in ((outs_a, 0), (outs_c, 6), (outs_d, 10)):
            for cp in ship(outs, base, i):
                cp.wait()
        return carry

    lax.fori_loop(0, L.nblk, drain, 0)


def front(L, tok, vecs, wk, wv, wr, wo, kshard, vshard):
    R, D, n_f, U = L.R, L.D, L.n_f, L.U
    _, flat = gather_steps(L)
    rb, rf = sds((R, D), BF16), sds((R, D))
    dma = pltpu.SemaphoreType.DMA
    return pl.pallas_call(
        functools.partial(front_kernel, L),
        out_shape=(rb,) * 6 + (rf,) * 4 + (rb, rf) + (sds((16, D)), sds((16, D)), sds((n_f, D, U), BF16), sds((n_f, U, D), BF16)),
        in_specs=[ANY] + [VMEM] * NVEC + [ANY] * 6,
        out_specs=(ANY,) * 12 + (VMEM, VMEM, ANY, ANY),
        scratch_shapes=[
            pltpu.VMEM((R, D), BF16), pltpu.VMEM((4, D, D), BF16), pltpu.VMEM((R + 8, D), F32),
            *([pltpu.VMEM((R, D), BF16)] * 6), *([pltpu.VMEM((R, D), F32)] * 6), pltpu.VMEM((R, D), BF16),
            pltpu.VMEM((SPAN, D), F32), pltpu.VMEM((SPAN, D), F32), pltpu.VMEM((SPAN, 2 * SPAN), BF16),
            pltpu.VMEM((L.nspan, 8, D), F32), pltpu.VMEM((8, D), F32), pltpu.VMEM((n_f, 8, D), F32),
            pltpu.VMEM((16, D), BF16), pltpu.VMEM((8, D), F32), pltpu.VMEM((8, D), F32),
            dma((5,)), dma((12, L.nblk)), dma((2,)), dma((2,)), dma((n_f,)), dma((n_f,)),
            dma((2, flat)), dma((2, flat)), dma((2, flat)), dma((2, flat)),
        ],
        compiler_params=pltpu.CompilerParams(collective_id=0, has_side_effects=True, vmem_limit_bytes=VLIMIT),
        cost_estimate=pl.CostEstimate(flops=10 * R * D * D, bytes_accessed=40 * R * D, transcendentals=4 * R * D),
        name="front",
    )(tok, *vecs, wk, wv, wr, wo, kshard, vshard)


def squeeze(mask, bit):
    return ((mask >> (bit + 1)) << bit) | (mask & ((1 << bit) - 1))


def middle_kernel(
    L, lens, ck, cr, x1, og, kall, vall, kshard, vshard, wc,
    mixed_o, g2_o, gck_o, gcr_o, big_o, dc_o,
    kv, vv, wcv, ck_s, cr_s, x1_s, gate_s, og_s, mix_s, gv_s, gg_s, ckt_s, gvt_s, h_s, p_s, dk_s, dv_s, dc_s, inc, r0,
    in_sem, w_sem, out_sem, g_sem, x_ssem, x_rsem, h_ssem, h_rsem, g_ssem, g_rsem, c_ssem, c_rsem,
):
    BR, n_f, D, U = 2 * L.BR, L.n_f, L.D, L.U
    nblk, tile = L.R // BR, L.BR
    dp, me = lax.axis_index("dp"), lax.axis_index("ffn")
    core = dp % 2
    buddy = dp + 1 - 2 * core
    half = D // 2
    hk = half // L.parts
    length = lens[me // L.per_slot]
    start = (me % L.per_slot) * L.R
    masks = sorted(range(n_f), key=lambda m: (-bin(m).count("1"), m))

    def fetch(n, src, dst):
        return pltpu.make_async_copy(src, dst, w_sem.at[n])

    k_cp = [fetch(m, kall.at[m] if m else kshard, kv.at[m]) for m in range(n_f)]
    v_cp = [fetch(n_f, vshard, vv.at[0])]
    uh = U // 2
    for p in range(L.parts):
        m = 1 << L.order(p)[0]
        for c in range(2):
            r = pl.ds(c * uh + p * (uh // L.parts), uh // L.parts)
            v_cp.append(fetch(n_f + 1 + 2 * p + c, vall.at[m, r], vv.at[m, r]))
    pairs = ((ck, ck_s), (cr, cr_s), (wc, wcv), (x1, x1_s), (og, og_s))
    ins = [pltpu.make_async_copy(s, d, in_sem.at[n]) for n, (s, d) in enumerate(pairs)]
    for cp in [ins[0]] + k_cp:
        cp.start()

    greet([(buddy, me)] + [(dp, flip(me, b)) for b in range(L.bits)])

    first = [1 << L.order(p)[0] for p in range(L.parts)]
    values = Gather(
        L, core, dp, me, uh,
        lambda m, r: vshard.at[r] if m == 0 else (vall.at[m, r] if m in first else vv.at[m, r]),
        lambda m, r: vv.at[m, r],
        (g_ssem, g_rsem, c_ssem, c_rsem),
    )
    if L.bits > 1:
        for cp in values.link(1):
            cp.start()
    for cp in [ins[0]] + k_cp:
        cp.wait()
    for cp in ins[1:3] + v_cp + ins[3:]:
        cp.start()

    def keys_block(i, carry):
        r = rows_of(i, BR)
        ck_i = ck_s[r, :]
        for m in range(n_f):
            p = jnp.maximum(dot(ck_i, kv[m]), 0.0)
            p_s[m, r, :] = p.astype(BF16)
            h_s[m, r, :] = (p * p).astype(BF16)
        ckt_s[:, pl.ds(pl.multiple_of(i * BR, 128), BR)] = ck_i.T
        return carry

    lax.fori_loop(0, nblk, keys_block, 0)
    for cp in ins[1:3]:
        cp.wait()

    def gate_block(i, carry):
        r = rows_of(i, BR)
        gate_s[r, :] = sigmoid(dot(cr_s[r, :], wcv[...]))
        return carry

    lax.fori_loop(0, nblk, gate_block, 0)
    for cp in v_cp + ins[3:]:
        cp.wait()
    for t in range(1, L.bits):
        for cp in values.link(t):
            cp.wait_recv()
        for cp in values.across(t):
            cp.start()
        if t + 1 < L.bits:
            for cp in values.link(t + 1):
                cp.start()
    for t in range(1, L.bits):
        for cp in values.across(t):
            cp.wait_recv()

    def ship(i):
        r = rows_of(i, BR)
        both = ((mix_s, mixed_o), (og_s, g2_o), (ck_s, gck_o), (cr_s, gcr_o))
        return [pltpu.make_async_copy(s.at[r], d.at[r], out_sem.at[n, i]) for n, (s, d) in enumerate(both)]

    def values_block(i, carry):
        r = rows_of(i, BR)
        vsum = jnp.zeros((BR, D), F32)
        for m in range(n_f):
            vsum = vsum + dot(h_s[m, r, :], vv[m])
        pos = start + i * BR + lax.broadcasted_iota(jnp.int32, (BR, 1), 0)
        live = jnp.where(pos < length, 1.0, 0.0).astype(F32)
        gate_i = gate_s[r, :]
        mix_s[r, :] = ((x1_s[r, :] + gate_i * vsum) * live).astype(BF16)
        g2 = og_s[r, :].astype(F32) * live
        og_s[r, :] = g2.astype(BF16)
        gv32 = g2 * gate_i
        gv = gv32.astype(BF16)
        gv_s[r, :] = gv
        gg_s[r, :] = (gv32 * vsum * (1.0 - gate_i)).astype(BF16)
        gvt_s[:, pl.ds(pl.multiple_of(i * BR, 128), BR)] = gv.T
        for cp in ship(i)[:2]:
            cp.start()
        return carry

    lax.fori_loop(0, nblk, values_block, 0)

    own = pl.ds(pl.multiple_of(core * half, 16), half)
    away = pl.ds(pl.multiple_of((1 - core) * half, 16), half)

    def swaps(m):
        return [
            remote(g.at[m, away], inc.at[n, m], x_ssem.at[n, m], x_rsem.at[n, m], (buddy, me))
            for n, g in enumerate((dk_s, dv_s))
        ]

    def part_rows(p):
        return pl.ds(pl.multiple_of(core * half + p * hk, 16), hk)

    def halves(m):
        out = []
        for p in range(L.parts):
            bit = L.order(p)[0]
            if (m >> bit) & 1:
                k = squeeze(m, bit)
                for n, g in enumerate((dk_s, dv_s)):
                    out.append(
                        remote(g.at[m, part_rows(p)], r0.at[n, p, k], h_ssem.at[n, p, k], h_rsem.at[n, p, k],
                               (dp, flip(me, bit)))
                    )
        return out

    def merge(n, m):
        swaps(m)[n].wait_recv()
        g = (dk_s, dv_s)[n]
        g[m, own, :] = (g[m, own, :].astype(F32) + inc[n, m].astype(F32)).astype(BF16)
        for cp in halves(m)[n::2]:
            cp.start()

    def weight_grad(n, m):
        left, right, g = ((ckt_s, p_s, dk_s), (gvt_s, h_s, dv_s))[n]
        for c in range(D // tile):
            rr = slice(c * tile, (c + 1) * tile)
            g[m, rr, :] = dot(left[rr, :], right[m]).astype(BF16)
        swaps(m)[n].start()

    for n, m in enumerate(masks):
        weight_grad(1, m)
        if n > 0:
            merge(1, masks[n - 1])

    for n, m in enumerate(masks):
        def block(i, carry, m=m, n=n):
            r = rows_of(i, BR)
            gk = (dot(gv_s[r, :], vv[m], 1, 1) * (2.0 * p_s[m, r, :].astype(F32))).astype(BF16)
            p_s[m, r, :] = gk
            part = dot(gk, kv[m], 1, 1)
            total = part if n == 0 else x1_s[r, :] + part
            if n + 1 < n_f:
                x1_s[r, :] = total
            else:
                ck_s[r, :] = total.astype(BF16)
                ship(i)[2].start()
            return carry

        lax.fori_loop(0, nblk, block, 0)
        merge(0, masks[n - 1]) if n > 0 else merge(1, masks[-1])
        weight_grad(0, m)

    for c in range(D // tile):
        rr = slice(c * tile, (c + 1) * tile)
        dc_s[rr, :] = dot(cr_s[:, rr], gg_s[...], 0, 0).astype(BF16)
    merge(0, masks[-1])

    def last_block(i, carry):
        r = rows_of(i, BR)
        cr_s[r, :] = dot(gg_s[r, :], wcv[...], 1, 1).astype(BF16)
        ship(i)[3].start()
        return carry

    lax.fori_loop(0, nblk, last_block, 0)
    last = pltpu.make_async_copy(dc_s, dc_o, in_sem.at[0])
    last.start()

    outs = []
    for m in masks:
        for cp in halves(m):
            cp.wait_recv()
    for p in range(L.parts):
        bit = L.order(p)[0]
        for m in range(n_f):
            if (m >> bit) & 1:
                continue
            k = squeeze(m, bit)
            for n, g in enumerate((dk_s, dv_s)):
                r = part_rows(p)
                r0[n, p, k] = (g[m, r, :].astype(F32) + r0[n, p, k].astype(F32)).astype(BF16)
                outs.append(pltpu.make_async_copy(r0.at[n, p, k], big_o.at[n, p, k], g_sem.at[n, p, k]))
                outs[-1].start()
    for m in masks:
        for cp in halves(m) + swaps(m):
            cp.wait_send()
    for t in range(1, L.bits):
        for cp in values.link(t) + values.across(t):
            cp.wait_send()
    for i in range(nblk):
        for cp in ship(i):
            cp.wait()
    for cp in outs + [last]:
        cp.wait()


def middle(L, lens, ck, cr, x1, og, kall, vall, kshard, vshard, wc):
    R, D, n_f, U = L.R, L.D, L.n_f, L.U
    dma = pltpu.SemaphoreType.DMA
    rb = sds((R, D), BF16)
    vb, vf = pltpu.VMEM((R, D), BF16), pltpu.VMEM((R, D), F32)
    hid = pltpu.VMEM((n_f, R, U), BF16)
    kept = (2, L.parts, n_f // 2, D // 2 // L.parts, U)
    _, flat = gather_steps(L)
    sem3 = dma(kept[:3])
    return pl.pallas_call(
        functools.partial(middle_kernel, L),
        out_shape=(rb, rb, rb, rb, sds(kept, BF16), sds((D, D), BF16)),
        in_specs=[SMEM] + [ANY] * 9,
        out_specs=(ANY,) * 6,
        scratch_shapes=[
            pltpu.VMEM((n_f, D, U), BF16), pltpu.VMEM((n_f, U, D), BF16), pltpu.VMEM((D, D), BF16),
            vb, vb, vf, vf, vb, vb, vb, vb, pltpu.VMEM((D, R), BF16), pltpu.VMEM((D, R), BF16), hid, hid,
            pltpu.VMEM((n_f, D, U), BF16), pltpu.VMEM((n_f, D, U), BF16), pltpu.VMEM((D, D), BF16),
            pltpu.VMEM((2, n_f, D // 2, U), BF16), pltpu.VMEM(kept, BF16),
            dma((6,)), dma((n_f + 1 + 2 * L.parts,)), dma((4, L.nblk)), sem3, dma((2, n_f)), dma((2, n_f)),
            sem3, sem3, dma((flat,)), dma((flat,)), dma((flat,)), dma((flat,)),
        ],
        compiler_params=pltpu.CompilerParams(collective_id=1, has_side_effects=True, vmem_limit_bytes=VLIMIT),
        cost_estimate=pl.CostEstimate(flops=52 * R * D * D, bytes_accessed=60 * R * D, transcendentals=0),
        name="middle",
    )(lens, ck, cr, x1, og, kall, vall, kshard, vshard, wc)


class Pool:
    def __init__(self, ssem, rsem):
        self.ssem, self.rsem, self.n = ssem, rsem, 0

    def copy(self, src, dst, dev):
        k = self.n
        self.n = k + 1
        return remote(src, dst, self.ssem.at[k], self.rsem.at[k], dev)


def begin(copies):
    for cp in copies:
        cp.start()
    return copies


def landed(copies):
    for cp in copies:
        cp.wait_recv()


class Unit:
    def __init__(self, env, order, rows, done, acc, rbuf, zbuf, final, source=None, swap=None, gather=False):
        self.env, self.rows, self.acc, self.rbuf, self.zbuf, self.final = env, rows, acc, rbuf, zbuf, final
        self.source = source
        self.order = order
        self.sent, self.pending, self.now = [], None, []
        self.off, self.size, self.zoff, self.split, self.slot = 0, rows, 0, [], 0
        steps = [swap] if swap else []
        steps += [functools.partial(self.halve, t) for t in range(done, len(order))]
        steps += [functools.partial(self.halve_z, b) for b in range(env.zbits)]
        steps += [self.home]
        if gather:
            steps += [functools.partial(self.double, t) for t in range(len(order))]
        steps += [self.cross]
        self.steps = steps

    def keep(self, copies):
        self.sent += copies
        self.now = begin(copies)

    def advance(self):
        landed(self.now)
        self.now = []
        if self.pending:
            self.pending()
            self.pending = None
        if not self.steps:
            return False
        self.steps.pop(0)()
        return True

    def halve(self, t):
        e, bit = self.env, self.order[t]
        masks = spans(self.order[t + 1 :])
        base, src = self.slot, self.source or self.acc
        self.slot += len(masks)
        self.source = None
        self.keep([
            e.pool.copy(src(m | (1 << bit)), self.rbuf(base + n), (e.dp, flip(e.me, bit))) for n, m in enumerate(masks)
        ])

        def end():
            for n, m in enumerate(masks):
                view = self.acc(m)
                view[...] = (view[...].astype(F32) + self.rbuf(base + n)[...].astype(F32)).astype(BF16)

        self.pending = end

    def part(self, off, size):
        return pl.ds(pl.multiple_of(off, 16), size)

    def halve_z(self, b):
        e, mine = self.env, (self.env.zi // (1 << b)) % 2
        split = (self.size // 2) % 16 == 0
        size = self.size // 2 if split else self.size
        kept = self.off + (mine * size if split else 0)
        sent = self.off + ((1 - mine) * size if split else 0)
        buf = self.zbuf(pl.ds(self.zoff, size))
        self.zoff += size
        peer = (flip(e.zi, b) * 2 + e.core, e.me)
        self.keep([e.pool.copy(self.acc(0).at[self.part(sent, size)], buf, peer)])
        if split:
            self.split.append((b, self.off, self.size))
        self.off, self.size = kept, size

        def end():
            if not split:
                self.sent.pop().wait_send()
            view = self.acc(0).at[self.part(kept, size)]
            view[...] = (view[...].astype(F32) + buf[...].astype(F32)).astype(BF16)

        self.pending = end

    def home(self):
        e = self.env
        here = self.acc(0).at[self.part(self.off, self.size)]
        self.local = pltpu.make_async_copy(here, self.final(0, self.off, self.size), e.lsem.at[e.nl])
        e.nl += 1
        self.local.start()
        self.steps = [functools.partial(self.double_z, n) for n in reversed(range(len(self.split)))] + self.steps
        self.first = here
        if self.split:
            self.steps.pop(0)()
        else:
            self.pending = self.local.wait

    def double_z(self, n):
        e = self.env
        b, off, size = self.split[n]
        src = self.final(0, self.off, self.size) if self.first is None else self.first
        self.keep([e.pool.copy(src, self.final(0, self.off, self.size), (flip(e.zi, b) * 2 + e.core, e.me))])
        if self.first is not None:
            self.first = None
            self.pending = self.local.wait
        self.off, self.size = off, size

    def double(self, t):
        e, o = self.env, self.order
        out = []
        for m in spans(o[:t]):
            v = self.final(m, 0, self.rows)
            out.append(e.pool.copy(v, v, (e.dp, flip(e.me, o[t]))))
        self.keep(out)

    def cross(self):
        e = self.env
        v = self.final(None, 0, self.rows)
        self.keep([e.pool.copy(v, v, (e.dp + 1 - 2 * e.core, e.me))])


class Env:
    pass


KEY, VALUE, RECEPT, OUT, CMR = range(5)
FLIPPED = (OUT, VALUE)
HOOKS = {
    "1a": "M",
    "1b": "",
    "out": "ac",
    "rec": "",
    "key": "ORMbd",
    "value": "",
    "3a": "",
    "3b": "KVRMab",
    "4a": "O",
    "4b": "",
    "tail": "McdRKOMVWRKVOMRKOWabVRMKOMRVcOKdRVaKbOMV",
    "end": "KcdMabROabVcdRKOcdKVV",
}
V_LN1G, V_LN1B, V_TD, V_TF, V_MK, V_MV, V_MR, V_LN2G, V_LN2B, V_CMK, V_CMR = range(11)


def back_kernel(
    L, tok, par, edge, g2, gck, gcr, x1, y, sr, wkv, rd, a, v, xk, xv, xr, wk, wv, wr, wo, bigh, dch,
    ig_o, dkr, dvr, rep, vec_o,
    gkb_s, grb_s, srb_s, gck_s, gcr_s, x1_s, a_s, wkv_s, rd_s, v_s, g2_s, y_s, xr_s, gr_s, gk_s, gv_s, w3, dw, acc1,
    inc, r1, r2, z1, z2, grow, fade, tri, ent, st_out, st_in, carry, gpad, tpad, vacc, vown, vf, vd, dev_in,
    blk_sem, in_sem, out_sem, e_ssem, e_rsem, s_ssem, s_rsem, v_ssem, v_rsem, lsem, p_ssem, p_rsem,
):
    D, BR, n_f, n_dp, U, R = L.D, L.BR, L.n_f, L.n_dp, L.U, L.R
    dp, me = lax.axis_index("dp"), lax.axis_index("ffn")
    core = dp % 2
    buddy = dp + 1 - 2 * core
    place = me % L.per_slot
    opens = jnp.where(place == 0, 0.0, 1.0).astype(F32)
    stays = jnp.where(place == L.per_slot - 1, 0.0, 1.0).astype(F32)
    half = D // 2

    blocks = ((gck, gkb_s), (gcr, grb_s), (x1, x1_s), (g2, g2_s), (sr, srb_s), (wkv, wkv_s), (rd, rd_s))

    def load(i, which):
        r = rows_of(i, BR)
        return [pltpu.make_async_copy(blocks[n][0].at[r], blocks[n][1].at[r], blk_sem.at[n, i]) for n in which]

    wo_cp = pltpu.make_async_copy(wo, w3.at[2], in_sem.at[0])
    begin(load(0, range(7)) + [wo_cp])
    for i in range(1, L.nblk):
        begin(load(i, range(7)))
    acc_cp = pltpu.make_async_copy(bigh, acc1, in_sem.at[1])
    y_cp = pltpu.make_async_copy(y, y_s, in_sem.at[3])
    xr_cp = pltpu.make_async_copy(xr, xr_s, in_sem.at[4])
    v_cp = pltpu.make_async_copy(v, v_s, in_sem.at[5])
    a_cp = pltpu.make_async_copy(a, a_s, in_sem.at[11])
    dc_cps = [
        pltpu.make_async_copy(dch.at[:, pl.ds(h * half, half)], dw.at[CMR, h], in_sem.at[6 + h]) for h in range(2)
    ]
    w_cps = [pltpu.make_async_copy(w, w3.at[n], in_sem.at[8 + n]) for n, w in enumerate((wk, wv))]
    begin(dc_cps)

    greet(
        [(dp, (me + k) % n_f) for k in range(1, n_f)] + [((dp + k) % n_dp, me) for k in range(1, n_dp)]
    )

    prv = (me + n_f - 1) % n_f
    edges = begin([
        remote(g.at[pl.ds(0, 16)], gpad.at[n], e_ssem.at[n], e_rsem.at[n], (dp, prv)) for n, g in enumerate((gck, gcr))
    ])

    e = Env()
    e.me, e.dp, e.core, e.zi, e.zbits = me, dp, core, dp // 2, L.nz.bit_length() - 1
    e.pool, e.lsem, e.nl = Pool(p_ssem, p_rsem), lsem, 0

    hk = half // L.parts
    big = []
    for n, res in enumerate((dkr, dvr)):
        for p in range(L.parts):
            o, off = L.order(p), p * hk

            def acc(m, n=n, p=p, o=o):
                return acc1.at[n, p, squeeze(m, o[0])]

            def source(m, n=n, p=p, o=o):
                return bigh.at[n, p, squeeze(m, o[0])]

            def rbuf(k, n=n, p=p):
                return r1.at[n, p, k]

            def zbuf(r, n=n, p=p):
                return z1.at[n, p, r]

            def final(m, r0, size, res=res, off=off):
                return res.at[pl.ds(pl.multiple_of(core * half + off + r0, 16), size)]

            big.append(Unit(e, o, hk, 1, acc, rbuf, zbuf, final, source))
    shard = D // n_f
    small = []
    for m_ in range(5):
        def acc(m, i=m_):
            return dw.at[i, core, pl.ds(pl.multiple_of(flips(me, m) * shard, 16), shard)]

        def rbuf(k, i=m_):
            return r2.at[i, k]

        def zbuf(r, i=m_):
            return z2.at[i, r]

        def final(m, r0, size, i=m_):
            cols = pl.ds(pl.multiple_of(core * half, 128), half)
            if m is None:
                return rep.at[i, :, cols]
            return rep.at[i, pl.ds(pl.multiple_of(flips(me, m) * shard + r0, 16), size), cols]

        def swap(i=m_):
            u = small[i]
            u.keep([e.pool.copy(dw.at[i, 1 - core], inc.at[i], (buddy, me))])

            def end():
                dw[i, core] = (dw[i, core].astype(F32) + inc[i].astype(F32)).astype(BF16)

            u.pending = end

        o = L.order(1) if m_ in FLIPPED else L.order(0)
        small.append(Unit(e, o, shard, 0, acc, rbuf, zbuf, final, None, swap, True))
    units = dict(zip("MORKV", (small[CMR], small[OUT], small[RECEPT], small[KEY], small[VALUE])))
    units.update(zip("abcd" if L.parts == 2 else "ac", big))

    class Vectors:
        def __init__(self):
            self.stage = 0

        def advance(self):
            self.stage += 1
            if self.stage == 1:
                vown[...] = jnp.sum(vacc[...], axis=1)
                vf[0] = vown[...]
                self.now = begin([
                    remote(vown, vf.at[k], v_ssem.at[0, k], v_rsem.at[0, k], (dp, (me + k) % n_f))
                    for k in range(1, n_f)
                ])
            elif self.stage == 2:
                for cp in self.now:
                    cp.wait()
                total = vf[me % n_f]
                for f in range(1, n_f):
                    total = total + vf[(me - f + n_f) % n_f]
                vd[0] = total
                self.now = begin([
                    remote(vd.at[0], vd.at[k], v_ssem.at[1, k], v_rsem.at[1, k], ((dp + k) % n_dp, me))
                    for k in range(1, n_dp)
                ])
            elif self.stage == 3:
                for cp in self.now:
                    cp.wait()
                total = vd[dp % n_dp]
                for f in range(1, n_dp):
                    total = total + vd[(dp - f + n_dp) % n_dp]
                vec_o[...] = total
                vec_o[V_TD : V_TD + 1, :] = w * (total[V_TD : V_TD + 1] - total[V_TF : V_TF + 1])
            return self.stage < 3

    units["W"] = Vectors()

    def go(names):
        for name in names:
            if name in units:
                units[name].advance()

    go("abcd")

    w = jnp.exp(par[TD : TD + 1, :])
    ew = jnp.exp(w)
    eu = jnp.exp(par[TF : TF + 1, :])
    age = lax.broadcasted_iota(jnp.int32, (SPAN, D), 0).astype(F32) * w
    grow[...] = jnp.exp(age)
    fade[...] = jnp.exp(-age)
    tri[...] = tri_pair(False)
    full_fade = jnp.exp(-float(SPAN) * w)
    tail_fade = jnp.exp(-float(SPAN - 1) * w)
    vacc[...] = jnp.zeros_like(vacc)
    carry[...] = edge[8:16, :]

    def add_up(n, x):
        vacc[n] = vacc[n] + jnp.sum(x.reshape(-1, 8, D), axis=0)

    for cp in dc_cps:
        cp.wait()
    go("M")
    wo_cp.wait()
    for cp in load(0, (0, 1)):
        cp.wait()

    def phase_1(i, _):
        @pl.when(i + 1 < L.nblk)
        def _wait():
            for cp in load(i + 1, (0, 1)):
                cp.wait()

        for cp in load(i, range(2, 7)):
            cp.wait()
        r = rows_of(i, BR)
        win = pl.ds(pl.multiple_of(i * BR, 16), BR + 16)
        mk, mr = par[CK : CK + 1, :], par[CR : CR + 1, :]
        gk = gkb_s[win, :].astype(F32)
        gr = grb_s[win, :].astype(F32)
        t = gk * (1.0 - mk) + gr * (1.0 - mr)
        t = pltpu.roll(t, BR + 15, 0)[:BR]
        gk, gr = gk[:BR], gr[:BR]
        gn = gk * mk + gr * mr + t
        n2, rs = normed(x1_s[r, :])
        norm2 = n2 * par[G2 : G2 + 1, :] + par[B2 : B2 + 1, :]
        prev = pltpu.roll(jnp.concatenate([carry[...], norm2], axis=0), 1, 0)[8:]
        carry[...] = norm2[BR - 8 :]
        d = norm2 - prev
        add_up(V_CMK, gk * d)
        add_up(V_CMR, gr * d)
        add_up(V_LN2G, gn * n2)
        add_up(V_LN2B, gn)
        q1 = gn * par[G2 : G2 + 1, :]
        m1 = jnp.mean(q1, axis=-1, keepdims=True)
        m2 = jnp.mean(q1 * n2, axis=-1, keepdims=True)
        g1 = g2_s[r, :].astype(F32) + (q1 - m1 - n2 * m2) * rs
        x1_s[r, :] = g1
        ga = g1.astype(BF16)
        g2_s[r, :] = ga
        s = srb_s[r, :].astype(F32)
        gys = dot(ga, w3[2], 1, 1) * s
        wk_ = wkv_s[r, :]
        gr_s[r, :] = (gys * wk_ * (1.0 - s)).astype(BF16)
        q = gys * rd_s[r, :]
        qw = q * wk_
        rd_s[r, :] = q
        wkv_s[r, :] = qw
        for sb in range(BR // SPAN):
            b = i * (BR // SPAN) + sb
            rb = rows_of(b, SPAN)
            sl = slice(sb * SPAN, (sb + 1) * SPAN)
            fd = fade[...]
            both = jnp.concatenate([fd * q[sl], fd * qw[sl]], axis=1)
            suf = dot(tri[...], split2(both))
            gs = grow[...] * ew
            gck_s[rb, :] = gs * suf[:, :D]
            gcr_s[rb, :] = gs * suf[:, D:]
            tot = suf[0:1] + both[0:1]
            ent[b, 0:1, :] = tot[:, :D]
            ent[b, 1:2, :] = tot[:, D:]
        return 0

    cut = L.nblk // 2
    lax.fori_loop(0, cut, phase_1, 0)
    begin([acc_cp, y_cp, xr_cp, a_cp, v_cp] + w_cps)
    go(HOOKS["1a"])
    lax.fori_loop(cut, L.nblk - 1, phase_1, 0)
    for cp in edges:
        cp.wait()
    gkb_s[R : R + 16, :] = (gpad[0].astype(F32) * stays).astype(BF16)
    grb_s[R : R + 16, :] = (gpad[1].astype(F32) * stays).astype(BF16)
    phase_1(L.nblk - 1, 0)

    acc_cp.wait()
    go(HOOKS["1b"])
    xq = jnp.zeros((1, D), F32)
    xw = jnp.zeros((1, D), F32)
    for b in reversed(range(L.nspan)):
        tq, tw = ent[b, 0:1, :], ent[b, 1:2, :]
        ent[b, 0:1, :] = xq
        ent[b, 1:2, :] = xw
        xq = tq + full_fade * xq
        xw = tw + full_fade * xw
    st_out[...] = jnp.zeros_like(st_out)
    st_out[0:1, :] = xq
    st_out[1:2, :] = xw
    states = begin([
        remote(st_out, st_in.at[k], s_ssem.at[k], s_rsem.at[k], (dp, (me + n_f - k) % n_f)) for k in range(1, n_f)
    ])
    w_cps.append(pltpu.make_async_copy(wr, w3.at[2], in_sem.at[10]))
    w_cps[-1].start()

    def product(m, left, right):
        for c in range(D // BR):
            rr = slice(c * BR, (c + 1) * BR)
            full = dot(left[:, rr], right[...], 0, 0).astype(BF16)
            dw[m, 0, rr, :] = full[:, :half]
            dw[m, 1, rr, :] = full[:, half:]

    y_cp.wait()
    product(OUT, y_s, g2_s)
    xk_cp = pltpu.make_async_copy(xk, y_s, in_sem.at[12])
    xv_cp = pltpu.make_async_copy(xv, g2_s, in_sem.at[14])
    begin([xk_cp, xv_cp])
    go("O" + HOOKS["out"])
    xr_cp.wait()
    product(RECEPT, xr_s, gr_s)
    go("R" + HOOKS["rec"])

    for cp in states:
        cp.wait()
    qi = jnp.zeros((1, D), F32)
    wi = jnp.zeros((1, D), F32)
    for k in range(1, L.per_slot):
        f = jnp.exp(-float((k - 1) * R) * w) * jnp.where(place + k < L.per_slot, 1.0, 0.0).astype(F32)
        qi = qi + f * st_in[k, 0:1, :]
        wi = wi + f * st_in[k, 1:2, :]
    dev_in[0:1, :] = qi
    dev_in[1:2, :] = wi
    a_cp.wait()
    v_cp.wait()
    first = place * R - (L.per_slot * R) // 2

    def phase_2(b, _):
        rb = rows_of(b, SPAN)
        fb = jnp.exp(w * ((b + 1 - L.nspan) * SPAN).astype(F32))
        eq = ent[b, 0:1, :] + fb * dev_in[0:1, :]
        ewk = ent[b, 1:2, :] + fb * dev_in[1:2, :]
        ff = grow[...] * tail_fade
        q, qw, av, vv = rd_s[rb, :], wkv_s[rb, :], a_s[rb, :], v_s[rb, :]
        gvr = av * (eu * q + gck_s[rb, :] + ff * eq)
        gkr = vv * gvr - av * (eu * qw + gcr_s[rb, :] + ff * ewk)
        gk_s[rb, :] = gkr.astype(BF16)
        gv_s[rb, :] = gvr.astype(BF16)
        add_up(V_TF, eu * av * (q * vv - qw))
        pos = (first + b * SPAN + lax.broadcasted_iota(jnp.int32, (SPAN, 1), 0)).astype(F32)
        add_up(V_TD, pos * gkr)
        return 0

    lax.fori_loop(0, L.nspan, phase_2, 0)
    xk_cp.wait()
    product(KEY, y_s, gk_s)
    tok_cp = pltpu.make_async_copy(tok, y_s, in_sem.at[13])
    tok_cp.start()
    go("K" + HOOKS["key"])
    xv_cp.wait()
    product(VALUE, g2_s, gv_s)
    go("V" + HOOKS["value"])

    for cp in w_cps:
        cp.wait()
    tok_cp.wait()
    carry[...] = edge[0:8, :]

    def phase_3(i, _):
        r = rows_of(i, BR)
        mk, mv, mr = par[MK : MK + 1, :], par[MV : MV + 1, :], par[MR : MR + 1, :]
        n1_, _rs = normed(y_s[r, :].astype(F32))
        norm1 = n1_ * par[G1 : G1 + 1, :] + par[B1 : B1 + 1, :]
        prev = pltpu.roll(jnp.concatenate([carry[...], norm1], axis=0), 1, 0)[8:]
        carry[...] = norm1[BR - 8 :]
        d = norm1 - prev
        gxk = dot(gk_s[r, :], w3[0], 1, 1)
        gxv = dot(gv_s[r, :], w3[1], 1, 1)
        gxr = dot(gr_s[r, :], w3[2], 1, 1)
        add_up(V_MK, gxk * d)
        add_up(V_MV, gxv * d)
        add_up(V_MR, gxr * d)
        now = gxk * mk + gxv * mv + gxr * mr
        gck_s[r, :] = gxk + gxv + gxr - now
        gcr_s[r, :] = now
        return 0

    lax.fori_loop(0, cut, phase_3, 0)
    t_cp = remote(gck_s.at[pl.ds(0, 8)], tpad, e_ssem.at[2], e_rsem.at[2], (dp, prv))
    t_cp.start()
    go(HOOKS["3a"])
    lax.fori_loop(cut, L.nblk, phase_3, 0)
    go(HOOKS["3b"])
    t_cp.wait()
    gck_s[R : R + 8, :] = tpad[...] * stays

    def phase_4(i, _):
        r = rows_of(i, BR)
        t = gck_s[pl.ds(pl.multiple_of(i * BR, 8), BR + 8), :]
        gn = gcr_s[r, :] + pltpu.roll(t, BR + 7, 0)[:BR]
        n1_, rs = normed(y_s[r, :].astype(F32))
        add_up(V_LN1G, gn * n1_)
        add_up(V_LN1B, gn)
        q1 = gn * par[G1 : G1 + 1, :]
        m1 = jnp.mean(q1, axis=-1, keepdims=True)
        m2 = jnp.mean(q1 * n1_, axis=-1, keepdims=True)
        y_s[r, :] = (x1_s[r, :] + (q1 - m1 - n1_ * m2) * rs).astype(BF16)
        pltpu.make_async_copy(y_s.at[r], ig_o.at[r], out_sem.at[i]).start()
        return 0

    lax.fori_loop(0, cut, phase_4, 0)
    go(HOOKS["4a"])
    lax.fori_loop(cut, L.nblk, phase_4, 0)
    go("W" + HOOKS["4b"])
    go(HOOKS["tail"])
    go(HOOKS["end"])
    live = [u for u in units.values()]
    while live:
        live = [u for u in live if u.advance()]
    for u in big + small:
        for cp in u.sent:
            cp.wait_send()
    for i in range(L.nblk):
        pltpu.make_async_copy(y_s.at[rows_of(i, BR)], ig_o.at[rows_of(i, BR)], out_sem.at[i]).wait()


def back(L, *args):
    R, D, n_f, n_dp, U = L.R, L.D, L.n_f, L.n_dp, L.U
    half, shard = D // 2, D // L.n_f
    hk = half // L.parts
    dma = pltpu.SemaphoreType.DMA
    bpad, fpad, full, low = pltpu.VMEM((R + 16, D), BF16), pltpu.VMEM((R + 8, D), F32), pltpu.VMEM((R, D), F32), pltpu.VMEM((R, D), BF16)
    rows8 = pltpu.VMEM((8, D), F32)
    zbits = L.nz.bit_length() - 1

    def z_rows(rows):
        total = 0
        for _ in range(zbits):
            rows = rows // 2 if (rows // 2) % 16 == 0 else rows
            total += rows
        return total

    n_r = n_f - 1
    n_pool = 2 * L.parts * (n_r + 2 * zbits + 1) + 5 * (2 * n_r + 2 * zbits + 2)
    return pl.pallas_call(
        functools.partial(back_kernel, L),
        out_shape=(
            sds((R, D), BF16), sds((D, U), BF16), sds((D, U), BF16), sds((5, D, D), BF16), sds((16, D)),
        ),
        in_specs=[ANY, VMEM, VMEM] + [ANY] * 19,
        out_specs=(ANY, ANY, ANY, ANY, VMEM),
        scratch_shapes=[
            bpad, bpad, low, fpad, full, full, full, full, full, full, low, low, low, low, low, low,
            pltpu.VMEM((3, D, D), BF16), pltpu.VMEM((5, 2, D, half), BF16), pltpu.VMEM((2, L.parts, n_f // 2, hk, U), BF16),
            pltpu.VMEM((5, D, half), BF16), pltpu.VMEM((2, L.parts, max(n_f // 2 - 1, 1), hk, U), BF16),
            pltpu.VMEM((5, n_r, shard, half), BF16), pltpu.VMEM((2, L.parts, z_rows(hk), U), BF16),
            pltpu.VMEM((5, z_rows(shard), half), BF16),
            pltpu.VMEM((SPAN, D), F32), pltpu.VMEM((SPAN, D), F32), pltpu.VMEM((SPAN, 2 * SPAN), BF16),
            pltpu.VMEM((L.nspan, 8, D), F32), rows8, pltpu.VMEM((n_f, 8, D), F32), rows8,
            pltpu.VMEM((2, 16, D), BF16), rows8, pltpu.VMEM((16, 8, D), F32), pltpu.VMEM((16, D), F32),
            pltpu.VMEM((n_f, 16, D), F32), pltpu.VMEM((n_dp, 16, D), F32), rows8,
            dma((7, L.nblk)), dma((15,)), dma((L.nblk,)), dma((3,)), dma((3,)), dma((n_f,)), dma((n_f,)),
            dma((2, n_dp)), dma((2, n_dp)), dma((16,)), dma((n_pool,)), dma((n_pool,)),
        ],
        compiler_params=pltpu.CompilerParams(collective_id=2, has_side_effects=True, vmem_limit_bytes=VLIMIT),
        cost_estimate=pl.CostEstimate(flops=20 * R * D * D, bytes_accessed=60 * R * D, transcendentals=0),
        name="back",
    )(*args)


def finish_kernel(n, rep, dkr, dvr, mixed, ig, vec, *outs):
    mats, vecs = outs[:7], outs[9:]
    outs[7][...] = mixed[...]
    outs[8][...] = ig[...]
    for m in range(5):
        mats[m][...] = rep[m].astype(F32)
    mats[5][...] = dkr[...].astype(F32)
    mats[6][...] = dvr[...].astype(F32).T

    @pl.when(pl.program_id(0) == 0)
    def _():
        for k in range(NVEC):
            vecs[k][...] = vec[k, :]


def finish(L, rep, dkr, dvr, mixed, ig, vec):
    R, D, U = L.R, L.D, L.U
    n = 4 if U % 512 == 0 else 3
    n = 6 if U % 768 == 0 else n
    rows, cols, lines = D // n, U // n, -(-R // (16 * n)) * 16
    row = pl.BlockSpec((lines, D), lambda i: (i, 0))
    mat = pl.BlockSpec((rows, D), lambda i: (i, 0))
    return pl.pallas_call(
        functools.partial(finish_kernel, n),
        grid=(n,),
        out_shape=(sds((D, D)),) * 5 + (sds((D, U)), sds((U, D))) + (sds((R, D), BF16),) * 2 + (sds((D,)),) * NVEC,
        in_specs=[
            pl.BlockSpec((5, rows, D), lambda i: (0, i, 0)), pl.BlockSpec((rows, U), lambda i: (i, 0)),
            pl.BlockSpec((D, cols), lambda i: (0, i)), row, row, pl.BlockSpec((16, D), lambda i: (0, 0)),
        ],
        out_specs=(mat,) * 5 + (pl.BlockSpec((rows, U), lambda i: (i, 0)), pl.BlockSpec((cols, D), lambda i: (i, 0)), row, row)
        + (pl.BlockSpec((D,), lambda i: (0,)),) * NVEC,
        compiler_params=pltpu.CompilerParams(vmem_limit_bytes=VLIMIT),
        cost_estimate=pl.CostEstimate(flops=0, bytes_accessed=42 * D * D, transcendentals=0),
        name="finish",
    )(rep, dkr, dvr, mixed, ig, vec)


def solution(mesh):
    def step(
        tokens, lens, og, ln1g, ln1b, td, tf, mk, mv, mr, wk, wv, wr, wo, ln2g, ln2b, cmk, cmr, ckw, cvw, wc
    ):
        L = Layout(mesh, tokens.shape[0], tokens.shape[1], ckw.shape[1])
        vecs = [ln1g, ln1b, td, tf, mk, mv, mr, ln2g, ln2b, cmk, cmr]
        xk, xv, xr, y, ck, cr, a, v, rd, wkv, sr, x1, edge, par, kall, vall = front(
            L, tokens, vecs, wk, wv, wr, wo, ckw, cvw
        )
        mixed, g2, gck, gcr, big, dc = middle(L, lens, ck, cr, x1, og, kall, vall, ckw, cvw, wc)
        ig, dkr, dvr, rep, vec = back(
            L, tokens, par, edge, g2, gck, gcr, x1, y, sr, wkv, rd, a, v, xk, xv, xr, wk, wv, wr, wo, big, dc
        )
        done = finish(L, rep, dkr, dvr, mixed, ig, vec)
        mats, (mixed, ig), vecs = done[:7], done[7:9], done[9:]
        return (mixed, ig, *vecs[:7], *mats[:4], *vecs[7:], mats[5], mats[6], mats[4])

    row, none = P(("dp", "ffn"), None), P()
    return jax.shard_map(
        step,
        mesh=mesh,
        in_specs=(row, P("dp"), row) + (none,) * 15 + (P(None, "ffn"), P("ffn", None), none),
        out_specs=(row, row) + (none,) * 15 + (P(None, "ffn"), P("ffn", None), none),
        check_vma=False,
    )
```

```python
import functools

import jax
import jax.numpy as jnp
from jax import lax
from jax.experimental import pallas as pl
from jax.experimental.pallas import tpu as pltpu
from jax.sharding import PartitionSpec as P

MAX_LEN = 4096
SPAN = 128
EPS = 1e-05
MESH = pl.DeviceIdType.MESH
F32 = jnp.float32
BF16 = jnp.bfloat16
ANY = pl.BlockSpec(memory_space=pl.ANY)
VMEM = pl.BlockSpec(memory_space=pltpu.VMEM)
SMEM = pl.BlockSpec(memory_space=pltpu.SMEM)
VLIMIT = 62 * 2**20
G1, B1, TD, TF, MK, MV, MR, G2, B2, CK, CR = range(11)
NVEC = 11


def dot(a, b, da=1, db=0):
    return lax.dot_general(a, b, (((da,), (db,)), ((), ())), preferred_element_type=F32)


def sds(shape, dtype=F32):
    return jax.ShapeDtypeStruct(shape, dtype)


def flip(i, bit):
    s = 1 << bit
    return i + s - 2 * s * ((i // s) % 2)


def rows_of(i, n):
    return pl.ds(pl.multiple_of(i * n, n), n)


def sigmoid(x):
    return 1.0 / (1.0 + jnp.exp(-x))


def normed(x):
    c = x - jnp.mean(x, axis=-1, keepdims=True)
    rs = lax.rsqrt(jnp.mean(c * c, axis=-1, keepdims=True) + EPS)
    return c * rs, rs


def split2(x):
    hi = x.astype(BF16)
    lo = (x - hi.astype(F32)).astype(BF16)
    return jnp.concatenate([hi, lo], axis=0)


def tri_pair(below):
    r = lax.broadcasted_iota(jnp.int32, (SPAN, 2 * SPAN), 0)
    c = lax.broadcasted_iota(jnp.int32, (SPAN, 2 * SPAN), 1) % SPAN
    keep = (r > c) if below else (r < c)
    return jnp.where(keep, 1.0, 0.0).astype(BF16)


def greet(peers):
    bar = pltpu.get_barrier_semaphore()
    for p in peers:
        pl.semaphore_signal(bar, inc=1, device_id=p, device_id_type=MESH)
    pl.semaphore_wait(bar, len(peers))


def remote(src, dst, ssem, rsem, dev):
    return pltpu.make_async_remote_copy(
        src_ref=src, dst_ref=dst, send_sem=ssem, recv_sem=rsem, device_id=dev, device_id_type=MESH
    )


class Layout:
    def __init__(self, mesh, rows, width, local_units):
        self.n_f = mesh.shape["ffn"]
        self.n_dp = mesh.shape["dp"]
        self.R = rows
        self.D = width
        self.U = local_units
        self.BR = 256
        self.nblk = rows // self.BR
        self.nspan = rows // SPAN
        slot_len = min(MAX_LEN, rows * self.n_f)
        self.per_slot = slot_len // rows
        self.bits = self.n_f.bit_length() - 1
        self.parts = 2 if self.bits == 2 else 1
        self.nz = self.n_dp // 2

    def order(self, part):
        b = list(range(self.bits))
        return b if part == 0 else b[::-1]


def flips(i, mask):
    b = 0
    while mask >> b:
        if (mask >> b) & 1:
            i = flip(i, b)
        b += 1
    return i


def spans(bits):
    out = [0]
    for b in bits:
        out = out + [m | (1 << b) for m in out]
    return out


def gather_steps(L):
    steps, flat = [], 0
    for t in range(L.bits):
        here = []
        for p in range(L.parts):
            o = L.order(p)
            for m in spans(o[:t]):
                here.append((p, o[t], m, flat))
                flat += 1
        steps.append(here)
    return steps, flat


class Gather:
    def __init__(self, L, core, dp, me, half, source, dest, sems):
        self.L, self.half, self.source, self.dest = L, half, source, dest
        self.core, self.dp, self.me = core, dp, me
        self.g_ssem, self.g_rsem, self.c_ssem, self.c_rsem = sems
        self.steps, _ = gather_steps(L)

    def rows(self, p):
        n = self.half // self.L.parts
        return pl.ds(pl.multiple_of(self.core * self.half + p * n, 16), n)

    def link(self, t, own=None):
        return [
            remote(self.source(m, self.rows(p)), self.dest(m | (1 << bit), self.rows(p)),
                   self.g_ssem.at[f], self.g_rsem.at[f], (self.dp, flip(self.me, bit)))
            for p, bit, m, f in self.steps[t]
            if own is None or own == (m == 0)
        ]

    def across(self, t):
        buddy = self.dp + 1 - 2 * self.core
        out = []
        for p, bit, m, f in self.steps[t]:
            ref = self.dest(m | (1 << bit), self.rows(p))
            out.append(remote(ref, ref, self.c_ssem.at[f], self.c_rsem.at[f], (buddy, self.me)))
        return out


def front_kernel(
    L, tok, *refs
):
    vecs, refs = refs[:NVEC], refs[NVEC:]
    (
        wk, wv, wr, wo, kshard, vshard,
        xk_o, xv_o, xr_o, y_o, ck_o, cr_o, a_o, v_o, rd_o, wkv_o, sr_o, x1_o, edge_o, par, kall, vall,
        tokv, w4, npad, xk_s, xv_s, xr_s, y_s, ck_s, cr_s, a_s, v_s, S_s, D_s, sr_s, x1_s, srb_s,
        grow, fade, tri, ent, st_out, st_in, tedge, nedge, dev_in,
        in_sem, out_sem, e_ssem, e_rsem, s_ssem, s_rsem, g_ssem, g_rsem, c_ssem, c_rsem,
    ) = refs
    D, BR, n_f = L.D, L.BR, L.n_f
    dp, me = lax.axis_index("dp"), lax.axis_index("ffn")
    core = dp % 2
    buddy = dp + 1 - 2 * core
    place = me % L.per_slot
    keep = jnp.where(place == 0, 0.0, 1.0).astype(F32)
    ins = [pltpu.make_async_copy(tok, tokv, in_sem.at[0])]
    for n, w in enumerate((wk, wv, wr, wo)):
        ins.append(pltpu.make_async_copy(w, w4.at[n], in_sem.at[1 + n]))
    for cp in ins:
        cp.start()
    greet([(dp, (me + k) % n_f) for k in range(1, n_f)] + [(buddy, me)])

    nxt = (me + 1) % n_f
    tok_edge = remote(tok.at[pl.ds(L.R - 16, 16)], tedge, e_ssem.at[0], e_rsem.at[0], (dp, nxt))
    tok_edge.start()

    def gather(n, shard, full, half):
        return Gather(
            L, core, dp, me, half,
            lambda m, r: full.at[m, r] if m else shard.at[r],
            lambda m, r: full.at[m, r],
            (g_ssem.at[n], g_rsem.at[n], c_ssem.at[n], c_rsem.at[n]),
        )

    keys, values = gather(0, kshard, kall, D // 2), gather(1, vshard, vall, L.U // 2)
    for cp in keys.link(0) + values.link(0):
        cp.start()
    for n in range(NVEC):
        par[n : n + 1, :] = vecs[n][...].reshape(1, D)

    w = jnp.exp(par[TD : TD + 1, :])
    ew = jnp.exp(w)
    eu = jnp.exp(par[TF : TF + 1, :])
    age = lax.broadcasted_iota(jnp.int32, (SPAN, D), 0).astype(F32) * w
    grow[...] = jnp.exp(age)
    fade[...] = jnp.exp(-age)
    tri[...] = tri_pair(True)
    full_fade = jnp.exp(-float(SPAN) * w)
    tail_fade = jnp.exp(-float(SPAN - 1) * w)
    st_out[...] = jnp.zeros_like(st_out)

    ins[0].wait()
    tok_edge.wait()
    en, _ = normed(tedge[...].astype(F32))
    en = (en * par[G1 : G1 + 1, :] + par[B1 : B1 + 1, :])[8:16] * keep
    npad[0:8, :] = en
    edge_o[0:8, :] = en
    for cp in ins[1:4]:
        cp.wait()

    outs_a = ((xk_s, xk_o), (xv_s, xv_o), (xr_s, xr_o), (a_s, a_o), (v_s, v_o), (srb_s, sr_o))
    outs_c = ((y_s, y_o), (S_s, wkv_o), (D_s, rd_o), (x1_s, x1_o))
    outs_d = ((ck_s, ck_o), (cr_s, cr_o))

    def ship(outs, base, i):
        return [
            pltpu.make_async_copy(s.at[rows_of(i, BR)], o.at[rows_of(i, BR)], out_sem.at[base + n, i])
            for n, (s, o) in enumerate(outs)
        ]

    def phase_a(i, carry):
        r = rows_of(i, BR)
        n1, _ = normed(tokv[r, :].astype(F32))
        n1 = n1 * par[G1 : G1 + 1, :] + par[B1 : B1 + 1, :]
        npad[pl.ds(pl.multiple_of(i * BR + 8, 8), BR), :] = n1
        prev = pltpu.roll(npad[pl.ds(pl.multiple_of(i * BR, 8), BR + 8), :], 1, 0)[8:]
        d = n1 - prev
        xk = (prev + d * par[MK : MK + 1, :]).astype(BF16)
        xv = (prev + d * par[MV : MV + 1, :]).astype(BF16)
        xr = (prev + d * par[MR : MR + 1, :]).astype(BF16)
        xk_s[r, :] = xk
        xv_s[r, :] = xv
        xr_s[r, :] = xr
        a = jnp.exp(dot(xk, w4[0]))
        v = dot(xv, w4[1])
        a_s[r, :] = a
        v_s[r, :] = v
        for sb in range(BR // SPAN):
            b = i * (BR // SPAN) + sb
            aa = a[sb * SPAN : (sb + 1) * SPAN]
            vv = v[sb * SPAN : (sb + 1) * SPAN]
            ga = grow[...] * aa
            both = jnp.concatenate([ga * vv, ga], axis=1)
            pre = dot(tri[...], split2(both))
            fs = fade[...] * ew
            S_s[rows_of(b, SPAN), :] = fs * pre[:, :D]
            D_s[rows_of(b, SPAN), :] = fs * pre[:, D:]
            tot = pre[SPAN - 1 : SPAN] + both[SPAN - 1 : SPAN]
            num, den = st_out[0:1, :], st_out[1:2, :]
            ent[b, 0:1, :] = num
            ent[b, 1:2, :] = den
            st_out[0:1, :] = full_fade * num + tail_fade * tot[:, :D]
            st_out[1:2, :] = full_fade * den + tail_fade * tot[:, D:]
        sr = sigmoid(dot(xr, w4[2]))
        sr_s[r, :] = sr
        srb_s[r, :] = sr.astype(BF16)
        for cp in ship(outs_a, 0, i):
            cp.start()
        return carry

    lax.fori_loop(0, L.nblk, phase_a, 0)

    states = [
        remote(st_out, st_in.at[k], s_ssem.at[k], s_rsem.at[k], (dp, (me + k) % n_f)) for k in range(1, n_f)
    ]
    for cp in states:
        cp.start()

    for t in range(L.bits - 1):
        for cp in keys.link(t):
            cp.wait_recv()
        for cp in keys.link(t + 1):
            cp.start()
    for cp in values.link(0):
        cp.wait_recv()
    for t in range(L.bits - 1):
        for cp in keys.across(t):
            cp.start()
    for cp in values.across(0):
        cp.start()

    for cp in states:
        cp.wait()
    num_in = jnp.zeros((1, D), F32)
    den_in = jnp.zeros((1, D), F32)
    for k in range(1, L.per_slot):
        ok = jnp.where(place >= k, 1.0, 0.0).astype(F32)
        f = jnp.exp(-float((k - 1) * L.R) * w) * ok
        num_in = num_in + f * st_in[k, 0:1, :]
        den_in = den_in + f * st_in[k, 1:2, :]
    dev_in[0:1, :] = num_in
    dev_in[1:2, :] = den_in
    for cp in ins[4:]:
        cp.wait()

    def phase_c(i, carry):
        r = rows_of(i, BR)
        for sb in range(BR // SPAN):
            b = i * (BR // SPAN) + sb
            rb = rows_of(b, SPAN)
            fb = jnp.exp(w * (b * (-SPAN)).astype(F32))
            en = ent[b, 0:1, :] + fb * dev_in[0:1, :]
            ed = ent[b, 1:2, :] + fb * dev_in[1:2, :]
            F = eu * a_s[rb, :]
            fd = fade[...]
            num = S_s[rb, :] + fd * en + F * v_s[rb, :]
            rd = 1.0 / (D_s[rb, :] + fd * ed + F)
            wkv = num * rd
            S_s[rb, :] = wkv
            D_s[rb, :] = rd
            y_s[rb, :] = (sr_s[rb, :] * wkv).astype(BF16)
        x1 = tokv[r, :].astype(F32) + dot(y_s[r, :], w4[3])
        x1_s[r, :] = x1
        n2, _ = normed(x1)
        npad[pl.ds(pl.multiple_of(i * BR + 8, 8), BR), :] = n2 * par[G2 : G2 + 1, :] + par[B2 : B2 + 1, :]
        for cp in ship(outs_c, 6, i):
            cp.start()
        return carry

    lax.fori_loop(0, L.nblk, phase_c, 0)

    n_edge = remote(npad.at[pl.ds(L.R, 8)], nedge, e_ssem.at[1], e_rsem.at[1], (dp, nxt))
    n_edge.start()

    def phase_d(ii, carry):
        i = L.nblk - 1 - ii
        r = rows_of(i, BR)
        win = npad[pl.ds(pl.multiple_of(i * BR, 8), BR + 8), :]
        prev = pltpu.roll(win, 1, 0)[8:]
        d = win[8:] - prev
        ck_s[r, :] = (prev + d * par[CK : CK + 1, :]).astype(BF16)
        cr_s[r, :] = (prev + d * par[CR : CR + 1, :]).astype(BF16)
        for cp in ship(outs_d, 10, i):
            cp.start()
        return carry

    lax.fori_loop(0, L.nblk - 1, phase_d, 0)
    n_edge.wait()
    npad[0:8, :] = nedge[...] * keep
    edge_o[8:16, :] = nedge[...] * keep
    phase_d(L.nblk - 1, 0)

    for cp in keys.link(L.bits - 1):
        cp.wait_recv()
    for cp in keys.across(L.bits - 1):
        cp.start()
    for t in range(L.bits):
        for cp in keys.link(t):
            cp.wait_send()
        for cp in keys.across(t):
            cp.wait()
    for cp in values.link(0):
        cp.wait_send()
    for cp in values.across(0):
        cp.wait()

    def drain(i, carry):
        for outs, base in ((outs_a, 0), (outs_c, 6), (outs_d, 10)):
            for cp in ship(outs, base, i):
                cp.wait()
        return carry

    lax.fori_loop(0, L.nblk, drain, 0)


def front(L, tok, vecs, wk, wv, wr, wo, kshard, vshard):
    R, D, n_f, U = L.R, L.D, L.n_f, L.U
    _, flat = gather_steps(L)
    rb, rf = sds((R, D), BF16), sds((R, D))
    dma = pltpu.SemaphoreType.DMA
    return pl.pallas_call(
        functools.partial(front_kernel, L),
        out_shape=(rb,) * 6 + (rf,) * 4 + (rb, rf) + (sds((16, D)), sds((16, D)), sds((n_f, D, U), BF16), sds((n_f, U, D), BF16)),
        in_specs=[ANY] + [VMEM] * NVEC + [ANY] * 6,
        out_specs=(ANY,) * 12 + (VMEM, VMEM, ANY, ANY),
        scratch_shapes=[
            pltpu.VMEM((R, D), BF16), pltpu.VMEM((4, D, D), BF16), pltpu.VMEM((R + 8, D), F32),
            *([pltpu.VMEM((R, D), BF16)] * 6), *([pltpu.VMEM((R, D), F32)] * 6), pltpu.VMEM((R, D), BF16),
            pltpu.VMEM((SPAN, D), F32), pltpu.VMEM((SPAN, D), F32), pltpu.VMEM((SPAN, 2 * SPAN), BF16),
            pltpu.VMEM((L.nspan, 8, D), F32), pltpu.VMEM((8, D), F32), pltpu.VMEM((n_f, 8, D), F32),
            pltpu.VMEM((16, D), BF16), pltpu.VMEM((8, D), F32), pltpu.VMEM((8, D), F32),
            dma((5,)), dma((12, L.nblk)), dma((2,)), dma((2,)), dma((n_f,)), dma((n_f,)),
            dma((2, flat)), dma((2, flat)), dma((2, flat)), dma((2, flat)),
        ],
        compiler_params=pltpu.CompilerParams(collective_id=0, has_side_effects=True, vmem_limit_bytes=VLIMIT),
        cost_estimate=pl.CostEstimate(flops=10 * R * D * D, bytes_accessed=40 * R * D, transcendentals=4 * R * D),
        name="front",
    )(tok, *vecs, wk, wv, wr, wo, kshard, vshard)


def squeeze(mask, bit):
    return ((mask >> (bit + 1)) << bit) | (mask & ((1 << bit) - 1))


def middle_kernel(
    L, lens, ck, cr, x1, og, kall, vall, kshard, vshard, wc,
    mixed_o, g2_o, gck_o, gcr_o, big_o, dc_o,
    kv, vv, wcv, ck_s, cr_s, x1_s, gate_s, og_s, mix_s, gv_s, gg_s, ckt_s, gvt_s, h_s, p_s, dk_s, dv_s, dc_s, inc, r0,
    in_sem, w_sem, out_sem, g_sem, x_ssem, x_rsem, h_ssem, h_rsem, g_ssem, g_rsem, c_ssem, c_rsem,
):
    BR, n_f, D, U = 2 * L.BR, L.n_f, L.D, L.U
    nblk, tile = L.R // BR, L.BR
    dp, me = lax.axis_index("dp"), lax.axis_index("ffn")
    core = dp % 2
    buddy = dp + 1 - 2 * core
    half = D // 2
    hk = half // L.parts
    length = lens[me // L.per_slot]
    start = (me % L.per_slot) * L.R
    masks = sorted(range(n_f), key=lambda m: (-bin(m).count("1"), m))

    def fetch(n, src, dst):
        return pltpu.make_async_copy(src, dst, w_sem.at[n])

    k_cp = [fetch(m, kall.at[m] if m else kshard, kv.at[m]) for m in range(n_f)]
    v_cp = [fetch(n_f, vshard, vv.at[0])]
    uh = U // 2
    for p in range(L.parts):
        m = 1 << L.order(p)[0]
        for c in range(2):
            r = pl.ds(c * uh + p * (uh // L.parts), uh // L.parts)
            v_cp.append(fetch(n_f + 1 + 2 * p + c, vall.at[m, r], vv.at[m, r]))
    pairs = ((ck, ck_s), (cr, cr_s), (wc, wcv), (x1, x1_s), (og, og_s))
    ins = [pltpu.make_async_copy(s, d, in_sem.at[n]) for n, (s, d) in enumerate(pairs)]
    for cp in [ins[0]] + k_cp:
        cp.start()

    greet([(buddy, me)] + [(dp, flip(me, b)) for b in range(L.bits)])

    first = [1 << L.order(p)[0] for p in range(L.parts)]
    values = Gather(
        L, core, dp, me, uh,
        lambda m, r: vshard.at[r] if m == 0 else (vall.at[m, r] if m in first else vv.at[m, r]),
        lambda m, r: vv.at[m, r],
        (g_ssem, g_rsem, c_ssem, c_rsem),
    )
    if L.bits > 1:
        for cp in values.link(1):
            cp.start()
    for cp in [ins[0]] + k_cp:
        cp.wait()
    for cp in ins[1:3] + v_cp + ins[3:]:
        cp.start()

    def keys_block(i, carry):
        r = rows_of(i, BR)
        ck_i = ck_s[r, :]
        for m in range(n_f):
            p = jnp.maximum(dot(ck_i, kv[m]), 0.0)
            p_s[m, r, :] = p.astype(BF16)
            h_s[m, r, :] = (p * p).astype(BF16)
        ckt_s[:, pl.ds(pl.multiple_of(i * BR, 128), BR)] = ck_i.T
        return carry

    lax.fori_loop(0, nblk, keys_block, 0)
    for cp in ins[1:3]:
        cp.wait()

    def gate_block(i, carry):
        r = rows_of(i, BR)
        gate_s[r, :] = sigmoid(dot(cr_s[r, :], wcv[...]))
        return carry

    lax.fori_loop(0, nblk, gate_block, 0)
    for cp in v_cp + ins[3:]:
        cp.wait()
    for t in range(1, L.bits):
        for cp in values.link(t):
            cp.wait_recv()
        for cp in values.across(t):
            cp.start()
        if t + 1 < L.bits:
            for cp in values.link(t + 1):
                cp.start()
    for t in range(1, L.bits):
        for cp in values.across(t):
            cp.wait_recv()

    def ship(i):
        r = rows_of(i, BR)
        both = ((mix_s, mixed_o), (og_s, g2_o), (ck_s, gck_o), (cr_s, gcr_o))
        return [pltpu.make_async_copy(s.at[r], d.at[r], out_sem.at[n, i]) for n, (s, d) in enumerate(both)]

    def values_block(i, carry):
        r = rows_of(i, BR)
        vsum = jnp.zeros((BR, D), F32)
        for m in range(n_f):
            vsum = vsum + dot(h_s[m, r, :], vv[m])
        pos = start + i * BR + lax.broadcasted_iota(jnp.int32, (BR, 1), 0)
        live = jnp.where(pos < length, 1.0, 0.0).astype(F32)
        gate_i = gate_s[r, :]
        mix_s[r, :] = ((x1_s[r, :] + gate_i * vsum) * live).astype(BF16)
        g2 = og_s[r, :].astype(F32) * live
        og_s[r, :] = g2.astype(BF16)
        gv32 = g2 * gate_i
        gv = gv32.astype(BF16)
        gv_s[r, :] = gv
        gg_s[r, :] = (gv32 * vsum * (1.0 - gate_i)).astype(BF16)
        gvt_s[:, pl.ds(pl.multiple_of(i * BR, 128), BR)] = gv.T
        for cp in ship(i)[:2]:
            cp.start()
        return carry

    lax.fori_loop(0, nblk, values_block, 0)

    own = pl.ds(pl.multiple_of(core * half, 16), half)
    away = pl.ds(pl.multiple_of((1 - core) * half, 16), half)

    def swaps(m):
        return [
            remote(g.at[m, away], inc.at[n, m], x_ssem.at[n, m], x_rsem.at[n, m], (buddy, me))
            for n, g in enumerate((dk_s, dv_s))
        ]

    def part_rows(p):
        return pl.ds(pl.multiple_of(core * half + p * hk, 16), hk)

    def halves(m):
        out = []
        for p in range(L.parts):
            bit = L.order(p)[0]
            if (m >> bit) & 1:
                k = squeeze(m, bit)
                for n, g in enumerate((dk_s, dv_s)):
                    out.append(
                        remote(g.at[m, part_rows(p)], r0.at[n, p, k], h_ssem.at[n, p, k], h_rsem.at[n, p, k],
                               (dp, flip(me, bit)))
                    )
        return out

    def merge(n, m):
        swaps(m)[n].wait_recv()
        g = (dk_s, dv_s)[n]
        g[m, own, :] = (g[m, own, :].astype(F32) + inc[n, m].astype(F32)).astype(BF16)
        for cp in halves(m)[n::2]:
            cp.start()

    def weight_grad(n, m):
        left, right, g = ((ckt_s, p_s, dk_s), (gvt_s, h_s, dv_s))[n]
        for c in range(D // tile):
            rr = slice(c * tile, (c + 1) * tile)
            g[m, rr, :] = dot(left[rr, :], right[m]).astype(BF16)
        swaps(m)[n].start()

    for n, m in enumerate(masks):
        weight_grad(1, m)
        if n > 0:
            merge(1, masks[n - 1])

    for n, m in enumerate(masks):
        def block(i, carry, m=m, n=n):
            r = rows_of(i, BR)
            gk = (dot(gv_s[r, :], vv[m], 1, 1) * (2.0 * p_s[m, r, :].astype(F32))).astype(BF16)
            p_s[m, r, :] = gk
            part = dot(gk, kv[m], 1, 1)
            total = part if n == 0 else x1_s[r, :] + part
            if n + 1 < n_f:
                x1_s[r, :] = total
            else:
                ck_s[r, :] = total.astype(BF16)
                ship(i)[2].start()
            return carry

        lax.fori_loop(0, nblk, block, 0)
        merge(0, masks[n - 1]) if n > 0 else merge(1, masks[-1])
        weight_grad(0, m)

    for c in range(D // tile):
        rr = slice(c * tile, (c + 1) * tile)
        dc_s[rr, :] = dot(cr_s[:, rr], gg_s[...], 0, 0).astype(BF16)
    merge(0, masks[-1])

    def last_block(i, carry):
        r = rows_of(i, BR)
        cr_s[r, :] = dot(gg_s[r, :], wcv[...], 1, 1).astype(BF16)
        ship(i)[3].start()
        return carry

    lax.fori_loop(0, nblk, last_block, 0)
    last = pltpu.make_async_copy(dc_s, dc_o, in_sem.at[0])
    last.start()

    outs = []
    for m in masks:
        for cp in halves(m):
            cp.wait_recv()
    for p in range(L.parts):
        bit = L.order(p)[0]
        for m in range(n_f):
            if (m >> bit) & 1:
                continue
            k = squeeze(m, bit)
            for n, g in enumerate((dk_s, dv_s)):
                r = part_rows(p)
                r0[n, p, k] = (g[m, r, :].astype(F32) + r0[n, p, k].astype(F32)).astype(BF16)
                outs.append(pltpu.make_async_copy(r0.at[n, p, k], big_o.at[n, p, k], g_sem.at[n, p, k]))
                outs[-1].start()
    for m in masks:
        for cp in halves(m) + swaps(m):
            cp.wait_send()
    for t in range(1, L.bits):
        for cp in values.link(t) + values.across(t):
            cp.wait_send()
    for i in range(nblk):
        for cp in ship(i):
            cp.wait()
    for cp in outs + [last]:
        cp.wait()


def middle(L, lens, ck, cr, x1, og, kall, vall, kshard, vshard, wc):
    R, D, n_f, U = L.R, L.D, L.n_f, L.U
    dma = pltpu.SemaphoreType.DMA
    rb = sds((R, D), BF16)
    vb, vf = pltpu.VMEM((R, D), BF16), pltpu.VMEM((R, D), F32)
    hid = pltpu.VMEM((n_f, R, U), BF16)
    kept = (2, L.parts, n_f // 2, D // 2 // L.parts, U)
    _, flat = gather_steps(L)
    sem3 = dma(kept[:3])
    return pl.pallas_call(
        functools.partial(middle_kernel, L),
        out_shape=(rb, rb, rb, rb, sds(kept, BF16), sds((D, D), BF16)),
        in_specs=[SMEM] + [ANY] * 9,
        out_specs=(ANY,) * 6,
        scratch_shapes=[
            pltpu.VMEM((n_f, D, U), BF16), pltpu.VMEM((n_f, U, D), BF16), pltpu.VMEM((D, D), BF16),
            vb, vb, vf, vf, vb, vb, vb, vb, pltpu.VMEM((D, R), BF16), pltpu.VMEM((D, R), BF16), hid, hid,
            pltpu.VMEM((n_f, D, U), BF16), pltpu.VMEM((n_f, D, U), BF16), pltpu.VMEM((D, D), BF16),
            pltpu.VMEM((2, n_f, D // 2, U), BF16), pltpu.VMEM(kept, BF16),
            dma((6,)), dma((n_f + 1 + 2 * L.parts,)), dma((4, L.nblk)), sem3, dma((2, n_f)), dma((2, n_f)),
            sem3, sem3, dma((flat,)), dma((flat,)), dma((flat,)), dma((flat,)),
        ],
        compiler_params=pltpu.CompilerParams(collective_id=1, has_side_effects=True, vmem_limit_bytes=VLIMIT),
        cost_estimate=pl.CostEstimate(flops=52 * R * D * D, bytes_accessed=60 * R * D, transcendentals=0),
        name="middle",
    )(lens, ck, cr, x1, og, kall, vall, kshard, vshard, wc)


class Pool:
    def __init__(self, ssem, rsem):
        self.ssem, self.rsem, self.n = ssem, rsem, 0

    def copy(self, src, dst, dev):
        k = self.n
        self.n = k + 1
        return remote(src, dst, self.ssem.at[k], self.rsem.at[k], dev)


def begin(copies):
    for cp in copies:
        cp.start()
    return copies


def landed(copies):
    for cp in copies:
        cp.wait_recv()


class Unit:
    def __init__(self, env, order, rows, done, acc, rbuf, zbuf, final, source=None, swap=None, gather=False):
        self.env, self.rows, self.acc, self.rbuf, self.zbuf, self.final = env, rows, acc, rbuf, zbuf, final
        self.source = source
        self.order = order
        self.sent, self.pending, self.now = [], None, []
        self.off, self.size, self.zoff, self.split, self.slot = 0, rows, 0, [], 0
        steps = [swap] if swap else []
        steps += [functools.partial(self.halve, t) for t in range(done, len(order))]
        steps += [functools.partial(self.halve_z, b) for b in range(env.zbits)]
        steps += [self.home]
        if gather:
            steps += [functools.partial(self.double, t) for t in range(len(order))]
        steps += [self.cross]
        self.steps = steps

    def keep(self, copies):
        self.sent += copies
        self.now = begin(copies)

    def advance(self):
        landed(self.now)
        self.now = []
        if self.pending:
            self.pending()
            self.pending = None
        if not self.steps:
            return False
        self.steps.pop(0)()
        return True

    def halve(self, t):
        e, bit = self.env, self.order[t]
        masks = spans(self.order[t + 1 :])
        base, src = self.slot, self.source or self.acc
        self.slot += len(masks)
        self.source = None
        self.keep([
            e.pool.copy(src(m | (1 << bit)), self.rbuf(base + n), (e.dp, flip(e.me, bit))) for n, m in enumerate(masks)
        ])

        def end():
            for n, m in enumerate(masks):
                view = self.acc(m)
                view[...] = (view[...].astype(F32) + self.rbuf(base + n)[...].astype(F32)).astype(BF16)

        self.pending = end

    def part(self, off, size):
        return pl.ds(pl.multiple_of(off, 16), size)

    def halve_z(self, b):
        e, mine = self.env, (self.env.zi // (1 << b)) % 2
        split = (self.size // 2) % 16 == 0
        size = self.size // 2 if split else self.size
        kept = self.off + (mine * size if split else 0)
        sent = self.off + ((1 - mine) * size if split else 0)
        buf = self.zbuf(pl.ds(self.zoff, size))
        self.zoff += size
        peer = (flip(e.zi, b) * 2 + e.core, e.me)
        self.keep([e.pool.copy(self.acc(0).at[self.part(sent, size)], buf, peer)])
        if split:
            self.split.append((b, self.off, self.size))
        self.off, self.size = kept, size

        def end():
            if not split:
                self.sent.pop().wait_send()
            view = self.acc(0).at[self.part(kept, size)]
            view[...] = (view[...].astype(F32) + buf[...].astype(F32)).astype(BF16)

        self.pending = end

    def home(self):
        e = self.env
        here = self.acc(0).at[self.part(self.off, self.size)]
        self.local = pltpu.make_async_copy(here, self.final(0, self.off, self.size), e.lsem.at[e.nl])
        e.nl += 1
        self.local.start()
        self.steps = [functools.partial(self.double_z, n) for n in reversed(range(len(self.split)))] + self.steps
        self.first = here
        if self.split:
            self.steps.pop(0)()
        else:
            self.pending = self.local.wait

    def double_z(self, n):
        e = self.env
        b, off, size = self.split[n]
        src = self.final(0, self.off, self.size) if self.first is None else self.first
        self.keep([e.pool.copy(src, self.final(0, self.off, self.size), (flip(e.zi, b) * 2 + e.core, e.me))])
        if self.first is not None:
            self.first = None
            self.pending = self.local.wait
        self.off, self.size = off, size

    def double(self, t):
        e, o = self.env, self.order
        out = []
        for m in spans(o[:t]):
            v = self.final(m, 0, self.rows)
            out.append(e.pool.copy(v, v, (e.dp, flip(e.me, o[t]))))
        self.keep(out)

    def cross(self):
        e = self.env
        v = self.final(None, 0, self.rows)
        self.keep([e.pool.copy(v, v, (e.dp + 1 - 2 * e.core, e.me))])


class Env:
    pass


KEY, VALUE, RECEPT, OUT, CMR = range(5)
FLIPPED = (CMR, RECEPT, VALUE,)
HOOKS = {
    "1a": "M",
    "1b": "abcd",
    "out": "",
    "rec": "M",
    "key": "ORM",
    "value": "",
    "3a": "K",
    "3b": "MORV",
    "4a": "abM",
    "4b": "",
    "tail": "ORKMOWRVMOKRVMKOWVRKOcVRMKdOabMVKRcVOKdO",
    "end": "abRVcRdKKVabcdaVbcd",
}
V_LN1G, V_LN1B, V_TD, V_TF, V_MK, V_MV, V_MR, V_LN2G, V_LN2B, V_CMK, V_CMR = range(11)


def back_kernel(
    L, tok, par, edge, g2, gck, gcr, x1, y, sr, wkv, rd, a, v, xk, xv, xr, wk, wv, wr, wo, bigh, dch,
    ig_o, dkr, dvr, rep, vec_o,
    gkb_s, grb_s, srb_s, gck_s, gcr_s, x1_s, a_s, wkv_s, rd_s, v_s, g2_s, y_s, xr_s, gr_s, gk_s, gv_s, w3, dw, acc1,
    inc, r1, r2, z1, z2, grow, fade, tri, ent, st_out, st_in, carry, gpad, tpad, vacc, vown, vf, vd, dev_in,
    blk_sem, in_sem, out_sem, e_ssem, e_rsem, s_ssem, s_rsem, v_ssem, v_rsem, lsem, p_ssem, p_rsem,
):
    D, BR, n_f, n_dp, U, R = L.D, L.BR, L.n_f, L.n_dp, L.U, L.R
    dp, me = lax.axis_index("dp"), lax.axis_index("ffn")
    core = dp % 2
    buddy = dp + 1 - 2 * core
    place = me % L.per_slot
    opens = jnp.where(place == 0, 0.0, 1.0).astype(F32)
    stays = jnp.where(place == L.per_slot - 1, 0.0, 1.0).astype(F32)
    half = D // 2

    blocks = ((gck, gkb_s), (gcr, grb_s), (x1, x1_s), (g2, g2_s), (sr, srb_s), (wkv, wkv_s), (rd, rd_s))

    def load(i, which):
        r = rows_of(i, BR)
        return [pltpu.make_async_copy(blocks[n][0].at[r], blocks[n][1].at[r], blk_sem.at[n, i]) for n in which]

    wo_cp = pltpu.make_async_copy(wo, w3.at[2], in_sem.at[0])
    begin(load(0, range(7)) + [wo_cp])
    for i in range(1, L.nblk):
        begin(load(i, range(7)))
    acc_cp = pltpu.make_async_copy(bigh, acc1, in_sem.at[1])
    y_cp = pltpu.make_async_copy(y, y_s, in_sem.at[3])
    xr_cp = pltpu.make_async_copy(xr, xr_s, in_sem.at[4])
    v_cp = pltpu.make_async_copy(v, v_s, in_sem.at[5])
    a_cp = pltpu.make_async_copy(a, a_s, in_sem.at[11])
    dc_cps = [
        pltpu.make_async_copy(dch.at[:, pl.ds(h * half, half)], dw.at[CMR, h], in_sem.at[6 + h]) for h in range(2)
    ]
    w_cps = [pltpu.make_async_copy(w, w3.at[n], in_sem.at[8 + n]) for n, w in enumerate((wk, wv))]
    begin(dc_cps)

    greet(
        [(dp, (me + k) % n_f) for k in range(1, n_f)] + [((dp + k) % n_dp, me) for k in range(1, n_dp)]
    )

    prv = (me + n_f - 1) % n_f
    edges = begin([
        remote(g.at[pl.ds(0, 16)], gpad.at[n], e_ssem.at[n], e_rsem.at[n], (dp, prv)) for n, g in enumerate((gck, gcr))
    ])

    e = Env()
    e.me, e.dp, e.core, e.zi, e.zbits = me, dp, core, dp // 2, L.nz.bit_length() - 1
    e.pool, e.lsem, e.nl = Pool(p_ssem, p_rsem), lsem, 0

    hk = half // L.parts
    big = []
    for n, res in enumerate((dkr, dvr)):
        for p in range(L.parts):
            o, off = L.order(p), p * hk

            def acc(m, n=n, p=p, o=o):
                return acc1.at[n, p, squeeze(m, o[0])]

            def source(m, n=n, p=p, o=o):
                return bigh.at[n, p, squeeze(m, o[0])]

            def rbuf(k, n=n, p=p):
                return r1.at[n, p, k]

            def zbuf(r, n=n, p=p):
                return z1.at[n, p, r]

            def final(m, r0, size, res=res, off=off):
                return res.at[pl.ds(pl.multiple_of(core * half + off + r0, 16), size)]

            big.append(Unit(e, o, hk, 1, acc, rbuf, zbuf, final, source))
    shard = D // n_f
    small = []
    for m_ in range(5):
        def acc(m, i=m_):
            return dw.at[i, core, pl.ds(pl.multiple_of(flips(me, m) * shard, 16), shard)]

        def rbuf(k, i=m_):
            return r2.at[i, k]

        def zbuf(r, i=m_):
            return z2.at[i, r]

        def final(m, r0, size, i=m_):
            cols = pl.ds(pl.multiple_of(core * half, 128), half)
            if m is None:
                return rep.at[i, :, cols]
            return rep.at[i, pl.ds(pl.multiple_of(flips(me, m) * shard + r0, 16), size), cols]

        def swap(i=m_):
            u = small[i]
            u.keep([e.pool.copy(dw.at[i, 1 - core], inc.at[i], (buddy, me))])

            def end():
                dw[i, core] = (dw[i, core].astype(F32) + inc[i].astype(F32)).astype(BF16)

            u.pending = end

        o = L.order(1) if m_ in FLIPPED else L.order(0)
        small.append(Unit(e, o, shard, 0, acc, rbuf, zbuf, final, None, swap, True))
    units = dict(zip("MORKV", (small[CMR], small[OUT], small[RECEPT], small[KEY], small[VALUE])))
    units.update(zip("abcd" if L.parts == 2 else "ac", big))

    class Vectors:
        def __init__(self):
            self.stage = 0

        def advance(self):
            self.stage += 1
            if self.stage == 1:
                vown[...] = jnp.sum(vacc[...], axis=1)
                vf[0] = vown[...]
                self.now = begin([
                    remote(vown, vf.at[k], v_ssem.at[0, k], v_rsem.at[0, k], (dp, (me + k) % n_f))
                    for k in range(1, n_f)
                ])
            elif self.stage == 2:
                for cp in self.now:
                    cp.wait()
                total = vf[me % n_f]
                for f in range(1, n_f):
                    total = total + vf[(me - f + n_f) % n_f]
                vd[0] = total
                self.now = begin([
                    remote(vd.at[0], vd.at[k], v_ssem.at[1, k], v_rsem.at[1, k], ((dp + k) % n_dp, me))
                    for k in range(1, n_dp)
                ])
            elif self.stage == 3:
                for cp in self.now:
                    cp.wait()
                total = vd[dp % n_dp]
                for f in range(1, n_dp):
                    total = total + vd[(dp - f + n_dp) % n_dp]
                vec_o[...] = total
                vec_o[V_TD : V_TD + 1, :] = w * (total[V_TD : V_TD + 1] - total[V_TF : V_TF + 1])
            return self.stage < 3

    units["W"] = Vectors()

    def go(names):
        for name in names:
            if name in units:
                units[name].advance()

    go("abcd")

    w = jnp.exp(par[TD : TD + 1, :])
    ew = jnp.exp(w)
    eu = jnp.exp(par[TF : TF + 1, :])
    age = lax.broadcasted_iota(jnp.int32, (SPAN, D), 0).astype(F32) * w
    grow[...] = jnp.exp(age)
    fade[...] = jnp.exp(-age)
    tri[...] = tri_pair(False)
    full_fade = jnp.exp(-float(SPAN) * w)
    tail_fade = jnp.exp(-float(SPAN - 1) * w)
    vacc[...] = jnp.zeros_like(vacc)
    carry[...] = edge[8:16, :]

    def add_up(n, x):
        vacc[n] = vacc[n] + jnp.sum(x.reshape(-1, 8, D), axis=0)

    for cp in dc_cps:
        cp.wait()
    go("M")
    wo_cp.wait()
    for cp in load(0, (0, 1)):
        cp.wait()

    def phase_1(i, _):
        @pl.when(i + 1 < L.nblk)
        def _wait():
            for cp in load(i + 1, (0, 1)):
                cp.wait()

        for cp in load(i, range(2, 7)):
            cp.wait()
        r = rows_of(i, BR)
        win = pl.ds(pl.multiple_of(i * BR, 16), BR + 16)
        mk, mr = par[CK : CK + 1, :], par[CR : CR + 1, :]
        gk = gkb_s[win, :].astype(F32)
        gr = grb_s[win, :].astype(F32)
        t = gk * (1.0 - mk) + gr * (1.0 - mr)
        t = pltpu.roll(t, BR + 15, 0)[:BR]
        gk, gr = gk[:BR], gr[:BR]
        gn = gk * mk + gr * mr + t
        n2, rs = normed(x1_s[r, :])
        norm2 = n2 * par[G2 : G2 + 1, :] + par[B2 : B2 + 1, :]
        prev = pltpu.roll(jnp.concatenate([carry[...], norm2], axis=0), 1, 0)[8:]
        carry[...] = norm2[BR - 8 :]
        d = norm2 - prev
        add_up(V_CMK, gk * d)
        add_up(V_CMR, gr * d)
        add_up(V_LN2G, gn * n2)
        add_up(V_LN2B, gn)
        q1 = gn * par[G2 : G2 + 1, :]
        m1 = jnp.mean(q1, axis=-1, keepdims=True)
        m2 = jnp.mean(q1 * n2, axis=-1, keepdims=True)
        g1 = g2_s[r, :].astype(F32) + (q1 - m1 - n2 * m2) * rs
        x1_s[r, :] = g1
        ga = g1.astype(BF16)
        g2_s[r, :] = ga
        s = srb_s[r, :].astype(F32)
        gys = dot(ga, w3[2], 1, 1) * s
        wk_ = wkv_s[r, :]
        gr_s[r, :] = (gys * wk_ * (1.0 - s)).astype(BF16)
        q = gys * rd_s[r, :]
        qw = q * wk_
        rd_s[r, :] = q
        wkv_s[r, :] = qw
        for sb in range(BR // SPAN):
            b = i * (BR // SPAN) + sb
            rb = rows_of(b, SPAN)
            sl = slice(sb * SPAN, (sb + 1) * SPAN)
            fd = fade[...]
            both = jnp.concatenate([fd * q[sl], fd * qw[sl]], axis=1)
            suf = dot(tri[...], split2(both))
            gs = grow[...] * ew
            gck_s[rb, :] = gs * suf[:, :D]
            gcr_s[rb, :] = gs * suf[:, D:]
            tot = suf[0:1] + both[0:1]
            ent[b, 0:1, :] = tot[:, :D]
            ent[b, 1:2, :] = tot[:, D:]
        return 0

    cut = L.nblk // 2
    lax.fori_loop(0, cut, phase_1, 0)
    begin([acc_cp, y_cp, xr_cp, a_cp, v_cp] + w_cps)
    go(HOOKS["1a"])
    lax.fori_loop(cut, L.nblk - 1, phase_1, 0)
    for cp in edges:
        cp.wait()
    gkb_s[R : R + 16, :] = (gpad[0].astype(F32) * stays).astype(BF16)
    grb_s[R : R + 16, :] = (gpad[1].astype(F32) * stays).astype(BF16)
    phase_1(L.nblk - 1, 0)

    acc_cp.wait()
    go(HOOKS["1b"])
    xq = jnp.zeros((1, D), F32)
    xw = jnp.zeros((1, D), F32)
    for b in reversed(range(L.nspan)):
        tq, tw = ent[b, 0:1, :], ent[b, 1:2, :]
        ent[b, 0:1, :] = xq
        ent[b, 1:2, :] = xw
        xq = tq + full_fade * xq
        xw = tw + full_fade * xw
    st_out[...] = jnp.zeros_like(st_out)
    st_out[0:1, :] = xq
    st_out[1:2, :] = xw
    states = begin([
        remote(st_out, st_in.at[k], s_ssem.at[k], s_rsem.at[k], (dp, (me + n_f - k) % n_f)) for k in range(1, n_f)
    ])
    w_cps.append(pltpu.make_async_copy(wr, w3.at[2], in_sem.at[10]))
    w_cps[-1].start()

    def product(m, left, right):
        for c in range(D // BR):
            rr = slice(c * BR, (c + 1) * BR)
            full = dot(left[:, rr], right[...], 0, 0).astype(BF16)
            dw[m, 0, rr, :] = full[:, :half]
            dw[m, 1, rr, :] = full[:, half:]

    y_cp.wait()
    product(OUT, y_s, g2_s)
    xk_cp = pltpu.make_async_copy(xk, y_s, in_sem.at[12])
    xv_cp = pltpu.make_async_copy(xv, g2_s, in_sem.at[14])
    begin([xk_cp, xv_cp])
    go("O" + HOOKS["out"])
    xr_cp.wait()
    product(RECEPT, xr_s, gr_s)
    go("R" + HOOKS["rec"])

    for cp in states:
        cp.wait()
    qi = jnp.zeros((1, D), F32)
    wi = jnp.zeros((1, D), F32)
    for k in range(1, L.per_slot):
        f = jnp.exp(-float((k - 1) * R) * w) * jnp.where(place + k < L.per_slot, 1.0, 0.0).astype(F32)
        qi = qi + f * st_in[k, 0:1, :]
        wi = wi + f * st_in[k, 1:2, :]
    dev_in[0:1, :] = qi
    dev_in[1:2, :] = wi
    a_cp.wait()
    v_cp.wait()
    first = place * R - (L.per_slot * R) // 2

    def phase_2(b, _):
        rb = rows_of(b, SPAN)
        fb = jnp.exp(w * ((b + 1 - L.nspan) * SPAN).astype(F32))
        eq = ent[b, 0:1, :] + fb * dev_in[0:1, :]
        ewk = ent[b, 1:2, :] + fb * dev_in[1:2, :]
        ff = grow[...] * tail_fade
        q, qw, av, vv = rd_s[rb, :], wkv_s[rb, :], a_s[rb, :], v_s[rb, :]
        gvr = av * (eu * q + gck_s[rb, :] + ff * eq)
        gkr = vv * gvr - av * (eu * qw + gcr_s[rb, :] + ff * ewk)
        gk_s[rb, :] = gkr.astype(BF16)
        gv_s[rb, :] = gvr.astype(BF16)
        add_up(V_TF, eu * av * (q * vv - qw))
        pos = (first + b * SPAN + lax.broadcasted_iota(jnp.int32, (SPAN, 1), 0)).astype(F32)
        add_up(V_TD, pos * gkr)
        return 0

    lax.fori_loop(0, L.nspan, phase_2, 0)
    xk_cp.wait()
    product(KEY, y_s, gk_s)
    tok_cp = pltpu.make_async_copy(tok, y_s, in_sem.at[13])
    tok_cp.start()
    go("K" + HOOKS["key"])
    xv_cp.wait()
    product(VALUE, g2_s, gv_s)
    go("V" + HOOKS["value"])

    for cp in w_cps:
        cp.wait()
    tok_cp.wait()
    carry[...] = edge[0:8, :]

    def phase_3(i, _):
        r = rows_of(i, BR)
        mk, mv, mr = par[MK : MK + 1, :], par[MV : MV + 1, :], par[MR : MR + 1, :]
        n1_, _rs = normed(y_s[r, :].astype(F32))
        norm1 = n1_ * par[G1 : G1 + 1, :] + par[B1 : B1 + 1, :]
        prev = pltpu.roll(jnp.concatenate([carry[...], norm1], axis=0), 1, 0)[8:]
        carry[...] = norm1[BR - 8 :]
        d = norm1 - prev
        gxk = dot(gk_s[r, :], w3[0], 1, 1)
        gxv = dot(gv_s[r, :], w3[1], 1, 1)
        gxr = dot(gr_s[r, :], w3[2], 1, 1)
        add_up(V_MK, gxk * d)
        add_up(V_MV, gxv * d)
        add_up(V_MR, gxr * d)
        now = gxk * mk + gxv * mv + gxr * mr
        gck_s[r, :] = gxk + gxv + gxr - now
        gcr_s[r, :] = now
        return 0

    lax.fori_loop(0, cut, phase_3, 0)
    t_cp = remote(gck_s.at[pl.ds(0, 8)], tpad, e_ssem.at[2], e_rsem.at[2], (dp, prv))
    t_cp.start()
    go(HOOKS["3a"])
    lax.fori_loop(cut, L.nblk, phase_3, 0)
    go(HOOKS["3b"])
    t_cp.wait()
    gck_s[R : R + 8, :] = tpad[...] * stays

    def phase_4(i, _):
        r = rows_of(i, BR)
        t = gck_s[pl.ds(pl.multiple_of(i * BR, 8), BR + 8), :]
        gn = gcr_s[r, :] + pltpu.roll(t, BR + 7, 0)[:BR]
        n1_, rs = normed(y_s[r, :].astype(F32))
        add_up(V_LN1G, gn * n1_)
        add_up(V_LN1B, gn)
        q1 = gn * par[G1 : G1 + 1, :]
        m1 = jnp.mean(q1, axis=-1, keepdims=True)
        m2 = jnp.mean(q1 * n1_, axis=-1, keepdims=True)
        y_s[r, :] = (x1_s[r, :] + (q1 - m1 - n1_ * m2) * rs).astype(BF16)
        pltpu.make_async_copy(y_s.at[r], ig_o.at[r], out_sem.at[i]).start()
        return 0

    lax.fori_loop(0, cut, phase_4, 0)
    go(HOOKS["4a"])
    lax.fori_loop(cut, L.nblk, phase_4, 0)
    go("W" + HOOKS["4b"])
    go(HOOKS["tail"])
    go(HOOKS["end"])
    live = [u for u in units.values()]
    while live:
        live = [u for u in live if u.advance()]
    for u in big + small:
        for cp in u.sent:
            cp.wait_send()
    for i in range(L.nblk):
        pltpu.make_async_copy(y_s.at[rows_of(i, BR)], ig_o.at[rows_of(i, BR)], out_sem.at[i]).wait()


def back(L, *args):
    R, D, n_f, n_dp, U = L.R, L.D, L.n_f, L.n_dp, L.U
    half, shard = D // 2, D // L.n_f
    hk = half // L.parts
    dma = pltpu.SemaphoreType.DMA
    bpad, fpad, full, low = pltpu.VMEM((R + 16, D), BF16), pltpu.VMEM((R + 8, D), F32), pltpu.VMEM((R, D), F32), pltpu.VMEM((R, D), BF16)
    rows8 = pltpu.VMEM((8, D), F32)
    zbits = L.nz.bit_length() - 1

    def z_rows(rows):
        total = 0
        for _ in range(zbits):
            rows = rows // 2 if (rows // 2) % 16 == 0 else rows
            total += rows
        return total

    n_r = n_f - 1
    n_pool = 2 * L.parts * (n_r + 2 * zbits + 1) + 5 * (2 * n_r + 2 * zbits + 2)
    return pl.pallas_call(
        functools.partial(back_kernel, L),
        out_shape=(
            sds((R, D), BF16), sds((D, U), BF16), sds((D, U), BF16), sds((5, D, D), BF16), sds((16, D)),
        ),
        in_specs=[ANY, VMEM, VMEM] + [ANY] * 19,
        out_specs=(ANY, ANY, ANY, ANY, VMEM),
        scratch_shapes=[
            bpad, bpad, low, fpad, full, full, full, full, full, full, low, low, low, low, low, low,
            pltpu.VMEM((3, D, D), BF16), pltpu.VMEM((5, 2, D, half), BF16), pltpu.VMEM((2, L.parts, n_f // 2, hk, U), BF16),
            pltpu.VMEM((5, D, half), BF16), pltpu.VMEM((2, L.parts, max(n_f // 2 - 1, 1), hk, U), BF16),
            pltpu.VMEM((5, n_r, shard, half), BF16), pltpu.VMEM((2, L.parts, z_rows(hk), U), BF16),
            pltpu.VMEM((5, z_rows(shard), half), BF16),
            pltpu.VMEM((SPAN, D), F32), pltpu.VMEM((SPAN, D), F32), pltpu.VMEM((SPAN, 2 * SPAN), BF16),
            pltpu.VMEM((L.nspan, 8, D), F32), rows8, pltpu.VMEM((n_f, 8, D), F32), rows8,
            pltpu.VMEM((2, 16, D), BF16), rows8, pltpu.VMEM((16, 8, D), F32), pltpu.VMEM((16, D), F32),
            pltpu.VMEM((n_f, 16, D), F32), pltpu.VMEM((n_dp, 16, D), F32), rows8,
            dma((7, L.nblk)), dma((15,)), dma((L.nblk,)), dma((3,)), dma((3,)), dma((n_f,)), dma((n_f,)),
            dma((2, n_dp)), dma((2, n_dp)), dma((16,)), dma((n_pool,)), dma((n_pool,)),
        ],
        compiler_params=pltpu.CompilerParams(collective_id=2, has_side_effects=True, vmem_limit_bytes=VLIMIT),
        cost_estimate=pl.CostEstimate(flops=20 * R * D * D, bytes_accessed=60 * R * D, transcendentals=0),
        name="back",
    )(*args)


def finish_kernel(n, rep, dkr, dvr, mixed, ig, vec, *outs):
    mats, vecs = outs[:7], outs[9:]
    outs[7][...] = mixed[...]
    outs[8][...] = ig[...]
    for m in range(5):
        mats[m][...] = rep[m].astype(F32)
    mats[5][...] = dkr[...].astype(F32)
    mats[6][...] = dvr[...].astype(F32).T

    @pl.when(pl.program_id(0) == 0)
    def _():
        for k in range(NVEC):
            vecs[k][...] = vec[k, :]


def finish(L, rep, dkr, dvr, mixed, ig, vec):
    R, D, U = L.R, L.D, L.U
    n = 4 if U % 512 == 0 else 3
    n = 6 if U % 768 == 0 else n
    rows, cols, lines = D // n, U // n, -(-R // (16 * n)) * 16
    row = pl.BlockSpec((lines, D), lambda i: (i, 0))
    mat = pl.BlockSpec((rows, D), lambda i: (i, 0))
    return pl.pallas_call(
        functools.partial(finish_kernel, n),
        grid=(n,),
        out_shape=(sds((D, D)),) * 5 + (sds((D, U)), sds((U, D))) + (sds((R, D), BF16),) * 2 + (sds((D,)),) * NVEC,
        in_specs=[
            pl.BlockSpec((5, rows, D), lambda i: (0, i, 0)), pl.BlockSpec((rows, U), lambda i: (i, 0)),
            pl.BlockSpec((D, cols), lambda i: (0, i)), row, row, pl.BlockSpec((16, D), lambda i: (0, 0)),
        ],
        out_specs=(mat,) * 5 + (pl.BlockSpec((rows, U), lambda i: (i, 0)), pl.BlockSpec((cols, D), lambda i: (i, 0)), row, row)
        + (pl.BlockSpec((D,), lambda i: (0,)),) * NVEC,
        compiler_params=pltpu.CompilerParams(vmem_limit_bytes=VLIMIT),
        cost_estimate=pl.CostEstimate(flops=0, bytes_accessed=42 * D * D, transcendentals=0),
        name="finish",
    )(rep, dkr, dvr, mixed, ig, vec)


def solution(mesh):
    def step(
        tokens, lens, og, ln1g, ln1b, td, tf, mk, mv, mr, wk, wv, wr, wo, ln2g, ln2b, cmk, cmr, ckw, cvw, wc
    ):
        L = Layout(mesh, tokens.shape[0], tokens.shape[1], ckw.shape[1])
        vecs = [ln1g, ln1b, td, tf, mk, mv, mr, ln2g, ln2b, cmk, cmr]
        xk, xv, xr, y, ck, cr, a, v, rd, wkv, sr, x1, edge, par, kall, vall = front(
            L, tokens, vecs, wk, wv, wr, wo, ckw, cvw
        )
        mixed, g2, gck, gcr, big, dc = middle(L, lens, ck, cr, x1, og, kall, vall, ckw, cvw, wc)
        ig, dkr, dvr, rep, vec = back(
            L, tokens, par, edge, g2, gck, gcr, x1, y, sr, wkv, rd, a, v, xk, xv, xr, wk, wv, wr, wo, big, dc
        )
        done = finish(L, rep, dkr, dvr, mixed, ig, vec)
        mats, (mixed, ig), vecs = done[:7], done[7:9], done[9:]
        return (mixed, ig, *vecs[:7], *mats[:4], *vecs[7:], mats[5], mats[6], mats[4])

    row, none = P(("dp", "ffn"), None), P()
    return jax.shard_map(
        step,
        mesh=mesh,
        in_specs=(row, P("dp"), row) + (none,) * 15 + (P(None, "ffn"), P("ffn", None), none),
        out_specs=(row, row) + (none,) * 15 + (P(None, "ffn"), P("ffn", None), none),
        check_vma=False,
    )
```
